32 devices in a mesh: dp: 8 (over z, x), head: 4 (over y, core).
Axes of the slice: x: 2, y: 2, z: 4, core: 2. Of those that a mesh axis runs over, the one named last changes fastest.
Arguments:
- latents: bfloat16 [16384, 1280], P(('dp', 'head')), may hold values from -6 to 6
- live_keys: int32 [64], P('dp'), may hold values from 64 to 256, as said below
- cotangent: bfloat16 [16384, 1280], P(('dp', 'head')), may hold values from -6 to 6
- inner_weights: float32 [4, 1280, 1280], P(None, 'dp', 'head'), may hold values from -1 to 1
- outer_weights: float32 [2, 1280, 1280], P(None, 'head', 'dp'), may hold values from -1 to 1
- norm_params: float32 [4, 1280], replicated, may hold values from -1 to 3
- inner_first: float32 [4, 1280, 1280], P(None, 'dp', 'head'), may hold values from -6 to 6
- inner_second: float32 [4, 1280, 1280], P(None, 'dp', 'head'), may hold values from 1.048576 to 4.194304
- inner_average: float32 [4, 1280, 1280], P(None, 'dp', 'head'), may hold values from -0.15625 to 0.15625
- outer_first: float32 [2, 1280, 1280], P(None, 'head', 'dp'), may hold values from -6 to 6
- outer_second: float32 [2, 1280, 1280], P(None, 'head', 'dp'), may hold values from 1.048576 to 4.194304
- outer_average: float32 [2, 1280, 1280], P(None, 'head', 'dp'), may hold values from -0.15625 to 0.15625
- norm_first: float32 [4, 1280], replicated, may hold values from -12 to 12
- norm_second: float32 [4, 1280], replicated, may hold values from 4.194304 to 16.777216
Outputs:
- block_output: bfloat16 [16384, 1280], P(('dp', 'head'))
- latent_grad: bfloat16 [16384, 1280], P(('dp', 'head'))
- grad_norm: float32 [], replicated
- inner_moment: float32 [4, 1280, 1280], P(None, 'dp', 'head')
- inner_square: float32 [4, 1280, 1280], P(None, 'dp', 'head')
- inner_update: float32 [4, 1280, 1280], P(None, 'dp', 'head')
- inner_smooth: float32 [4, 1280, 1280], P(None, 'dp', 'head')
- inner_copy: bfloat16 [4, 1280, 1280], P(None, 'dp', 'head')
- outer_moment: float32 [2, 1280, 1280], P(None, 'head', 'dp')
- outer_square: float32 [2, 1280, 1280], P(None, 'head', 'dp')
- outer_update: float32 [2, 1280, 1280], P(None, 'head', 'dp')
- outer_smooth: float32 [2, 1280, 1280], P(None, 'head', 'dp')
- outer_copy: bfloat16 [2, 1280, 1280], P(None, 'head', 'dp')
- norm_moment: float32 [4, 1280], replicated
- norm_square: float32 [4, 1280], replicated
- norm_update: float32 [4, 1280], replicated
- norm_two_grad: float32 [2, 1280], replicated
The draws below stay inside these ranges and needn't reach their ends.
Inputs may be any that keep to these rules, and one draw needn't show every extreme that they name: Keys of item i at positions below live_keys[i] take part; in every draw some item has all 256.
All inputs are finite; a program needn't handle non-finite values.
Results may differ from the reference program's by a relative error of at most 0.018.
Values may be sent and summed in bfloat16 or wider, within the bound.
A program may use at most 192 MiB of HBM per device.

```python
import math
import jax
import jax.numpy as jnp
from jax import lax

HEADS = 8
HS = 160
D = 1280
LAT = 256
ITEMS_DEV = 8
STEP = 5
ITEMS = 64
TOKENS = 16384
N_DP = 8


def rising(count, low_end, high_end):
    position = jnp.arange(count, dtype=jnp.float32) / max(count - 1, 1)
    return low_end + (high_end - low_end) * position


def column_rise(count):
    return rising(count, 0.6, 1.8)


def base_draw(key, shape):
    return jnp.clip(jax.random.normal(key, shape, jnp.float32), -3.0, 3.0)


def draw_live_keys(key, part):
    counts = jax.random.randint(key, (ITEMS,), LAT // 4, LAT + 1)
    full_item = jax.random.randint(jax.random.fold_in(key, 7), (), 0, ITEMS)
    return jnp.where(jnp.arange(ITEMS) == full_item, LAT, counts).astype(jnp.int32)


def draw_cotangent(key, part):
    noise_draw = base_draw(key, (TOKENS, D))
    return (noise_draw * column_rise(D)[None, :]).astype(jnp.bfloat16)


def draw_inner_weights(key, part):
    noise_draw = base_draw(key, (4, D, D)) * D ** (-0.5)
    rise_cols = jnp.broadcast_to(column_rise(D)[None, None, :], (2, 1, D))
    col_scale = jnp.concatenate([jnp.ones((2, 1, D), jnp.float32), rise_cols], axis=0)
    return noise_draw * col_scale


def draw_outer_weights(key, part):
    noise_draw = base_draw(key, (2, D, D))
    scales = jnp.array([(LAT / (3.0 * D)) ** 0.5, D ** (-0.5)], dtype=jnp.float32).reshape(2, 1, 1)
    return noise_draw * scales


def draw_norm_params(key, part):
    noise_draw = base_draw(key, (4, D))
    gain_rows = column_rise(D)[None, :] * (1.0 + 0.1 * noise_draw)
    bias_rows = 0.3 * noise_draw
    gain_mask = jnp.array([1.0, 0.0, 1.0, 0.0], dtype=jnp.float32)[:, None]
    return gain_mask * gain_rows + (1.0 - gain_mask) * bias_rows


def shard_levels(own_key, extent, split, low, largest):
    loudness, own = 1.0, jax.random.fold_in(own_key, 6)
    for axis_at, parts in split:
        steps = jnp.exp(jax.random.uniform(jax.random.fold_in(own, axis_at), (parts,), jnp.float32, low / len(split), largest / len(split)))
        loudness = loudness * jnp.repeat(steps, extent[axis_at] // parts).reshape([-1 if axis == axis_at else 1 for axis in range(len(extent))])
    return loudness


def normal_values(rng, shape, scale, reach, split=(), held_as=jnp.bfloat16):
    level = shard_levels(rng, shape, split, -0.22, 0.18) if split else 1.0
    values = jax.random.normal(rng, shape, jnp.float32) * scale * level
    return jnp.minimum(jnp.maximum(values, -reach), reach).astype(held_as)


def setup_inputs(seed: int = 0) -> dict:
    key_list = jax.random.split(jax.random.key(seed), 15)
    latents = normal_values(key_list[0], (TOKENS, D), 1.0, 6.0, ((0, 32),))
    live_keys = draw_live_keys(jax.random.fold_in(key_list[14], 71), 0)
    cotangent = draw_cotangent(jax.random.fold_in(key_list[14], 71), 0)
    inner_weights = draw_inner_weights(jax.random.fold_in(key_list[14], 71), 0)
    outer_weights = draw_outer_weights(jax.random.fold_in(key_list[14], 71), 0)
    norm_params = draw_norm_params(jax.random.fold_in(key_list[14], 71), 0)
    inner_first = normal_values(key_list[6], (4, D, D), (0.008 * TOKENS ** 0.5), 6.0, ((1, 8), (2, 4)), jnp.float32)
    inner_second = jnp.clip(jnp.exp(math.log(4.194304) - 1.3862944 * jax.random.uniform(key_list[7], (4, D, D), jnp.float32) ** shard_levels(key_list[7], (4, D, D), ((1, 8), (2, 4)), -0.2, 0.2)), 1.048576, 4.194304)
    inner_average = normal_values(key_list[8], (4, D, D), D ** -0.5, 0.15625, ((1, 8), (2, 4)), jnp.float32)
    outer_first = normal_values(key_list[9], (2, D, D), (0.008 * TOKENS ** 0.5), 6.0, ((1, 4), (2, 8)), jnp.float32)
    outer_second = jnp.clip(jnp.exp(math.log(4.194304) - 1.3862944 * jax.random.uniform(key_list[10], (2, D, D), jnp.float32) ** shard_levels(key_list[10], (2, D, D), ((1, 4), (2, 8)), -0.2, 0.2)), 1.048576, 4.194304)
    outer_average = normal_values(key_list[11], (2, D, D), D ** -0.5, 0.15625, ((1, 4), (2, 8)), jnp.float32)
    norm_first = normal_values(key_list[12], (4, D), (0.016 * TOKENS ** 0.5), 12.0, (), jnp.float32)
    norm_second = jnp.clip(jnp.exp(jax.random.uniform(key_list[13], (4, D), jnp.float32, math.log(4.194304), math.log(16.777216))), 4.194304, 16.777216)
    return {"latents": latents, "live_keys": live_keys, "cotangent": cotangent, "inner_weights": inner_weights, "outer_weights": outer_weights, "norm_params": norm_params, "inner_first": inner_first, "inner_second": inner_second, "inner_average": inner_average, "outer_first": outer_first, "outer_second": outer_second, "outer_average": outer_average, "norm_first": norm_first, "norm_second": norm_second}


@jax.custom_vjp
def low(v):
    return lax.optimization_barrier(v.astype(jnp.bfloat16)).astype(jnp.float32)

@jax.custom_vjp
def low_back(v):
    return v

def low_keep(v):
    return (low(v), None)

def low_pass(kept, grad):
    return (grad,)

def back_keep(v):
    return (v, None)

def back_low(kept, grad):
    return (low(grad),)
low.defvjp(low_keep, low_pass)
low_back.defvjp(back_keep, back_low)
NORM_EPS = 1e-05
MASKED = -1e+30
CLIP_RATE = 0.02
ADAM_EPS = 1e-08
DECAY_RATE = 0.1
NORM_RATE = 0.3
SMOOTH_RATE = 0.9

def layer_norm(values, gain_row, bias_row):
    centre = values - lax.optimization_barrier(jnp.mean(values, axis=-1, keepdims=True))
    spread = lax.optimization_barrier(jnp.mean(centre * centre, axis=-1, keepdims=True))
    return centre * lax.rsqrt(spread + NORM_EPS) * gain_row + bias_row

def matmul(left, right):
    return jnp.dot(left, right, precision=lax.Precision.HIGHEST)

def block(values, live_rows, inner, outer, norms):
    row_count = values.shape[0]
    item_count = row_count // LAT
    inner_b = low(inner)
    outer_b = low(outer)
    normed = low(layer_norm(values, norms[0], norms[1]))
    query = low(low_back(matmul(normed, inner_b[0]))).reshape(item_count, LAT, HEADS, HS)
    key_rows = low(low_back(matmul(normed, inner_b[1]))).reshape(item_count, LAT, HEADS, HS)
    value_rows = low(low_back(matmul(normed, inner_b[2]))).reshape(item_count, LAT, HEADS, HS)
    scores = jnp.einsum('iqhd,ikhd->ihqk', query, key_rows, precision=lax.Precision.HIGHEST) * HS ** (-0.5)
    valid = jnp.arange(LAT, dtype=jnp.int32)[None, None, None, :] < live_rows[:, None, None, None]
    scores = low_back(jnp.where(valid, scores, MASKED))
    probs = low(jax.nn.softmax(scores, axis=-1))
    attended = jnp.einsum('ihqk,ikhd->iqhd', probs, value_rows, precision=lax.Precision.HIGHEST)
    attended = low(low_back(attended.reshape(row_count, D)))
    residual = values + low_back(matmul(attended, outer_b[0]))
    normed_two = low(layer_norm(residual, norms[2], norms[3]))
    preact = low_back(matmul(normed_two, inner_b[3]))
    activation = low(jax.nn.gelu(preact, approximate=False))
    return residual + low_back(matmul(activation, outer_b[1]))

def adam_step(weight, grad, first, second, rate, decay):
    moment = 0.5 * first + 0.5 * grad
    square = 0.5 * second + 0.5 * grad * grad
    fix = 1.0 - 0.5 ** STEP
    update = weight - rate * (moment / fix / (jnp.sqrt(square / fix) + ADAM_EPS) + decay * weight)
    return (moment, square, update)

def reference(latents, live_keys, cotangent, inner_weights, outer_weights, norm_params, inner_first, inner_second, inner_average, outer_first, outer_second, outer_average, norm_first, norm_second):
    group_rows = ITEMS_DEV * LAT
    sources = latents.astype(jnp.float32).reshape(N_DP, group_rows, D)
    back_rows = cotangent.astype(jnp.float32).reshape(N_DP, group_rows, D)
    live_groups = live_keys.reshape(N_DP, ITEMS_DEV)

    def group_step(totals, pieces):
        source, live_rows, back = pieces

        def forward(values, inner, outer, norms):
            return block(values, live_rows, inner, outer, norms)
        result, pullback = jax.vjp(forward, source, inner_weights, outer_weights, norm_params)
        d_source, g_inner, g_outer, g_norms = pullback(back)
        totals = (totals[0] + g_inner, totals[1] + g_outer, totals[2] + g_norms)
        return (totals, (result.astype(jnp.bfloat16), d_source.astype(jnp.bfloat16)))
    zero_grads = (jnp.zeros_like(inner_weights), jnp.zeros_like(outer_weights), jnp.zeros_like(norm_params))
    totals, outputs = lax.scan(group_step, zero_grads, (sources, live_groups, back_rows))
    grad_inner, grad_outer, grad_norms = totals
    block_output = outputs[0].reshape(TOKENS, D)
    latent_grad = outputs[1].reshape(TOKENS, D)
    grad_norm = jnp.sqrt(jnp.sum(grad_inner * grad_inner) + jnp.sum(grad_outer * grad_outer) + jnp.sum(grad_norms * grad_norms))
    clip_limit = CLIP_RATE * D * jnp.sqrt(jnp.float32(TOKENS))
    factor = jnp.minimum(1.0, clip_limit / grad_norm)
    inner_rate = D ** (-0.5)
    outer_rate = jnp.array([(LAT / (3.0 * D)) ** 0.5, D ** (-0.5)], dtype=jnp.float32).reshape(2, 1, 1)
    clipped_norms = grad_norms * factor
    inner_new = adam_step(inner_weights, grad_inner * factor, inner_first, inner_second, inner_rate, DECAY_RATE)
    outer_new = adam_step(outer_weights, grad_outer * factor, outer_first, outer_second, outer_rate, DECAY_RATE)
    norm_new = adam_step(norm_params, clipped_norms, norm_first, norm_second, NORM_RATE, 0.0)
    inner_smooth = SMOOTH_RATE * inner_average + (1.0 - SMOOTH_RATE) * inner_new[2]
    outer_smooth = SMOOTH_RATE * outer_average + (1.0 - SMOOTH_RATE) * outer_new[2]
    return (block_output, latent_grad, grad_norm, inner_new[0], inner_new[1], inner_new[2], inner_smooth, inner_new[2].astype(jnp.bfloat16), outer_new[0], outer_new[1], outer_new[2], outer_smooth, outer_new[2].astype(jnp.bfloat16), norm_new[0], norm_new[1], norm_new[2], clipped_norms[2:4])
```

```python
import jax
import jax.numpy as jnp
from jax import lax
from jax.sharding import PartitionSpec as P

HEADS = 8
HS = 160
D = 1280
LAT = 256
STEP = 5


NORM_EPS = 1e-05
MASKED = -1e30
CLIP_RATE = 0.02
ADAM_EPS = 1e-08
DECAY_RATE = 0.1
NORM_RATE = 0.3
SMOOTH_RATE = 0.9


def layer_norm(values, gain_row, bias_row):
    centre = values - jnp.mean(values, axis=-1, keepdims=True)
    spread = jnp.mean(centre * centre, axis=-1, keepdims=True)
    return centre * lax.rsqrt(spread + NORM_EPS) * gain_row + bias_row


def gelu_exact(values):
    return jax.nn.gelu(values, approximate=False)


def split_heads(matrix, item_count, head_count):
    return matrix.reshape(
        item_count, matrix.shape[0] // item_count, head_count, matrix.shape[1] // head_count
    )


def masked_scores(query_heads, key_heads, live_rows):
    scores = jnp.einsum(
        "iqhd,ikhd->ihqk", query_heads, key_heads, preferred_element_type=jnp.float32
    ) * HS ** (-0.5)
    length = key_heads.shape[1]
    valid = lax.broadcasted_iota(jnp.int32, (1, 1, 1, length), 3) < live_rows[:, None, None, None]
    return jnp.where(valid, scores, MASKED)


def attend(projected, live_rows, head_count):
    item_count = live_rows.shape[0]
    query_heads = split_heads(projected[0], item_count, head_count)
    key_heads = split_heads(projected[1], item_count, head_count)
    value_heads = split_heads(projected[2], item_count, head_count)
    scores = masked_scores(query_heads, key_heads, live_rows)
    row_peak = jnp.max(scores, axis=-1, keepdims=True)
    log_total = row_peak + jnp.log(jnp.sum(jnp.exp(scores - row_peak), axis=-1, keepdims=True))
    probs_b = jnp.exp(scores - log_total).astype(jnp.bfloat16)
    attended = jnp.einsum(
        "ihqk,ikhd->iqhd", probs_b, value_heads, preferred_element_type=jnp.float32
    )
    return (
        attended.reshape(projected.shape[1], projected.shape[2]).astype(jnp.bfloat16),
        log_total,
    )


def attend_back(projected, d_attended, log_total, live_rows, head_count):
    item_count = live_rows.shape[0]
    query_heads = split_heads(projected[0], item_count, head_count)
    key_heads = split_heads(projected[1], item_count, head_count)
    value_heads = split_heads(projected[2], item_count, head_count)
    back_heads = split_heads(d_attended, item_count, head_count)
    scores = masked_scores(query_heads, key_heads, live_rows)
    attn_probs = jnp.exp(scores - log_total)
    probs_b = attn_probs.astype(jnp.bfloat16)
    d_value = jnp.einsum("ihqk,iqhd->ikhd", probs_b, back_heads, preferred_element_type=jnp.float32)
    d_probs = jnp.einsum(
        "iqhd,ikhd->ihqk", back_heads, value_heads, preferred_element_type=jnp.float32
    )
    d_scores = (
        attn_probs * (d_probs - jnp.sum(attn_probs * d_probs, axis=-1, keepdims=True))
    ).astype(jnp.bfloat16)
    score_scale = HS ** (-0.5)
    d_query = (
        jnp.einsum("ihqk,ikhd->iqhd", d_scores, key_heads, preferred_element_type=jnp.float32)
        * score_scale
    )
    d_key = (
        jnp.einsum("ihqk,iqhd->ikhd", d_scores, query_heads, preferred_element_type=jnp.float32)
        * score_scale
    )
    flat_shape = projected.shape[1:]
    return jnp.stack(
        [d_query.reshape(flat_shape), d_key.reshape(flat_shape), d_value.reshape(flat_shape)]
    ).astype(jnp.bfloat16)


def adam_step(weight, grad, first, second, rate, decay):
    moment = 0.5 * first + 0.5 * grad
    square = 0.5 * second + 0.5 * grad * grad
    fix = 1.0 - 0.5**STEP
    update = weight - rate * (moment / fix / (jnp.sqrt(square / fix) + ADAM_EPS) + decay * weight)
    return (moment, square, update)


def shards(
    latents,
    live_keys,
    cotangent,
    inner_weights,
    outer_weights,
    norm_params,
    inner_first,
    inner_second,
    inner_average,
    outer_first,
    outer_second,
    outer_average,
    norm_first,
    norm_second,
):
    head_devices = lax.axis_size("head")
    data_devices = lax.axis_size("dp")
    row_count = latents.shape[0]
    item_count = row_count // LAT
    inner_b, outer_b = (
        lax.all_gather(
            lax.all_gather(inner_weights.astype(jnp.bfloat16), "dp", axis=1, tiled=True),
            "head", axis=2, tiled=True),
        lax.all_gather(
            lax.all_gather(outer_weights.astype(jnp.bfloat16), "dp", axis=2, tiled=True),
            "head", axis=1, tiled=True),
    )
    live_own = lax.dynamic_slice(
        live_keys, (lax.axis_index("head") * item_count,), (item_count,))
    source = latents.astype(jnp.float32)
    normed = layer_norm(source, norm_params[0], norm_params[1]).astype(jnp.bfloat16)
    qkv_b = inner_b[:3]
    proj_b = outer_b[0]
    up_b = inner_b[3]
    down_b = outer_b[1]
    projected = jnp.einsum(
        "rd,tdc->trc", normed, qkv_b, preferred_element_type=jnp.float32
    ).astype(jnp.bfloat16)
    attended, log_total = attend(projected, live_own, HEADS)
    residual = source + jnp.dot(attended, proj_b, preferred_element_type=jnp.float32)
    normed_two = layer_norm(residual, norm_params[2], norm_params[3]).astype(jnp.bfloat16)
    preact = jnp.dot(normed_two, up_b, preferred_element_type=jnp.float32)
    activation = gelu_exact(preact).astype(jnp.bfloat16)
    mlp_part = jnp.dot(activation, down_b, preferred_element_type=jnp.float32)
    block_output = (residual + mlp_part).astype(jnp.bfloat16)
    grad_down = jnp.einsum("rc,rd->cd", activation, cotangent, preferred_element_type=jnp.float32)
    d_activ = jnp.einsum("rd,cd->rc", cotangent, down_b, preferred_element_type=jnp.float32)
    gelu_back = jax.vjp(gelu_exact, preact)[1]
    d_pre = gelu_back(d_activ)[0].astype(jnp.bfloat16)
    grad_up = jnp.einsum("rd,rc->dc", normed_two, d_pre, preferred_element_type=jnp.float32)
    d_normed_two = jnp.einsum("rc,dc->rd", d_pre, up_b, preferred_element_type=jnp.float32)
    norm_back_two = jax.vjp(layer_norm, residual, norm_params[2], norm_params[3])[1]
    d_resid_norm, grad_gain_two, grad_bias_two = norm_back_two(d_normed_two)
    d_resid = cotangent.astype(jnp.float32) + d_resid_norm
    d_resid_b = d_resid.astype(jnp.bfloat16)
    grad_outproj = jnp.einsum(
        "rc,rd->cd", attended, d_resid_b, preferred_element_type=jnp.float32
    )
    d_attended = jnp.einsum(
        "rd,cd->rc", d_resid_b, proj_b, preferred_element_type=jnp.float32
    ).astype(jnp.bfloat16)
    d_proj = attend_back(projected, d_attended, log_total, live_own, HEADS)
    grad_qkv = jnp.einsum("rd,trc->tdc", normed, d_proj, preferred_element_type=jnp.float32)
    d_normed = jnp.einsum("trc,tdc->rd", d_proj, qkv_b, preferred_element_type=jnp.float32)
    norm_back_one = jax.vjp(layer_norm, source, norm_params[0], norm_params[1])[1]
    d_source_norm, grad_gain_one, grad_bias_one = norm_back_one(d_normed)
    latent_grad = (d_resid + d_source_norm).astype(jnp.bfloat16)
    grad_inner = jnp.concatenate([grad_qkv, grad_up[None]], axis=0)
    grad_outer = jnp.stack([grad_outproj, grad_down])
    grad_inner, grad_outer = (
        lax.psum_scatter(
            lax.psum_scatter(
                grad_inner.astype(jnp.bfloat16), "head", scatter_dimension=2, tiled=True
            ), "dp", scatter_dimension=1, tiled=True).astype(jnp.float32),
        lax.psum_scatter(
            lax.psum_scatter(
                grad_outer.astype(jnp.bfloat16), "head", scatter_dimension=1, tiled=True
            ), "dp", scatter_dimension=2, tiled=True).astype(jnp.float32),
    )
    norm_part = jnp.stack([grad_gain_one, grad_bias_one, grad_gain_two, grad_bias_two])
    local_squares = jnp.sum(grad_inner * grad_inner) + jnp.sum(grad_outer * grad_outer)
    grad_norms, squares_all = lax.psum((norm_part, local_squares), ("dp", "head"))
    grad_norm = jnp.sqrt(squares_all + jnp.sum(grad_norms * grad_norms))
    token_total = row_count * head_devices * data_devices
    clip_limit = CLIP_RATE * D * token_total**0.5
    factor = jnp.minimum(1.0, clip_limit / grad_norm)
    inner_rate = D ** (-0.5)
    outer_rate = jnp.array([(LAT / (3.0 * D)) ** 0.5, D ** (-0.5)], dtype=jnp.float32).reshape(
        2, 1, 1
    )
    clipped_norms = grad_norms * factor
    inner_new = adam_step(
        inner_weights, grad_inner * factor, inner_first, inner_second, inner_rate, DECAY_RATE
    )
    outer_new = adam_step(
        outer_weights, grad_outer * factor, outer_first, outer_second, outer_rate, DECAY_RATE
    )
    norm_new = adam_step(norm_params, clipped_norms, norm_first, norm_second, NORM_RATE, 0.0)
    inner_smooth = SMOOTH_RATE * inner_average + (1.0 - SMOOTH_RATE) * inner_new[2]
    outer_smooth = SMOOTH_RATE * outer_average + (1.0 - SMOOTH_RATE) * outer_new[2]
    return (
        block_output,
        latent_grad,
        grad_norm,
        inner_new[0],
        inner_new[1],
        inner_new[2],
        inner_smooth,
        inner_new[2].astype(jnp.bfloat16),
        outer_new[0],
        outer_new[1],
        outer_new[2],
        outer_smooth,
        outer_new[2].astype(jnp.bfloat16),
        norm_new[0],
        norm_new[1],
        norm_new[2],
        clipped_norms[2:4],
    )


def solution(mesh):
    return jax.shard_map(
        shards,
        mesh=mesh,
        in_specs=(
            P(("dp", "head"), None),
            P("dp"),
            P(("dp", "head"), None),
            P(None, "dp", "head"),
            P(None, "head", "dp"),
            P(),
            P(None, "dp", "head"),
            P(None, "dp", "head"),
            P(None, "dp", "head"),
            P(None, "head", "dp"),
            P(None, "head", "dp"),
            P(None, "head", "dp"),
            P(),
            P(),
        ),
        out_specs=(
            P(("dp", "head"), None),
            P(("dp", "head"), None),
            P(),
            P(None, "dp", "head"),
            P(None, "dp", "head"),
            P(None, "dp", "head"),
            P(None, "dp", "head"),
            P(None, "dp", "head"),
            P(None, "head", "dp"),
            P(None, "head", "dp"),
            P(None, "head", "dp"),
            P(None, "head", "dp"),
            P(None, "head", "dp"),
            P(),
            P(),
            P(),
            P(),
        ),
        check_vma=False,
    )
```

```python
import jax
import jax.numpy as jnp
from jax import lax
from jax.experimental import pallas as pl
from jax.experimental.pallas import tpu as pltpu
from jax.sharding import PartitionSpec as P

HEADS = 8
HS = 160
D = 1280
LAT = 256
STEP = 5


NORM_EPS = 1e-05
MASKED = -1e30
CLIP_RATE = 0.02
ADAM_EPS = 1e-08
DECAY_RATE = 0.1
NORM_RATE = 0.3
SMOOTH_RATE = 0.9


NM = 6
MESH = pl.DeviceIdType.MESH


def ids():
    d = lax.axis_index("dp")
    h = lax.axis_index("head")
    return d % 2, h // 2, d // 2, h % 2


def dev(x, y, z, c):
    return (z * 2 + x, y * 2 + c)


def ag_kernel(sh, w_out, W, sh_in, s0,r0,sz,rz,sa,ra,sb,rb,sd,rd,so):
    x,y,z,c=ids()
    sib=dev(x,y,z,1-c); xn=dev(1-x,y,z,c); yn=dev(x,1-y,z,c)
    zp=[dev(x,y,lax.rem(z+k,4),c) for k in (1,2,3)]
    bar=pltpu.get_barrier_semaphore()
    for d in [sib,xn,yn]+zp:
        pl.semaphore_signal(bar,inc=1,device_id=d,device_id_type=MESH)
    pl.semaphore_wait(bar,6)
    yc=pl.ds(pl.multiple_of(y*640,128),640)
    def rc(src,dst,s,r,d): return pltpu.make_async_remote_copy(src,dst,s,r,device_id=d,device_id_type=MESH)
    def c0(m): return rc(sh.at[m,1-c], sh_in.at[m], s0.at[m], r0.at[m], sib)
    unit=lambda m: W.at[m,z,x,c,:,yc]
    def cz(m,k): return rc(unit(m),unit(m),sz.at[m,k],rz.at[m,k],zp[k])
    line=lambda m: W.at[m,:,x,c,:,yc]
    def ca(m,d): return rc(line(m),line(m),sa.at[m],ra.at[m],d)
    pb0=lambda m: W.at[m,:,:,0,:,yc]
    pb1=lambda m: W.at[m,:,x,1,:,:]
    def cb0(m): return rc(pb0(m),pb0(m),sb.at[m],rb.at[m],yn)
    def cb1(m): return rc(pb1(m),pb1(m),sb.at[m],rb.at[m],xn)
    pd=lambda m: W.at[m,:,:,c]
    def cd(m): return rc(pd(m),pd(m),sd.at[m],rd.at[m],sib)
    def co(m): return pltpu.make_async_copy(W.at[m], w_out.at[m], so.at[m])
    def startA(m):
        @pl.when(c==0)
        def _(): ca(m,xn).start()
        @pl.when(c==1)
        def _(): ca(m,yn).start()
    def startB(m):
        @pl.when(c==0)
        def _(): cb0(m).start()
        @pl.when(c==1)
        def _(): cb1(m).start()
    for m in range(NM): c0(m).start()
    for m in range(NM):
        c0(m).wait()
        own=sh[m,c]; oth=sh_in[m]
        lo=jnp.where(c==0,own,oth); hi=jnp.where(c==0,oth,own)
        W[m,z,x,c,:,yc]=jnp.concatenate([lo,hi],axis=-1)
        for k in range(3): cz(m,k).start()
    for s in range(NM+3):
        if s<NM:
            for k in range(3): cz(s,k).wait()
            startA(s)
        if 1<=s<NM+1:
            m=s-1; ca(m,xn).wait(); startB(m)
        if 2<=s<NM+2:
            m=s-2; cb0(m).wait(); cd(m).start()
        if 3<=s:
            m=s-3; cd(m).wait(); co(m).start()
    for m in range(NM): co(m).wait()
def ag(sh):
    D=pltpu.SemaphoreType.DMA
    return pl.pallas_call(ag_kernel,
      out_shape=jax.ShapeDtypeStruct((NM,4,2,2,80,1280),jnp.bfloat16),
      in_specs=[pl.BlockSpec(memory_space=pltpu.VMEM)], out_specs=pl.BlockSpec(memory_space=pl.ANY),
      scratch_shapes=[pltpu.VMEM((NM,4,2,2,80,1280),jnp.bfloat16),pltpu.VMEM((NM,80,320),jnp.bfloat16),
        D((NM,)),D((NM,)),D((NM,3)),D((NM,3)),D((NM,)),D((NM,)),D((NM,)),D((NM,)),D((NM,)),D((NM,)),D((NM,))],
      compiler_params=pltpu.CompilerParams(collective_id=0,has_side_effects=True,vmem_limit_bytes=60<<20),
      name="kag")(sh.reshape(NM,2,80,320))


def rs_kernel(G_in, out, G, sG, RD, RB, RA, RZ, F, FX, sD,rD,sB,rB,sA,rA,sZ,rZ,sF,rF):
    x,y,z,c=ids()
    sib=dev(x,y,z,1-c); xn=dev(1-x,y,z,c); yn=dev(x,1-y,z,c)
    zp=[dev(x,y,lax.rem(z+k,4),c) for k in (1,2,3)]
    bar=pltpu.get_barrier_semaphore()
    for d in [sib,xn,yn]+zp:
        pl.semaphore_signal(bar,inc=1,device_id=d,device_id_type=MESH)
    pl.semaphore_wait(bar,6)
    def cols(j): return pl.ds(pl.multiple_of(j*640,128),640)
    def rc(src,dst,s,r,d): return pltpu.make_async_remote_copy(src,dst,s,r,device_id=d,device_id_type=MESH)
    def cD(m): return rc(G.at[m,:,:,1-c],RD.at[m],sD.at[m],rD.at[m],sib)
    own2=jnp.where(c==0,x,y)
    def srcB(m,j,core):
        return G.at[m,:,j,0,:,cols(1-y)] if core==0 else G.at[m,:,1-x,1,:,cols(j)]
    def cB(m,t,core):
        j = 1-own2 if t==0 else own2
        return rc(srcB(m,j,core),RB.at[m,t],sB.at[m,t],rB.at[m,t],yn if core==0 else xn)
    def keepB(m,t,core):
        j = 1-own2 if t==0 else own2
        return G.at[m,:,j,0,:,cols(y)] if core==0 else G.at[m,:,x,1,:,cols(j)]
    def cA(m,core): return rc(keepB(m,0,core),RA.at[m],sA.at[m],rA.at[m],xn if core==0 else yn)
    def cZ(m,k):
        zt=lax.rem(z+k+1,4)
        return rc(G.at[m,zt,x,c,:,cols(y)],RZ.at[m,k],sZ.at[m,k],rZ.at[m,k],zp[k])
    def both(fn):
        for core in (0,1):
            @pl.when(c==core)
            def _(): fn(core)
    def addD(m):
        def body(i,_):
            a=i//2; b=i%2
            G[m,a,b,c]=G[m,a,b,c]+RD[m,a,b]
            return 0
        lax.fori_loop(0,8,body,0)
    def addB(m,t):
        def go(core):
            k=keepB(m,t,core)
            def body(i,_):
                k[i]=k[i]+RB[m,t,i]
                return 0
            lax.fori_loop(0,4,body,0)
        both(go)
    def addA(m):
        def body(i,_):
            r=G.at[m,i,x,c,:,cols(y)]
            r[...]=r[...]+RA[m,i]
            return 0
        lax.fori_loop(0,4,body,0)
    def cG(m): return pltpu.make_async_copy(G_in.at[m], G.at[m], sG.at[m])
    for m in range(NM): cG(m).start()
    for s in range(NM+4):
        if s<NM:
            cG(s).wait(); cD(s).start()
        if 1<=s<NM+1:
            m=s-1; cD(m).wait(); addD(m)
            both(lambda core: [cB(m,t,core).start() for t in (0,1)])
        if 2<=s<NM+2:
            m=s-2
            both(lambda core: cB(m,0,core).wait()); addB(m,0)
            both(lambda core: cA(m,core).start())
            both(lambda core: cB(m,1,core).wait()); addB(m,1)
        if 3<=s<NM+3:
            m=s-3
            cA(m,0).wait(); addA(m)
            for k in range(3): cZ(m,k).start()
        if 4<=s:
            m=s-4
            for k in range(3): cZ(m,k).wait()
            f=G[m,z,x,c,:,cols(y)].astype(jnp.float32)
            for k in range(3): f=f+RZ[m,k].astype(jnp.float32)
            F[m,0]=f[:,:384]; F[m,1]=f[:,256:]
    cF=rc(F.at[:,1-c],FX,sF,rF,sib)
    cF.start(); cF.wait()
    for m in range(NM):
        w=F[m,c]; out[m,c]=jnp.where(c==0,w[:,:320],w[:,64:])
        w=FX[m]; out[m,1-c]=jnp.where(c==0,w[:,:320],w[:,64:])
def rs(g):
    D=pltpu.SemaphoreType.DMA; bf=jnp.bfloat16
    return pl.pallas_call(rs_kernel,
      out_shape=jax.ShapeDtypeStruct((NM,2,80,320),jnp.float32),
      in_specs=[pl.BlockSpec(memory_space=pl.ANY)], out_specs=pl.BlockSpec(memory_space=pltpu.VMEM),
      scratch_shapes=[pltpu.VMEM((NM,4,2,2,80,1280),bf),D((NM,)),pltpu.VMEM((NM,4,2,80,1280),bf),pltpu.VMEM((NM,2,4,80,640),bf),pltpu.VMEM((NM,4,80,640),bf),pltpu.VMEM((NM,3,80,640),bf),
        pltpu.VMEM((NM,2,80,384),jnp.float32),pltpu.VMEM((NM,80,384),jnp.float32),
        D((NM,)),D((NM,)),D((NM,2)),D((NM,2)),D((NM,)),D((NM,)),D((NM,3)),D((NM,3)),D,D],
      compiler_params=pltpu.CompilerParams(collective_id=1,has_side_effects=True,vmem_limit_bytes=60<<20),
      name="krs")(g.reshape(NM,4,2,2,80,1280)).reshape(NM,160,320)


def layer_norm(values, gain_row, bias_row):
    centre = values - jnp.mean(values, axis=-1, keepdims=True)
    spread = jnp.mean(centre * centre, axis=-1, keepdims=True)
    return centre * lax.rsqrt(spread + NORM_EPS) * gain_row + bias_row


def gelu_exact(values):
    return jax.nn.gelu(values, approximate=False)


def split_heads(matrix, item_count, head_count):
    return matrix.reshape(
        item_count, matrix.shape[0] // item_count, head_count, matrix.shape[1] // head_count
    )


def masked_scores(query_heads, key_heads, live_rows):
    scores = jnp.einsum(
        "iqhd,ikhd->ihqk", query_heads, key_heads, preferred_element_type=jnp.float32
    ) * HS ** (-0.5)
    length = key_heads.shape[1]
    valid = lax.broadcasted_iota(jnp.int32, (1, 1, 1, length), 3) < live_rows[:, None, None, None]
    return jnp.where(valid, scores, MASKED)


def attend(projected, live_rows, head_count):
    item_count = live_rows.shape[0]
    query_heads = split_heads(projected[0], item_count, head_count)
    key_heads = split_heads(projected[1], item_count, head_count)
    value_heads = split_heads(projected[2], item_count, head_count)
    scores = masked_scores(query_heads, key_heads, live_rows)
    row_peak = jnp.max(scores, axis=-1, keepdims=True)
    log_total = row_peak + jnp.log(jnp.sum(jnp.exp(scores - row_peak), axis=-1, keepdims=True))
    probs_b = jnp.exp(scores - log_total).astype(jnp.bfloat16)
    attended = jnp.einsum(
        "ihqk,ikhd->iqhd", probs_b, value_heads, preferred_element_type=jnp.float32
    )
    return (
        attended.reshape(projected.shape[1], projected.shape[2]).astype(jnp.bfloat16),
        log_total,
    )


def attend_back(projected, d_attended, log_total, live_rows, head_count):
    item_count = live_rows.shape[0]
    query_heads = split_heads(projected[0], item_count, head_count)
    key_heads = split_heads(projected[1], item_count, head_count)
    value_heads = split_heads(projected[2], item_count, head_count)
    back_heads = split_heads(d_attended, item_count, head_count)
    scores = masked_scores(query_heads, key_heads, live_rows)
    attn_probs = jnp.exp(scores - log_total)
    probs_b = attn_probs.astype(jnp.bfloat16)
    d_value = jnp.einsum("ihqk,iqhd->ikhd", probs_b, back_heads, preferred_element_type=jnp.float32)
    d_probs = jnp.einsum(
        "iqhd,ikhd->ihqk", back_heads, value_heads, preferred_element_type=jnp.float32
    )
    d_scores = (
        attn_probs * (d_probs - jnp.sum(attn_probs * d_probs, axis=-1, keepdims=True))
    ).astype(jnp.bfloat16)
    score_scale = HS ** (-0.5)
    d_query = (
        jnp.einsum("ihqk,ikhd->iqhd", d_scores, key_heads, preferred_element_type=jnp.float32)
        * score_scale
    )
    d_key = (
        jnp.einsum("ihqk,iqhd->ikhd", d_scores, query_heads, preferred_element_type=jnp.float32)
        * score_scale
    )
    flat_shape = projected.shape[1:]
    return jnp.stack(
        [d_query.reshape(flat_shape), d_key.reshape(flat_shape), d_value.reshape(flat_shape)]
    ).astype(jnp.bfloat16)


def adam_step(weight, grad, first, second, rate, decay):
    moment = 0.5 * first + 0.5 * grad
    square = 0.5 * second + 0.5 * grad * grad
    fix = 1.0 - 0.5**STEP
    update = weight - rate * (moment / fix / (jnp.sqrt(square / fix) + ADAM_EPS) + decay * weight)
    return (moment, square, update)


def shards(
    latents,
    live_keys,
    cotangent,
    inner_weights,
    outer_weights,
    norm_params,
    inner_first,
    inner_second,
    inner_average,
    outer_first,
    outer_second,
    outer_average,
    norm_first,
    norm_second,
):
    head_devices = lax.axis_size("head")
    data_devices = lax.axis_size("dp")
    row_count = latents.shape[0]
    item_count = row_count // LAT
    fast = (data_devices, head_devices) == (8, 4)
    if fast:
        whole = ag(jnp.concatenate(
            [inner_weights[:3], outer_weights[:1].swapaxes(1, 2), inner_weights[3:],
             outer_weights[1:].swapaxes(1, 2)]).astype(jnp.bfloat16)).reshape(NM, D, D)
        inner_b = jnp.stack([whole[0], whole[1], whole[2], whole[4]])
        outer_b = jnp.stack([whole[3].T, whole[5].T])
    else:
      inner_b, outer_b = (
        lax.all_gather(
            lax.all_gather(inner_weights.astype(jnp.bfloat16), "dp", axis=1, tiled=True),
            "head", axis=2, tiled=True),
        lax.all_gather(
            lax.all_gather(outer_weights.astype(jnp.bfloat16), "dp", axis=2, tiled=True),
            "head", axis=1, tiled=True),
    )
    live_own = lax.dynamic_slice(
        live_keys, (lax.axis_index("head") * item_count,), (item_count,))
    source = latents.astype(jnp.float32)
    normed = layer_norm(source, norm_params[0], norm_params[1]).astype(jnp.bfloat16)
    qkv_b = inner_b[:3]
    proj_b = outer_b[0]
    up_b = inner_b[3]
    down_b = outer_b[1]
    projected = jnp.einsum(
        "rd,tdc->trc", normed, qkv_b, preferred_element_type=jnp.float32
    ).astype(jnp.bfloat16)
    attended, log_total = attend(projected, live_own, HEADS)
    residual = source + jnp.dot(attended, proj_b, preferred_element_type=jnp.float32)
    normed_two = layer_norm(residual, norm_params[2], norm_params[3]).astype(jnp.bfloat16)
    preact = jnp.dot(normed_two, up_b, preferred_element_type=jnp.float32)
    activation = gelu_exact(preact).astype(jnp.bfloat16)
    mlp_part = jnp.dot(activation, down_b, preferred_element_type=jnp.float32)
    block_output = (residual + mlp_part).astype(jnp.bfloat16)
    grad_down = jnp.einsum("rc,rd->cd", activation, cotangent, preferred_element_type=jnp.float32)
    d_activ = jnp.einsum("rd,cd->rc", cotangent, down_b, preferred_element_type=jnp.float32)
    gelu_back = jax.vjp(gelu_exact, preact)[1]
    d_pre = gelu_back(d_activ)[0].astype(jnp.bfloat16)
    grad_up = jnp.einsum("rd,rc->dc", normed_two, d_pre, preferred_element_type=jnp.float32)
    d_normed_two = jnp.einsum("rc,dc->rd", d_pre, up_b, preferred_element_type=jnp.float32)
    norm_back_two = jax.vjp(layer_norm, residual, norm_params[2], norm_params[3])[1]
    d_resid_norm, grad_gain_two, grad_bias_two = norm_back_two(d_normed_two)
    d_resid = cotangent.astype(jnp.float32) + d_resid_norm
    d_resid_b = d_resid.astype(jnp.bfloat16)
    grad_outproj = jnp.einsum(
        "rc,rd->cd", attended, d_resid_b, preferred_element_type=jnp.float32
    )
    d_attended = jnp.einsum(
        "rd,cd->rc", d_resid_b, proj_b, preferred_element_type=jnp.float32
    ).astype(jnp.bfloat16)
    d_proj = attend_back(projected, d_attended, log_total, live_own, HEADS)
    grad_qkv = jnp.einsum("rd,trc->tdc", normed, d_proj, preferred_element_type=jnp.float32)
    d_normed = jnp.einsum("trc,tdc->rd", d_proj, qkv_b, preferred_element_type=jnp.float32)
    norm_back_one = jax.vjp(layer_norm, source, norm_params[0], norm_params[1])[1]
    d_source_norm, grad_gain_one, grad_bias_one = norm_back_one(d_normed)
    latent_grad = (d_resid + d_source_norm).astype(jnp.bfloat16)
    if fast:
        got = rs(jnp.stack([grad_qkv[0], grad_qkv[1], grad_qkv[2], grad_outproj.T, grad_up,
                            grad_down.T]).astype(jnp.bfloat16))
        grad_inner = jnp.stack([got[0], got[1], got[2], got[4]])
        grad_outer = jnp.stack([got[3].T, got[5].T])
    else:
      grad_inner = jnp.concatenate([grad_qkv, grad_up[None]], axis=0)
      grad_outer = jnp.stack([grad_outproj, grad_down])
      grad_inner, grad_outer = (
        lax.psum_scatter(
            lax.psum_scatter(
                grad_inner.astype(jnp.bfloat16), "head", scatter_dimension=2, tiled=True
            ), "dp", scatter_dimension=1, tiled=True).astype(jnp.float32),
        lax.psum_scatter(
            lax.psum_scatter(
                grad_outer.astype(jnp.bfloat16), "head", scatter_dimension=1, tiled=True
            ), "dp", scatter_dimension=2, tiled=True).astype(jnp.float32),
    )
    norm_part = jnp.stack([grad_gain_one, grad_bias_one, grad_gain_two, grad_bias_two])
    local_squares = jnp.sum(grad_inner * grad_inner) + jnp.sum(grad_outer * grad_outer)
    grad_norms, squares_all = lax.psum((norm_part, local_squares), ("dp", "head"))
    grad_norm = jnp.sqrt(squares_all + jnp.sum(grad_norms * grad_norms))
    token_total = row_count * head_devices * data_devices
    clip_limit = CLIP_RATE * D * token_total**0.5
    factor = jnp.minimum(1.0, clip_limit / grad_norm)
    inner_rate = D ** (-0.5)
    outer_rate = jnp.array([(LAT / (3.0 * D)) ** 0.5, D ** (-0.5)], dtype=jnp.float32).reshape(
        2, 1, 1
    )
    clipped_norms = grad_norms * factor
    inner_new = adam_step(
        inner_weights, grad_inner * factor, inner_first, inner_second, inner_rate, DECAY_RATE
    )
    outer_new = adam_step(
        outer_weights, grad_outer * factor, outer_first, outer_second, outer_rate, DECAY_RATE
    )
    norm_new = adam_step(norm_params, clipped_norms, norm_first, norm_second, NORM_RATE, 0.0)
    inner_smooth = SMOOTH_RATE * inner_average + (1.0 - SMOOTH_RATE) * inner_new[2]
    outer_smooth = SMOOTH_RATE * outer_average + (1.0 - SMOOTH_RATE) * outer_new[2]
    return (
        block_output,
        latent_grad,
        grad_norm,
        inner_new[0],
        inner_new[1],
        inner_new[2],
        inner_smooth,
        inner_new[2].astype(jnp.bfloat16),
        outer_new[0],
        outer_new[1],
        outer_new[2],
        outer_smooth,
        outer_new[2].astype(jnp.bfloat16),
        norm_new[0],
        norm_new[1],
        norm_new[2],
        clipped_norms[2:4],
    )


def solution(mesh):
    return jax.shard_map(
        shards,
        mesh=mesh,
        in_specs=(
            P(("dp", "head"), None),
            P("dp"),
            P(("dp", "head"), None),
            P(None, "dp", "head"),
            P(None, "head", "dp"),
            P(),
            P(None, "dp", "head"),
            P(None, "dp", "head"),
            P(None, "dp", "head"),
            P(None, "head", "dp"),
            P(None, "head", "dp"),
            P(None, "head", "dp"),
            P(),
            P(),
        ),
        out_specs=(
            P(("dp", "head"), None),
            P(("dp", "head"), None),
            P(),
            P(None, "dp", "head"),
            P(None, "dp", "head"),
            P(None, "dp", "head"),
            P(None, "dp", "head"),
            P(None, "dp", "head"),
            P(None, "head", "dp"),
            P(None, "head", "dp"),
            P(None, "head", "dp"),
            P(None, "head", "dp"),
            P(None, "head", "dp"),
            P(),
            P(),
            P(),
            P(),
        ),
        check_vma=False,
    )
```

```python
import jax
import jax.numpy as jnp
from jax import lax
from jax.experimental import pallas as pl
from jax.experimental.pallas import tpu as pltpu
from jax.sharding import PartitionSpec as P

HEADS = 8
HS = 160
D = 1280
LAT = 256
STEP = 5


NORM_EPS = 1e-05
MASKED = -1e30
CLIP_RATE = 0.02
ADAM_EPS = 1e-08
DECAY_RATE = 0.1
NORM_RATE = 0.3
SMOOTH_RATE = 0.9


NM = 6
MESH = pl.DeviceIdType.MESH
NN = (((1,), (0,)), ((), ()))
NT = (((1,), (1,)), ((), ()))
TN = (((0,), (0,)), ((), ()))
ROWS = 512
CH = 64
SLOT = {5: 6, 4: 5, 3: 4, 0: 3, 1: 0, 2: 1}
RD_SLOTS = 2


def ids():
    d = lax.axis_index("dp")
    h = lax.axis_index("head")
    return d % 2, h // 2, d // 2, h % 2


def dev(x, y, z, c):
    return (z * 2 + x, y * 2 + c)


def dg(a, b, dims):
    return lax.dot_general(a, b, dims, preferred_element_type=jnp.float32)


def block_kernel(
    sh, lat_in, cot_in, live, norms,
    bo_out, lg_out, gout, nout,
    W, sh_in, lat, cot, n1, q, k, v, probs, att, resid, n2, act, gp, T,
    RD, RB, RA, RZ, F, FX, NG, NX, SQ, SX,
    s0, r0, sz, rz, sa, ra, sb, rb, sd, rd,
    sD, rD, sB, rB, sA, rA, sZ, rZ, sF, rF, sN, rN, sS, rS, lsem, free,
):
    bf, f32 = jnp.bfloat16, jnp.float32
    x, y, z, c = ids()
    sib, xn, yn = dev(x, y, z, 1 - c), dev(1 - x, y, z, c), dev(x, 1 - y, z, c)
    zp = [dev(x, y, lax.rem(z + j, 4), c) for j in (1, 2, 3)]

    c_lat = pltpu.make_async_copy(lat_in, lat, lsem.at[0])
    c_cot = pltpu.make_async_copy(cot_in, cot, lsem.at[1])
    c_lat.start()
    c_cot.start()
    bar = pltpu.get_barrier_semaphore()
    for d in [sib, xn, yn] + zp:
        pl.semaphore_signal(bar, inc=1, device_id=d, device_id_type=MESH)
    pl.semaphore_wait(bar, 6)

    def cols(j):
        return pl.ds(pl.multiple_of(j * 640, 128), 640)

    def rc(src, dst, s, r, d):
        return pltpu.make_async_remote_copy(src, dst, s, r, device_id=d, device_id_type=MESH)

    def both(fn):
        for core in (0, 1):
            @pl.when(c == core)
            def _():
                fn(core)

    def g_pair(m):
        return rc(sh.at[m, 1 - c], sh_in.at[m], s0.at[m], r0.at[m], sib)

    def g_z(m, j):
        u = W.at[m, z, x, c, :, cols(y)]
        return rc(u, u, sz.at[m, j], rz.at[m, j], zp[j])

    def g_a(m, core):
        u = W.at[m, :, x, c, :, cols(y)]
        return rc(u, u, sa.at[m], ra.at[m], xn if core == 0 else yn)

    def g_b(m, core):
        u = W.at[m, :, :, 0, :, cols(y)] if core == 0 else W.at[m, :, x, 1, :, :]
        return rc(u, u, sb.at[m], rb.at[m], yn if core == 0 else xn)

    def g_d(m):
        u = W.at[m, :, :, c]
        return rc(u, u, sd.at[m], rd.at[m], sib)

    def g_first(m):
        g_pair(m).wait()
        own, oth = sh[m, c], sh_in[m]
        W[m, z, x, c, :, cols(y)] = jnp.concatenate(
            [jnp.where(c == 0, own, oth), jnp.where(c == 0, oth, own)], axis=-1
        )
        for j in range(3):
            g_z(m, j).start()

    def g_step(s):
        if s + 1 < NM:
            g_first(s + 1)
        if s < NM:
            for j in range(3):
                g_z(s, j).wait()
            both(lambda core: g_a(s, core).start())
        if 0 <= s - 1 < NM:
            g_a(s - 1, 0).wait()
            both(lambda core: g_b(s - 1, core).start())
        if 0 <= s - 2 < NM:
            g_b(s - 2, 0).wait()
            g_d(s - 2).start()

    own2 = jnp.where(c == 0, x, y)

    def r_d(m):
        return rc(W.at[SLOT[m], :, :, 1 - c], RD.at[ORD[m] % RD_SLOTS], sD.at[m], rD.at[m], sib)

    def half(t):
        return 1 - own2 if t == 0 else own2

    def r_b(m, t, core):
        g = W.at[SLOT[m]]
        src = g.at[:, half(t), 0, :, cols(1 - y)] if core == 0 else g.at[:, 1 - x, 1, :, cols(half(t))]
        return rc(src, RB.at[m, t], sB.at[m, t], rB.at[m, t], yn if core == 0 else xn)

    def keep_b(m, t, core):
        g = W.at[SLOT[m]]
        return g.at[:, half(t), 0, :, cols(y)] if core == 0 else g.at[:, x, 1, :, cols(half(t))]

    def r_a(m, core):
        return rc(keep_b(m, 0, core), RA.at[m], sA.at[m], rA.at[m], xn if core == 0 else yn)

    def r_z(m, j):
        zt = lax.rem(z + j + 1, 4)
        return rc(W.at[SLOT[m], zt, x, c, :, cols(y)], RZ.at[m, j], sZ.at[m, j], rZ.at[m, j], zp[j])

    def r_f(m):
        return rc(F.at[m], FX.at[m], sF.at[m], rF.at[m], sib)

    def st_d(m):
        if ORD[m] >= RD_SLOTS:
            pl.semaphore_wait(free, 1)
        r_d(m).start()

    def st_b(m):
        r_d(m).wait()

        def body(i, _):
            a, b = i // 2, i % 2
            W[SLOT[m], a, b, c] = W[SLOT[m], a, b, c] + RD[ORD[m] % RD_SLOTS, a, b]
            return 0

        lax.fori_loop(0, 8, body, 0)
        if ORD[m] + RD_SLOTS < NM:
            pl.semaphore_signal(free, inc=1, device_id=sib, device_id_type=MESH)
        both(lambda core: [r_b(m, t, core).start() for t in (0, 1)])

    def add_b(m, t):
        def go(core):
            kept = keep_b(m, t, core)

            def body(i, _):
                kept[i] = kept[i] + RB[m, t, i]
                return 0

            lax.fori_loop(0, 4, body, 0)

        both(go)

    def st_a(m):
        both(lambda core: r_b(m, 0, core).wait())
        add_b(m, 0)
        both(lambda core: r_a(m, core).start())
        both(lambda core: r_b(m, 1, core).wait())
        add_b(m, 1)

    def st_z(m):
        r_a(m, 0).wait()

        def body(i, _):
            r = W.at[SLOT[m], i, x, c, :, cols(y)]
            r[...] = r[...] + RA[m, i]
            return 0

        lax.fori_loop(0, 4, body, 0)
        for j in range(3):
            r_z(m, j).start()

    def st_f(m):
        for j in range(3):
            r_z(m, j).wait()
        f = W[SLOT[m], z, x, c, :, cols(y)].astype(f32)
        for j in range(3):
            f = f + RZ[m, j].astype(f32)
        F[m] = jnp.where(c == 0, f[:, 256:], f[:, :384])
        gout[m, c] = jnp.where(c == 0, f[:, :320], f[:, 320:])
        r_f(m).start()
        ff = f * f
        ff = ff.reshape(10, 8, 640).sum(0)
        SQ[0] += ff[:, :128] + ff[:, 128:256] + ff[:, 256:384] + ff[:, 384:512] + ff[:, 512:]

    def mat(m):
        return W[m].reshape(D, D)

    def chunks(fn, init=0):
        return lax.fori_loop(
            0, ROWS // CH, lambda i, a: fn(pl.ds(pl.multiple_of(i * CH, CH), CH), a), init)

    def stats(vals):
        centre = vals - jnp.mean(vals, axis=-1, keepdims=True)
        r = lax.rsqrt(jnp.mean(centre * centre, axis=-1, keepdims=True) + NORM_EPS)
        return centre * r, r

    def ln_to(src, gi, dst):
        def body(r, a):
            xhat, _ = stats(src[r, :].astype(f32))
            dst[r, :] = (xhat * norms[gi:gi + 1, :] + norms[gi + 1:gi + 2, :]).astype(bf)
            return a

        chunks(body)

    def ln_back(src, gi, err, emit):
        def body(r, acc):
            xhat, inv = stats(src[r, :].astype(f32))
            e = err[r, :]
            eg = e * norms[gi:gi + 1, :]
            back = inv * (eg - jnp.mean(eg, axis=-1, keepdims=True)
                          - xhat * jnp.mean(eg * xhat, axis=-1, keepdims=True))
            emit(r, back)
            return (acc[0] + (e * xhat).reshape(CH // 8, 8, D).sum(0),
                    acc[1] + e.reshape(CH // 8, 8, D).sum(0))

        zero = jnp.zeros((8, D), f32)
        a, b = chunks(body, (zero, zero))
        NG[0, gi:gi + 1, :] = a.sum(0, keepdims=True)
        NG[0, gi + 1:gi + 2, :] = b.sum(0, keepdims=True)

    scale = HS ** (-0.5)
    lane = lax.broadcasted_iota(jnp.int32, (1, 256), 1)
    lane1 = lax.broadcasted_iota(jnp.int32, (1, 128), 1)

    def head_mask(hh):
        return jnp.where((lane >= 32 * hh) & (lane < 32 * hh + HS), 1.0, 0.0).astype(bf)

    def join(o, dst, rows, g):
        parts = [o[0][:, :128]]
        for hh in (1, 2, 3):
            parts.append(jnp.where(lane1 < 32 * hh, o[hh - 1][:, 128:], o[hh][:, :128]))
        parts.append(o[3][:, 128:])
        for j in range(5):
            dst[rows, pl.ds(pl.multiple_of(g * 640 + 128 * j, 128), 128)] = parts[j].astype(bf)

    h_first = (y * 2 + c) * 2

    def attn(i, g):
        rows = pl.ds(pl.multiple_of(i * LAT, LAT), LAT)
        count = live[h_first + i]
        outs = []
        for hh in range(4):
            win = pl.ds(pl.multiple_of(g * 640 + 128 * hh, 128), 256)
            s = dg(q[rows, win] * head_mask(hh), k[rows, win], NT) * scale
            s = jnp.where(lane < count, s, MASKED)
            e = jnp.exp(s - jnp.max(s, axis=-1, keepdims=True))
            p = (e * (1.0 / jnp.sum(e, axis=-1, keepdims=True))).astype(bf)
            probs[i * 8 + g * 4 + hh] = p
            outs.append(dg(p, v[rows, win], NN))
        join(outs, att, rows, g)

    def attn_back(i, g, do, dq, dk, dv):
        rows = pl.ds(pl.multiple_of(i * LAT, LAT), LAT)
        oq, ok, ov = [], [], []
        for hh in range(4):
            win = pl.ds(pl.multiple_of(g * 640 + 128 * hh, 128), 256)
            p = probs[i * 8 + g * 4 + hh]
            dow = do[rows, win]
            ov.append(dg(p, dow, TN))
            dp = dg(dow * head_mask(hh), v[rows, win], NT)
            pf = p.astype(f32)
            ds = (pf * (dp - jnp.sum(pf * dp, axis=-1, keepdims=True))).astype(bf)
            oq.append(dg(ds, k[rows, win], NN) * scale)
            ok.append(dg(ds, q[rows, win], TN) * scale)
        join(oq, dq, rows, g)
        join(ok, dk, rows, g)
        join(ov, dv, rows, g)

    for m in range(NM):
        g_pair(m).start()
    g_first(0)
    c_lat.wait()
    ln_to(lat, 0, n1)
    g_step(0)
    g_step(1)
    g_step(2)
    g_step(3)
    g_d(0).wait()
    q[...] = dg(n1[...], mat(0), NN).astype(bf)
    g_step(4)
    g_d(1).wait()
    k[...] = dg(n1[...], mat(1), NN).astype(bf)
    g_step(5)
    g_d(2).wait()
    v[...] = dg(n1[...], mat(2), NN).astype(bf)
    lax.fori_loop(0, 2, lambda i, a: (attn(i, 0), 0)[1], 0)
    g_step(6)
    lax.fori_loop(0, 2, lambda i, a: (attn(i, 1), 0)[1], 0)
    g_d(3).wait()
    T[...] = dg(att[...], mat(3), NT)

    def add_lat(r, a):
        resid[r, :] = T[r, :] + lat[r, :].astype(f32)
        return a

    chunks(add_lat)
    ln_to(resid, 2, n2)
    g_step(7)
    g_d(4).wait()
    T[...] = dg(n2[...], mat(4), NN)

    def gelu(r, a):
        p = T[r, :]
        cdf = 0.5 * (1.0 + lax.erf(p * (0.5 ** 0.5)))
        act[r, :] = (p * cdf).astype(bf)
        gp[r, :] = (cdf + p * (jnp.exp(-0.5 * p * p) * 0.3989422804014327)).astype(bf)
        return a

    chunks(gelu)
    c_cot.wait()
    W[SLOT[5]] = dg(cot[...], act[...], TN).astype(bf).reshape(4, 2, 2, 80, D)
    st_d(5)
    g_d(5).wait()
    T[...] = dg(cot[...], mat(5), NN)

    def to_pre(r, a):
        gp[r, :] = (T[r, :] * gp[r, :].astype(f32)).astype(bf)
        return a

    chunks(to_pre)
    T[...] = dg(act[...], mat(5), NT)

    def to_bo(r, a):
        act[r, :] = (T[r, :] + resid[r, :]).astype(bf)
        return a

    chunks(to_bo)
    c_bo = pltpu.make_async_copy(act, bo_out, lsem.at[2])
    c_bo.start()
    st_b(5)
    W[SLOT[4]] = dg(n2[...], gp[...], TN).astype(bf).reshape(4, 2, 2, 80, D)
    st_d(4)
    T[...] = dg(gp[...], mat(4), NT)

    def emit_two(r, back):
        d = cot[r, :].astype(f32) + back
        resid[r, :] = d
        n2[r, :] = d.astype(bf)

    ln_back(resid, 2, T, emit_two)
    st_b(4)
    W[SLOT[3]] = dg(n2[...], att[...], TN).astype(bf).reshape(4, 2, 2, 80, D)
    st_d(3)
    c_bo.wait()
    act[...] = dg(n2[...], mat(3), NN).astype(bf)
    st_b(3)
    lax.fori_loop(0, 2, lambda i, a: (attn_back(i, 0, act, cot, gp, att), 0)[1], 0)
    st_a(5)
    lax.fori_loop(0, 2, lambda i, a: (attn_back(i, 1, act, cot, gp, att), 0)[1], 0)
    W[SLOT[0]] = dg(n1[...], cot[...], TN).astype(bf).reshape(4, 2, 2, 80, D)
    st_d(0)
    T[...] = dg(cot[...], mat(0), NT)
    st_a(4)
    st_z(5)
    st_b(0)
    W[SLOT[1]] = dg(n1[...], gp[...], TN).astype(bf).reshape(4, 2, 2, 80, D)
    st_d(1)
    T[...] += dg(gp[...], mat(1), NT)
    st_b(1)
    W[SLOT[2]] = dg(n1[...], att[...], TN).astype(bf).reshape(4, 2, 2, 80, D)
    st_d(2)
    T[...] += dg(att[...], mat(2), NT)
    st_a(3)
    st_b(2)

    def emit_one(r, back):
        n2[r, :] = (resid[r, :] + back).astype(bf)

    ln_back(lat, 0, T, emit_one)
    c_lg = pltpu.make_async_copy(n2, lg_out, lsem.at[3])
    c_lg.start()

    def n_swap(t, d):
        cp = rc(NG.at[0], NX.at[t], sN.at[t], rN.at[t], d)
        return cp

    SQ[0] = jnp.zeros((8, 128), f32)
    n_swap(0, sib).start()
    st_z(4)
    st_f(5)
    n_swap(0, sib).wait()
    NG[0] = NG[0] + NX[0]
    n_swap(1, xn).start()
    st_a(0)
    st_z(3)
    st_f(4)
    n_swap(1, xn).wait()
    NG[0] = NG[0] + NX[1]
    n_swap(2, yn).start()
    st_a(1)
    st_z(0)
    st_f(3)
    n_swap(2, yn).wait()
    NG[0] = NG[0] + NX[2]
    for j in range(3):
        n_swap(3 + j, zp[j]).start()
    st_a(2)
    st_z(1)
    st_f(0)
    st_z(2)
    st_f(1)
    st_f(2)
    for j in range(3):
        n_swap(3 + j, zp[j]).wait()
    NG[0] = NG[0] + NX[3] + NX[4] + NX[5]

    def s_swap(t, d):
        return rc(SQ.at[0], SX.at[t], sS.at[t], rS.at[t], d)

    for t, d in enumerate((sib, xn, yn)):
        s_swap(t, d).start()
        s_swap(t, d).wait()
        SQ[0] = SQ[0] + SX[t]
    for j in range(3):
        s_swap(3 + j, zp[j]).start()
    for m in range(NM):
        r_f(m).wait()
        w = FX[m]
        gout[m, 1 - c] = jnp.where(c == 0, w[:, :320], w[:, 64:])
    for j in range(3):
        s_swap(3 + j, zp[j]).wait()
    nout[0:4, :] = NG[0]
    tot = SQ[0] + SX[3] + SX[4] + SX[5]
    nout[4:8, :] = jnp.zeros((4, D), f32) + jnp.sum(tot)
    c_lg.wait()


ORD = {5: 0, 4: 1, 3: 2, 0: 3, 1: 4, 2: 5}


def run_block(sh, lat, cot, live, norms):
    bf, f32 = jnp.bfloat16, jnp.float32
    dma = pltpu.SemaphoreType.DMA
    act = pltpu.VMEM((ROWS, D), bf)
    wide = pltpu.VMEM((ROWS, D), f32)
    vm, hbm = pl.BlockSpec(memory_space=pltpu.VMEM), pl.BlockSpec(memory_space=pl.ANY)
    return pl.pallas_call(
        block_kernel,
        out_shape=(
            jax.ShapeDtypeStruct((ROWS, D), bf),
            jax.ShapeDtypeStruct((ROWS, D), bf),
            jax.ShapeDtypeStruct((NM, 2, 80, 320), f32),
            jax.ShapeDtypeStruct((8, D), f32),
        ),
        in_specs=[vm, hbm, hbm, pl.BlockSpec(memory_space=pltpu.SMEM), vm],
        out_specs=(hbm, hbm, vm, vm),
        scratch_shapes=[
            pltpu.VMEM((7, 4, 2, 2, 80, D), bf), pltpu.VMEM((NM, 80, 320), bf),
            act, act, act, act, act, act, pltpu.VMEM((16, LAT, LAT), bf), act, wide, act, act, act, wide,
            pltpu.VMEM((RD_SLOTS, 4, 2, 80, D), bf), pltpu.VMEM((NM, 2, 4, 80, 640), bf),
            pltpu.VMEM((NM, 4, 80, 640), bf), pltpu.VMEM((NM, 3, 80, 640), bf),
            pltpu.VMEM((NM, 80, 384), f32), pltpu.VMEM((NM, 80, 384), f32),
            pltpu.VMEM((1, 4, D), f32), pltpu.VMEM((6, 4, D), f32),
            pltpu.VMEM((1, 8, 128), f32), pltpu.VMEM((6, 8, 128), f32),
            dma((NM,)), dma((NM,)), dma((NM, 3)), dma((NM, 3)), dma((NM,)), dma((NM,)),
            dma((NM,)), dma((NM,)), dma((NM,)), dma((NM,)),
            dma((NM,)), dma((NM,)), dma((NM, 2)), dma((NM, 2)), dma((NM,)), dma((NM,)),
            dma((NM, 3)), dma((NM, 3)), dma((NM,)), dma((NM,)), dma((6,)), dma((6,)),
            dma((6,)), dma((6,)), dma((4,)), pltpu.SemaphoreType.REGULAR,
        ],
        compiler_params=pltpu.CompilerParams(
            collective_id=0, has_side_effects=True, vmem_limit_bytes=64 * 1000 * 1000),
        name="block",
    )(sh.reshape(NM, 2, 80, 320), lat, cot, live, norms)


def layer_norm(values, gain_row, bias_row):
    centre = values - jnp.mean(values, axis=-1, keepdims=True)
    spread = jnp.mean(centre * centre, axis=-1, keepdims=True)
    return centre * lax.rsqrt(spread + NORM_EPS) * gain_row + bias_row


def gelu_exact(values):
    return jax.nn.gelu(values, approximate=False)


def split_heads(matrix, item_count, head_count):
    return matrix.reshape(
        item_count, matrix.shape[0] // item_count, head_count, matrix.shape[1] // head_count
    )


def masked_scores(query_heads, key_heads, live_rows):
    scores = jnp.einsum(
        "iqhd,ikhd->ihqk", query_heads, key_heads, preferred_element_type=jnp.float32
    ) * HS ** (-0.5)
    length = key_heads.shape[1]
    valid = lax.broadcasted_iota(jnp.int32, (1, 1, 1, length), 3) < live_rows[:, None, None, None]
    return jnp.where(valid, scores, MASKED)


def attend(projected, live_rows, head_count):
    item_count = live_rows.shape[0]
    query_heads = split_heads(projected[0], item_count, head_count)
    key_heads = split_heads(projected[1], item_count, head_count)
    value_heads = split_heads(projected[2], item_count, head_count)
    scores = masked_scores(query_heads, key_heads, live_rows)
    row_peak = jnp.max(scores, axis=-1, keepdims=True)
    log_total = row_peak + jnp.log(jnp.sum(jnp.exp(scores - row_peak), axis=-1, keepdims=True))
    probs_b = jnp.exp(scores - log_total).astype(jnp.bfloat16)
    attended = jnp.einsum(
        "ihqk,ikhd->iqhd", probs_b, value_heads, preferred_element_type=jnp.float32
    )
    return (
        attended.reshape(projected.shape[1], projected.shape[2]).astype(jnp.bfloat16),
        log_total,
    )


def attend_back(projected, d_attended, log_total, live_rows, head_count):
    item_count = live_rows.shape[0]
    query_heads = split_heads(projected[0], item_count, head_count)
    key_heads = split_heads(projected[1], item_count, head_count)
    value_heads = split_heads(projected[2], item_count, head_count)
    back_heads = split_heads(d_attended, item_count, head_count)
    scores = masked_scores(query_heads, key_heads, live_rows)
    attn_probs = jnp.exp(scores - log_total)
    probs_b = attn_probs.astype(jnp.bfloat16)
    d_value = jnp.einsum("ihqk,iqhd->ikhd", probs_b, back_heads, preferred_element_type=jnp.float32)
    d_probs = jnp.einsum(
        "iqhd,ikhd->ihqk", back_heads, value_heads, preferred_element_type=jnp.float32
    )
    d_scores = (
        attn_probs * (d_probs - jnp.sum(attn_probs * d_probs, axis=-1, keepdims=True))
    ).astype(jnp.bfloat16)
    score_scale = HS ** (-0.5)
    d_query = (
        jnp.einsum("ihqk,ikhd->iqhd", d_scores, key_heads, preferred_element_type=jnp.float32)
        * score_scale
    )
    d_key = (
        jnp.einsum("ihqk,iqhd->ikhd", d_scores, query_heads, preferred_element_type=jnp.float32)
        * score_scale
    )
    flat_shape = projected.shape[1:]
    return jnp.stack(
        [d_query.reshape(flat_shape), d_key.reshape(flat_shape), d_value.reshape(flat_shape)]
    ).astype(jnp.bfloat16)


def adam_step(weight, grad, first, second, rate, decay):
    moment = 0.5 * first + 0.5 * grad
    square = 0.5 * second + 0.5 * grad * grad
    fix = 1.0 - 0.5**STEP
    update = weight - rate * (moment / fix / (jnp.sqrt(square / fix) + ADAM_EPS) + decay * weight)
    return (moment, square, update)


def plain(latents, live_keys, cotangent, inner_weights, outer_weights, norm_params):
    head_devices = lax.axis_size("head")
    data_devices = lax.axis_size("dp")
    row_count = latents.shape[0]
    item_count = row_count // LAT
    inner_b, outer_b = (
        lax.all_gather(
            lax.all_gather(inner_weights.astype(jnp.bfloat16), "dp", axis=1, tiled=True),
            "head", axis=2, tiled=True),
        lax.all_gather(
            lax.all_gather(outer_weights.astype(jnp.bfloat16), "dp", axis=2, tiled=True),
            "head", axis=1, tiled=True),
    )
    live_own = lax.dynamic_slice(
        live_keys, (lax.axis_index("head") * item_count,), (item_count,))
    source = latents.astype(jnp.float32)
    normed = layer_norm(source, norm_params[0], norm_params[1]).astype(jnp.bfloat16)
    qkv_b = inner_b[:3]
    proj_b = outer_b[0]
    up_b = inner_b[3]
    down_b = outer_b[1]
    projected = jnp.einsum(
        "rd,tdc->trc", normed, qkv_b, preferred_element_type=jnp.float32
    ).astype(jnp.bfloat16)
    attended, log_total = attend(projected, live_own, HEADS)
    residual = source + jnp.dot(attended, proj_b, preferred_element_type=jnp.float32)
    normed_two = layer_norm(residual, norm_params[2], norm_params[3]).astype(jnp.bfloat16)
    preact = jnp.dot(normed_two, up_b, preferred_element_type=jnp.float32)
    activation = gelu_exact(preact).astype(jnp.bfloat16)
    mlp_part = jnp.dot(activation, down_b, preferred_element_type=jnp.float32)
    block_output = (residual + mlp_part).astype(jnp.bfloat16)
    grad_down = jnp.einsum("rc,rd->cd", activation, cotangent, preferred_element_type=jnp.float32)
    d_activ = jnp.einsum("rd,cd->rc", cotangent, down_b, preferred_element_type=jnp.float32)
    gelu_back = jax.vjp(gelu_exact, preact)[1]
    d_pre = gelu_back(d_activ)[0].astype(jnp.bfloat16)
    grad_up = jnp.einsum("rd,rc->dc", normed_two, d_pre, preferred_element_type=jnp.float32)
    d_normed_two = jnp.einsum("rc,dc->rd", d_pre, up_b, preferred_element_type=jnp.float32)
    norm_back_two = jax.vjp(layer_norm, residual, norm_params[2], norm_params[3])[1]
    d_resid_norm, grad_gain_two, grad_bias_two = norm_back_two(d_normed_two)
    d_resid = cotangent.astype(jnp.float32) + d_resid_norm
    d_resid_b = d_resid.astype(jnp.bfloat16)
    grad_outproj = jnp.einsum(
        "rc,rd->cd", attended, d_resid_b, preferred_element_type=jnp.float32
    )
    d_attended = jnp.einsum(
        "rd,cd->rc", d_resid_b, proj_b, preferred_element_type=jnp.float32
    ).astype(jnp.bfloat16)
    d_proj = attend_back(projected, d_attended, log_total, live_own, HEADS)
    grad_qkv = jnp.einsum("rd,trc->tdc", normed, d_proj, preferred_element_type=jnp.float32)
    d_normed = jnp.einsum("trc,tdc->rd", d_proj, qkv_b, preferred_element_type=jnp.float32)
    norm_back_one = jax.vjp(layer_norm, source, norm_params[0], norm_params[1])[1]
    d_source_norm, grad_gain_one, grad_bias_one = norm_back_one(d_normed)
    latent_grad = (d_resid + d_source_norm).astype(jnp.bfloat16)
    grad_inner = jnp.concatenate([grad_qkv, grad_up[None]], axis=0)
    grad_outer = jnp.stack([grad_outproj, grad_down])
    grad_inner, grad_outer = (
        lax.psum_scatter(
            lax.psum_scatter(
                grad_inner.astype(jnp.bfloat16), "head", scatter_dimension=2, tiled=True
            ), "dp", scatter_dimension=1, tiled=True).astype(jnp.float32),
        lax.psum_scatter(
            lax.psum_scatter(
                grad_outer.astype(jnp.bfloat16), "head", scatter_dimension=1, tiled=True
            ), "dp", scatter_dimension=2, tiled=True).astype(jnp.float32),
    )
    norm_part = jnp.stack([grad_gain_one, grad_bias_one, grad_gain_two, grad_bias_two])
    local_squares = jnp.sum(grad_inner * grad_inner) + jnp.sum(grad_outer * grad_outer)
    grad_norms, squares_all = lax.psum((norm_part, local_squares), ("dp", "head"))
    return block_output, latent_grad, grad_inner, grad_outer, grad_norms, squares_all


def shards(
    latents,
    live_keys,
    cotangent,
    inner_weights,
    outer_weights,
    norm_params,
    inner_first,
    inner_second,
    inner_average,
    outer_first,
    outer_second,
    outer_average,
    norm_first,
    norm_second,
):
    head_devices = lax.axis_size("head")
    data_devices = lax.axis_size("dp")
    row_count = latents.shape[0]
    token_total = row_count * head_devices * data_devices
    if (data_devices, head_devices) == (8, 4):
        sh = jnp.concatenate(
            [inner_weights[:3], outer_weights[:1].swapaxes(1, 2), inner_weights[3:],
             outer_weights[1:].swapaxes(1, 2)]).astype(jnp.bfloat16)
        block_output, latent_grad, got, small = run_block(
            sh, latents, cotangent, live_keys, norm_params)
        got = got.reshape(NM, 160, 320)
        grad_inner = jnp.stack([got[0], got[1], got[2], got[4]])
        grad_outer = jnp.stack([got[3].T, got[5].T])
        grad_norms, squares_all = small[:4], small[4, 0]
    else:
        block_output, latent_grad, grad_inner, grad_outer, grad_norms, squares_all = plain(
            latents, live_keys, cotangent, inner_weights, outer_weights, norm_params)
    grad_norm = jnp.sqrt(squares_all + jnp.sum(grad_norms * grad_norms))
    clip_limit = CLIP_RATE * D * token_total**0.5
    factor = jnp.minimum(1.0, clip_limit / grad_norm)
    inner_rate = D ** (-0.5)
    outer_rate = jnp.array([(LAT / (3.0 * D)) ** 0.5, D ** (-0.5)], dtype=jnp.float32).reshape(
        2, 1, 1
    )
    clipped_norms = grad_norms * factor
    inner_new = adam_step(
        inner_weights, grad_inner * factor, inner_first, inner_second, inner_rate, DECAY_RATE
    )
    outer_new = adam_step(
        outer_weights, grad_outer * factor, outer_first, outer_second, outer_rate, DECAY_RATE
    )
    norm_new = adam_step(norm_params, clipped_norms, norm_first, norm_second, NORM_RATE, 0.0)
    inner_smooth = SMOOTH_RATE * inner_average + (1.0 - SMOOTH_RATE) * inner_new[2]
    outer_smooth = SMOOTH_RATE * outer_average + (1.0 - SMOOTH_RATE) * outer_new[2]
    return (
        block_output,
        latent_grad,
        grad_norm,
        inner_new[0],
        inner_new[1],
        inner_new[2],
        inner_smooth,
        inner_new[2].astype(jnp.bfloat16),
        outer_new[0],
        outer_new[1],
        outer_new[2],
        outer_smooth,
        outer_new[2].astype(jnp.bfloat16),
        norm_new[0],
        norm_new[1],
        norm_new[2],
        clipped_norms[2:4],
    )


def solution(mesh):
    return jax.shard_map(
        shards,
        mesh=mesh,
        in_specs=(
            P(("dp", "head"), None),
            P("dp"),
            P(("dp", "head"), None),
            P(None, "dp", "head"),
            P(None, "head", "dp"),
            P(),
            P(None, "dp", "head"),
            P(None, "dp", "head"),
            P(None, "dp", "head"),
            P(None, "head", "dp"),
            P(None, "head", "dp"),
            P(None, "head", "dp"),
            P(),
            P(),
        ),
        out_specs=(
            P(("dp", "head"), None),
            P(("dp", "head"), None),
            P(),
            P(None, "dp", "head"),
            P(None, "dp", "head"),
            P(None, "dp", "head"),
            P(None, "dp", "head"),
            P(None, "dp", "head"),
            P(None, "head", "dp"),
            P(None, "head", "dp"),
            P(None, "head", "dp"),
            P(None, "head", "dp"),
            P(None, "head", "dp"),
            P(),
            P(),
            P(),
            P(),
        ),
        check_vma=False,
    )
```

```python
import jax
import jax.numpy as jnp
from jax import lax
from jax.experimental import pallas as pl
from jax.experimental.pallas import tpu as pltpu
from jax.sharding import PartitionSpec as P

HEADS = 8
HS = 160
D = 1280
LAT = 256
STEP = 5


NORM_EPS = 1e-05
MASKED = -1e30
CLIP_RATE = 0.02
ADAM_EPS = 1e-08
DECAY_RATE = 0.1
NORM_RATE = 0.3
SMOOTH_RATE = 0.9


NM = 6
MESH = pl.DeviceIdType.MESH
NN = (((1,), (0,)), ((), ()))
NT = (((1,), (1,)), ((), ()))
TN = (((0,), (0,)), ((), ()))
ROWS = 512
CH = 64
SLOT = {5: 6, 4: 5, 3: 4, 0: 3, 1: 0, 2: 1}
RD_SLOTS = 2
RB_SLOTS = 3
ORDER = (5, 4, 3, 0, 1, 2)
ORD = {m: i for i, m in enumerate(ORDER)}
GATHER = "FMFMMF"
REDUCE = "MFMFMF"
BASE = [sum(8 if t == "F" else 9 for t in REDUCE[:i]) for i in range(7)]


def ids():
    d = lax.axis_index("dp")
    h = lax.axis_index("head")
    return d % 2, h // 2, d // 2, h % 2


def dev(x, y, z, c):
    return (z * 2 + x, y * 2 + c)


def dg(a, b, dims):
    return lax.dot_general(a, b, dims, preferred_element_type=jnp.float32)


def block_kernel(
    sh, lat_in, cot_in, live, norms,
    bo_out, lg_out, gout, nout,
    W, sh_in, lat, cot, n1, q, k, v, probs, att, resid, n2, act, gp, T,
    RD, RB, U, F, FX, NG, NX, SQ, SX,
    s0, r0, sz, rz, sa, ra, sb, rb, sd, rd,
    sD, rD, sB, rB, sU, rU, sF, rF, sN, rN, sS, rS, lsem, free, free_b,
):
    bf, f32 = jnp.bfloat16, jnp.float32
    x, y, z, c = ids()
    sib, xn, yn = dev(x, y, z, 1 - c), dev(1 - x, y, z, c), dev(x, 1 - y, z, c)
    zp = [dev(x, y, lax.rem(z + j, 4), c) for j in (1, 2, 3)]

    c_lat = pltpu.make_async_copy(lat_in, lat, lsem.at[0])
    c_cot = pltpu.make_async_copy(cot_in, cot, lsem.at[1])
    c_lat.start()
    c_cot.start()
    bar = pltpu.get_barrier_semaphore()
    for d in [sib, xn, yn] + zp:
        pl.semaphore_signal(bar, inc=1, device_id=d, device_id_type=MESH)
    pl.semaphore_wait(bar, 6)

    def cols(j):
        return pl.ds(pl.multiple_of(j * 640, 128), 640)

    def rc(src, dst, s, r, d):
        return pltpu.make_async_remote_copy(src, dst, s, r, device_id=d, device_id_type=MESH)

    def pick(a, b):
        return jnp.where(c == 0, a, b)

    an = tuple(pick(a, b) for a, b in zip(xn, yn))
    bn = tuple(pick(a, b) for a, b in zip(yn, xn))

    def at_x(a, b):
        return pick(1 - x if a else x, 1 - x if b else x)

    def at_y(a, b):
        return pick(1 - y if b else y, 1 - y if a else y)

    def unit(w, dz, a, b):
        return w.at[lax.rem(z + dz, 4), at_x(a, b), c, :, cols(at_y(a, b))]

    def line(w, a, b):
        return w.at[:, at_x(a, b), c, :, cols(at_y(a, b))]

    def g_pair(m):
        return rc(sh.at[m, 1 - c], sh_in.at[m], s0.at[m], r0.at[m], sib)

    def g_z(m, a, j, dz, i):
        u = unit(W.at[m], dz, a, 0)
        return rc(u, u, sz.at[m, a, i], rz.at[m, a, (dz - j) % 4], zp[j - 1])

    def g_a(m):
        u = line(W.at[m], 0, 0) if GATHER[m] == "F" else unit(W.at[m], 0, 0, 0)
        return rc(u, u, sa.at[m], ra.at[m], an)

    def g_b(m, a):
        u = line(W.at[m], a, 0)
        return rc(u, u, sb.at[m, a], rb.at[m, a], bn)

    def g_d(m, a, b):
        u = line(W.at[m], a, b)
        return rc(u, u, sd.at[m, 2 * a + b], rd.at[m, 2 * a + b], sib)

    def g_z_do(m, a, what):
        def act_on(cp):
            if what == "start":
                cp.start()
            else:
                cp.wait_send()

        act_on(g_z(m, a, 2, 0, 1))
        for j, end in ((1, 3), (3, 0)):
            @pl.when(z != end)
            def _():
                act_on(g_z(m, a, j, 0, j - 1))

    def g_z_on(m, a, what):
        for at, j in ((2, 1), (1, 3)):
            @pl.when(z == at)
            def _():
                if what == "start":
                    g_z(m, a, j, 2, 3).start()
                else:
                    g_z(m, a, j, 2, 3).wait_send()

    def g_p(m):
        g_pair(m).wait()
        own, oth = sh[m, c], sh_in[m]
        W[m, z, x, c, :, cols(y)] = jnp.concatenate(
            [jnp.where(c == 0, own, oth), jnp.where(c == 0, oth, own)], axis=-1
        )
        if GATHER[m] == "M":
            g_a(m).start()

    def g_go(m, a):
        if a:
            g_a(m).wait_recv()
        g_z_do(m, a, "start")

    def g_on(m, a):
        g_z(m, a, 2, 0, 1).wait_recv()
        g_z_on(m, a, "start")

    def g_line(m, a):
        if a and GATHER[m] == "F":
            g_a(m).wait_recv()
        else:
            for j in (1, 3):
                g_z(m, a, j, 0, j - 1).wait_recv()
        if not a and GATHER[m] == "F":
            g_a(m).start()
        g_b(m, a).start()
        g_d(m, a, 0).start()

    def g_far(m, a):
        g_b(m, a).wait_recv()
        g_d(m, a, 1).start()

    def g_end(m):
        for a in (0, 1):
            for b in (0, 1):
                g_d(m, a, b).wait()
            g_b(m, a).wait_send()
            if a == 0 or GATHER[m] == "M":
                g_z_do(m, a, "wait")
                g_z_on(m, a, "wait")
        g_a(m).wait_send()

    def r_d(i):
        return rc(W.at[SLOT[ORDER[i]], :, :, 1 - c], RD.at[i % RD_SLOTS], sD.at[i], rD.at[i], sib)

    def grd(i):
        return W.at[SLOT[ORDER[i]]]

    def r_b(i, a):
        return rc(line(grd(i), a, 1), RB.at[i % RB_SLOTS, a], sB.at[i, a], rB.at[i, a], bn)

    def r_a(i):
        k = BASE[i]
        if REDUCE[i] == "F":
            return rc(line(grd(i), 1, 0), U.at[pl.ds(k, 4)], sU.at[k], rU.at[k], an)
        return rc(unit(grd(i), 0, 1, 0), U.at[k], sU.at[k], rU.at[k], an)

    def place(i, a, rel):
        return BASE[i] + (4 if REDUCE[i] == "F" else 1) + 4 * a + rel

    def r_z(i, a, dz):
        k = place(i, a, 4 - dz)
        return rc(unit(grd(i), dz, a, 0), U.at[k], sU.at[place(i, a, dz)], rU.at[k], zp[dz - 1])

    def r_y(i, a, dz, j):
        k = place(i, a, 0)
        return rc(unit(grd(i), dz, a, 0), U.at[k], sU.at[place(i, a, dz)], rU.at[k], zp[j - 1])

    def r_f(m):
        return rc(F.at[m], FX.at[m], sF.at[m], rF.at[m], sib)

    def r_z_go(i, a):
        for dz, end, j in ((1, 3, 3), (3, 0, 1)):
            @pl.when(z == end)
            def _():
                r_y(i, a, dz, j).start()

            @pl.when(z != end)
            def _():
                r_z(i, a, dz).start()

    def st_r(i, a):
        @pl.when((z == 1) | (z == 2))
        def _():
            r_y(i, a, 1, 1).wait_recv()
            u = unit(grd(i), 2, a, 0)
            u[...] = u[...] + U[place(i, a, 0)]

        r_z(i, a, 2).start()

    def r_z_in(i, a):
        u = unit(grd(i), 0, a, 0)

        def add(rel):
            u[...] = u[...] + U[place(i, a, rel)]

        r_z(i, a, 2).wait_recv()
        add(2)
        for rel, end in ((3, 0), (1, 3)):
            @pl.when(z != end)
            def _():
                r_z(i, a, 4 - rel).wait_recv()
                add(rel)

    def r_z_end(i, a):
        for dz in (1, 2, 3):
            r_z(i, a, dz).wait_send()

    def add_line(i, a, src):
        kept = line(grd(i), a, 0)

        def body(j, _):
            kept[j] = kept[j] + src[j]
            return 0

        lax.fori_loop(0, 4, body, 0)

    def st_d(i):
        if i >= RD_SLOTS:
            pl.semaphore_wait(free, 1)
        r_d(i).start()

    def st_b(i):
        r_d(i).wait()
        g = grd(i)

        def body(j, _):
            a, b = j // 2, j % 2
            g[a, b, c] = g[a, b, c] + RD[i % RD_SLOTS, a, b]
            return 0

        lax.fori_loop(0, 8, body, 0)
        if i + RD_SLOTS < NM:
            pl.semaphore_signal(free, inc=1, device_id=sib, device_id_type=MESH)
        if i >= RB_SLOTS:
            pl.semaphore_wait(free_b, 1)
        r_b(i, 1).start()
        r_b(i, 0).start()

    def st_a(i):
        r_b(i, 1).wait()
        add_line(i, 1, RB.at[i % RB_SLOTS, 1])
        if REDUCE[i] == "F":
            r_a(i).start()
        else:
            r_z_go(i, 1)

    def st_c(i):
        r_b(i, 0).wait()
        add_line(i, 0, RB.at[i % RB_SLOTS, 0])
        if i + RB_SLOTS < NM:
            pl.semaphore_signal(free_b, inc=1, device_id=bn, device_id_type=MESH)
        if REDUCE[i] == "M":
            r_z_go(i, 0)

    def st_z(i):
        if REDUCE[i] == "F":
            r_a(i).wait()
            add_line(i, 0, U.at[pl.ds(BASE[i], 4)])
            r_z_go(i, 0)
        else:
            st_r(i, 1)

    def st_y(i):
        r_z_in(i, 1)
        r_a(i).start()

    def st_f(i):
        m = ORDER[i]
        r_z_in(i, 0)
        f = unit(grd(i), 0, 0, 0)[...].astype(f32)
        if REDUCE[i] == "M":
            r_a(i).wait()
            f = f + U[BASE[i]].astype(f32)
            r_z_end(i, 1)
        r_z_end(i, 0)
        F[m] = jnp.where(c == 0, f[:, 256:], f[:, :384])
        gout[m, c] = jnp.where(c == 0, f[:, :320], f[:, 320:])
        r_f(m).start()
        ff = f * f
        ff = ff.reshape(10, 8, 640).sum(0)
        SQ[0] += ff[:, :128] + ff[:, 128:256] + ff[:, 256:384] + ff[:, 384:512] + ff[:, 512:]

    def mat(m):
        return W[m].reshape(D, D)

    def chunks(fn, init=0):
        return lax.fori_loop(
            0, ROWS // CH, lambda i, a: fn(pl.ds(pl.multiple_of(i * CH, CH), CH), a), init)

    def stats(vals):
        centre = vals - jnp.mean(vals, axis=-1, keepdims=True)
        r = lax.rsqrt(jnp.mean(centre * centre, axis=-1, keepdims=True) + NORM_EPS)
        return centre * r, r

    def ln_to(src, gi, dst):
        def body(r, a):
            xhat, _ = stats(src[r, :].astype(f32))
            dst[r, :] = (xhat * norms[gi:gi + 1, :] + norms[gi + 1:gi + 2, :]).astype(bf)
            return a

        chunks(body)

    def ln_back(src, gi, err, emit):
        def body(r, acc):
            xhat, inv = stats(src[r, :].astype(f32))
            e = err[r, :]
            eg = e * norms[gi:gi + 1, :]
            back = inv * (eg - jnp.mean(eg, axis=-1, keepdims=True)
                          - xhat * jnp.mean(eg * xhat, axis=-1, keepdims=True))
            emit(r, back)
            return (acc[0] + (e * xhat).reshape(CH // 8, 8, D).sum(0),
                    acc[1] + e.reshape(CH // 8, 8, D).sum(0))

        zero = jnp.zeros((8, D), f32)
        a, b = chunks(body, (zero, zero))
        NG[0, gi:gi + 1, :] = a.sum(0, keepdims=True)
        NG[0, gi + 1:gi + 2, :] = b.sum(0, keepdims=True)

    scale = HS ** (-0.5)
    lane = lax.broadcasted_iota(jnp.int32, (1, 256), 1)
    lane1 = lax.broadcasted_iota(jnp.int32, (1, 128), 1)

    def head_mask(hh):
        return jnp.where((lane >= 32 * hh) & (lane < 32 * hh + HS), 1.0, 0.0).astype(bf)

    def join(o, dst, rows, g):
        parts = [o[0][:, :128]]
        for hh in (1, 2, 3):
            parts.append(jnp.where(lane1 < 32 * hh, o[hh - 1][:, 128:], o[hh][:, :128]))
        parts.append(o[3][:, 128:])
        for j in range(5):
            dst[rows, pl.ds(pl.multiple_of(g * 640 + 128 * j, 128), 128)] = parts[j].astype(bf)

    h_first = (y * 2 + c) * 2

    def attn(i, g):
        rows = pl.ds(pl.multiple_of(i * LAT, LAT), LAT)
        count = live[h_first + i]
        outs = []
        for hh in range(4):
            win = pl.ds(pl.multiple_of(g * 640 + 128 * hh, 128), 256)
            s = dg(q[rows, win] * head_mask(hh), k[rows, win], NT) * scale
            s = jnp.where(lane < count, s, MASKED)
            e = jnp.exp(s - jnp.max(s, axis=-1, keepdims=True))
            p = (e * (1.0 / jnp.sum(e, axis=-1, keepdims=True))).astype(bf)
            probs[i * 8 + g * 4 + hh] = p
            outs.append(dg(p, v[rows, win], NN))
        join(outs, att, rows, g)

    def attn_back(i, g, do, dq, dk, dv):
        rows = pl.ds(pl.multiple_of(i * LAT, LAT), LAT)
        oq, ok, ov = [], [], []
        for hh in range(4):
            win = pl.ds(pl.multiple_of(g * 640 + 128 * hh, 128), 256)
            p = probs[i * 8 + g * 4 + hh]
            dow = do[rows, win]
            ov.append(dg(p, dow, TN))
            dp = dg(dow * head_mask(hh), v[rows, win], NT)
            pf = p.astype(f32)
            ds = (pf * (dp - jnp.sum(pf * dp, axis=-1, keepdims=True))).astype(bf)
            oq.append(dg(ds, k[rows, win], NN) * scale)
            ok.append(dg(ds, q[rows, win], TN) * scale)
        join(oq, dq, rows, g)
        join(ok, dk, rows, g)
        join(ov, dv, rows, g)

    def grad(m, left, right):
        W[SLOT[m]] = dg(left[...], right[...], TN).astype(bf).reshape(4, 2, 2, 80, D)
        st_d(ORD[m])

    def proj(dst, m):
        dst[...] = dg(n1[...], mat(m), NN).astype(bf)

    def begin():
        for m in range(NM):
            g_pair(m).start()
        g_p(0)
        g_go(0, 0)
        g_p(1)
        g_go(1, 0)
        for m in range(2, NM):
            g_p(m)
        g_go(1, 1)
        c_lat.wait()
        ln_to(lat, 0, n1)
        SQ[0] = jnp.zeros((8, 128), f32)

    def out_proj():
        T[...] = dg(att[...], mat(3), NT)

        def add_lat(r, a):
            resid[r, :] = T[r, :] + lat[r, :].astype(f32)
            return a

        chunks(add_lat)
        ln_to(resid, 2, n2)

    def up():
        T[...] = dg(n2[...], mat(4), NN)

        def gelu(r, a):
            p = T[r, :]
            cdf = 0.5 * (1.0 + lax.erf(p * (0.5 ** 0.5)))
            act[r, :] = (p * cdf).astype(bf)
            gp[r, :] = (cdf + p * (jnp.exp(-0.5 * p * p) * 0.3989422804014327)).astype(bf)
            return a

        chunks(gelu)
        c_cot.wait()

    def d_act():
        T[...] = dg(cot[...], mat(5), NN)

        def to_pre(r, a):
            gp[r, :] = (T[r, :] * gp[r, :].astype(f32)).astype(bf)
            return a

        chunks(to_pre)

    c_bo = pltpu.make_async_copy(act, bo_out, lsem.at[2])
    c_lg = pltpu.make_async_copy(n2, lg_out, lsem.at[3])

    def down():
        T[...] = dg(act[...], mat(5), NT)

        def to_bo(r, a):
            act[r, :] = (T[r, :] + resid[r, :]).astype(bf)
            return a

        chunks(to_bo)
        c_bo.start()

    def grad_after_down():
        down()
        grad(4, n2, gp)

    def d_two():
        T[...] = dg(gp[...], mat(4), NT)

        def emit_two(r, back):
            d = cot[r, :].astype(f32) + back
            resid[r, :] = d
            n2[r, :] = d.astype(bf)

        ln_back(resid, 2, T, emit_two)

    def d_att():
        c_bo.wait()
        act[...] = dg(n2[...], mat(3), NN).astype(bf)

    def d_in(m, src):
        if m == 0:
            T[...] = dg(src[...], mat(0), NT)
        else:
            T[...] += dg(src[...], mat(m), NT)

    def d_one():
        def emit_one(r, back):
            n2[r, :] = (resid[r, :] + back).astype(bf)

        ln_back(lat, 0, T, emit_one)
        c_lg.start()

    def n_swap(t):
        return rc(NG.at[0], NX.at[t], sN.at[t], rN.at[t], ([sib, xn, yn] + zp)[t])

    def n_step(t):
        if t > 0:
            n_swap(t - 1).wait()
            NG[0] = NG[0] + NX[t - 1]
        for j in (t,) if t < 3 else (3, 4, 5):
            n_swap(j).start()

    def n_end():
        for j in (3, 4, 5):
            n_swap(j).wait()
        NG[0] = NG[0] + NX[3] + NX[4] + NX[5]

    def s_swap(t):
        return rc(SQ.at[0], SX.at[t], sS.at[t], rS.at[t], ([sib, xn, yn] + zp)[t])

    def finish():
        for t in range(3):
            s_swap(t).start()
            s_swap(t).wait()
            SQ[0] = SQ[0] + SX[t]
        for t in (3, 4, 5):
            s_swap(t).start()
        for m in range(NM):
            r_f(m).wait()
            w = FX[m]
            gout[m, 1 - c] = jnp.where(c == 0, w[:, :320], w[:, 64:])
        for t in (3, 4, 5):
            s_swap(t).wait()
        nout[0:4, :] = NG[0]
        tot = SQ[0] + SX[3] + SX[4] + SX[5]
        nout[4:8, :] = jnp.zeros((4, D), f32) + jnp.sum(tot)
        c_lg.wait()

    def heads(fn, g, i, *refs):
        fn(i, g, *refs)

    P0, P1, P2, P3 = ((heads, attn, g, i) for g in (0, 1) for i in (0, 1))
    Q0, Q1, Q2, Q3 = ((heads, attn_back, g, i, act, cot, gp, att) for g in (0, 1) for i in (0, 1))
    program = [
        (begin,),
        (g_on, 0, 0), (g_go, 2, 0), (g_line, 0, 0),
        (g_on, 1, 0), (g_on, 1, 1), (g_go, 3, 0), (g_go, 3, 1), (g_line, 1, 0), (g_line, 1, 1),
        (g_line, 0, 1), (g_far, 0, 0),
        (g_on, 2, 0), (g_go, 4, 0), (g_go, 4, 1), (g_line, 2, 0),
        (g_far, 1, 0), (g_far, 0, 1), (g_end, 0),
        (proj, q, 0),
        (g_on, 3, 0), (g_on, 3, 1), (g_go, 5, 0), (g_line, 3, 0), (g_line, 3, 1),
        (g_line, 2, 1), (g_far, 2, 0), (g_far, 1, 1), (g_end, 1),
        (proj, k, 1),
        (g_on, 4, 0), (g_on, 4, 1), (g_line, 4, 0), (g_line, 4, 1),
        (g_far, 3, 0), (g_far, 2, 1), (g_end, 2),
        (proj, v, 2), P0,
        (g_on, 5, 0), (g_line, 5, 0), P1,
        (g_far, 4, 0), P2, (g_far, 3, 1), P3, (g_end, 3), (out_proj,),
        (g_line, 5, 1), (g_far, 5, 0), (g_far, 4, 1), (g_end, 4),
        (up,), (grad, 5, cot, act), (g_far, 5, 1), (st_b, 0), (g_end, 5),
        (d_act,), (grad_after_down,), (st_a, 0), (st_b, 1), (st_c, 0),
        (d_two,), (st_z, 0), (st_r, 0, 0), (grad, 3, n2, att), (st_a, 1), (d_att,), (st_b, 2),
        (st_c, 1), (st_y, 0), Q0, (st_z, 1), Q1, (st_f, 0), (st_a, 2), Q2, (st_r, 1, 0), (st_c, 2), Q3,
        (grad, 0, n1, cot), (st_z, 2), (st_r, 2, 0), (st_f, 1), (d_in, 0, cot), (st_b, 3),
        (grad, 1, n1, gp), (st_y, 2), (d_in, 1, gp), (st_a, 3), (st_b, 4),
        (grad, 2, n1, att), (st_c, 3), (d_in, 2, att), (st_f, 2), (st_b, 5), (st_z, 3), (d_one,),
        (n_step, 0), (st_a, 4), (st_r, 3, 0), (n_step, 1), (st_c, 4), (n_step, 2), (st_z, 4),
        (st_r, 4, 0), (n_step, 3), (st_f, 3), (st_a, 5), (st_y, 4), (st_c, 5), (st_f, 4), (st_z, 5),
        (n_end,), (st_r, 5, 0), (st_f, 5), (finish,),
    ]
    for fn, *given in program:
        fn(*given)


def run_block(sh, lat, cot, live, norms):
    bf, f32 = jnp.bfloat16, jnp.float32
    dma = pltpu.SemaphoreType.DMA
    act = pltpu.VMEM((ROWS, D), bf)
    wide = pltpu.VMEM((ROWS, D), f32)
    vm, hbm = pl.BlockSpec(memory_space=pltpu.VMEM), pl.BlockSpec(memory_space=pl.ANY)
    return pl.pallas_call(
        block_kernel,
        out_shape=(
            jax.ShapeDtypeStruct((ROWS, D), bf),
            jax.ShapeDtypeStruct((ROWS, D), bf),
            jax.ShapeDtypeStruct((NM, 2, 80, 320), f32),
            jax.ShapeDtypeStruct((8, D), f32),
        ),
        in_specs=[vm, hbm, hbm, pl.BlockSpec(memory_space=pltpu.SMEM), vm],
        out_specs=(hbm, hbm, vm, vm),
        scratch_shapes=[
            pltpu.VMEM((7, 4, 2, 2, 80, D), bf), pltpu.VMEM((NM, 80, 320), bf),
            act, act, act, act, act, act, pltpu.VMEM((16, LAT, LAT), bf), act, wide, act, act, act, wide,
            pltpu.VMEM((RD_SLOTS, 4, 2, 80, D), bf), pltpu.VMEM((RB_SLOTS, 2, 4, 80, 640), bf),
            pltpu.VMEM((BASE[6], 80, 640), bf),
            pltpu.VMEM((NM, 80, 384), f32), pltpu.VMEM((NM, 80, 384), f32),
            pltpu.VMEM((1, 4, D), f32), pltpu.VMEM((6, 4, D), f32),
            pltpu.VMEM((1, 8, 128), f32), pltpu.VMEM((6, 8, 128), f32),
            dma((NM,)), dma((NM,)), dma((NM, 2, 4)), dma((NM, 2, 4)), dma((NM,)), dma((NM,)),
            dma((NM, 2)), dma((NM, 2)), dma((NM, 4)), dma((NM, 4)),
            dma((NM,)), dma((NM,)), dma((NM, 2)), dma((NM, 2)), dma((BASE[6],)), dma((BASE[6],)),
            dma((NM,)), dma((NM,)), dma((6,)), dma((6,)), dma((6,)), dma((6,)), dma((4,)),
            pltpu.SemaphoreType.REGULAR, pltpu.SemaphoreType.REGULAR,
        ],
        compiler_params=pltpu.CompilerParams(
            collective_id=0, has_side_effects=True, vmem_limit_bytes=64 * 1000 * 1000),
        name="block",
    )(sh.reshape(NM, 2, 80, 320), lat, cot, live, norms)


def layer_norm(values, gain_row, bias_row):
    centre = values - jnp.mean(values, axis=-1, keepdims=True)
    spread = jnp.mean(centre * centre, axis=-1, keepdims=True)
    return centre * lax.rsqrt(spread + NORM_EPS) * gain_row + bias_row


def gelu_exact(values):
    return jax.nn.gelu(values, approximate=False)


def split_heads(matrix, item_count, head_count):
    return matrix.reshape(
        item_count, matrix.shape[0] // item_count, head_count, matrix.shape[1] // head_count
    )


def masked_scores(query_heads, key_heads, live_rows):
    scores = jnp.einsum(
        "iqhd,ikhd->ihqk", query_heads, key_heads, preferred_element_type=jnp.float32
    ) * HS ** (-0.5)
    length = key_heads.shape[1]
    valid = lax.broadcasted_iota(jnp.int32, (1, 1, 1, length), 3) < live_rows[:, None, None, None]
    return jnp.where(valid, scores, MASKED)


def attend(projected, live_rows, head_count):
    item_count = live_rows.shape[0]
    query_heads = split_heads(projected[0], item_count, head_count)
    key_heads = split_heads(projected[1], item_count, head_count)
    value_heads = split_heads(projected[2], item_count, head_count)
    scores = masked_scores(query_heads, key_heads, live_rows)
    row_peak = jnp.max(scores, axis=-1, keepdims=True)
    log_total = row_peak + jnp.log(jnp.sum(jnp.exp(scores - row_peak), axis=-1, keepdims=True))
    probs_b = jnp.exp(scores - log_total).astype(jnp.bfloat16)
    attended = jnp.einsum(
        "ihqk,ikhd->iqhd", probs_b, value_heads, preferred_element_type=jnp.float32
    )
    return (
        attended.reshape(projected.shape[1], projected.shape[2]).astype(jnp.bfloat16),
        log_total,
    )


def attend_back(projected, d_attended, log_total, live_rows, head_count):
    item_count = live_rows.shape[0]
    query_heads = split_heads(projected[0], item_count, head_count)
    key_heads = split_heads(projected[1], item_count, head_count)
    value_heads = split_heads(projected[2], item_count, head_count)
    back_heads = split_heads(d_attended, item_count, head_count)
    scores = masked_scores(query_heads, key_heads, live_rows)
    attn_probs = jnp.exp(scores - log_total)
    probs_b = attn_probs.astype(jnp.bfloat16)
    d_value = jnp.einsum("ihqk,iqhd->ikhd", probs_b, back_heads, preferred_element_type=jnp.float32)
    d_probs = jnp.einsum(
        "iqhd,ikhd->ihqk", back_heads, value_heads, preferred_element_type=jnp.float32
    )
    d_scores = (
        attn_probs * (d_probs - jnp.sum(attn_probs * d_probs, axis=-1, keepdims=True))
    ).astype(jnp.bfloat16)
    score_scale = HS ** (-0.5)
    d_query = (
        jnp.einsum("ihqk,ikhd->iqhd", d_scores, key_heads, preferred_element_type=jnp.float32)
        * score_scale
    )
    d_key = (
        jnp.einsum("ihqk,iqhd->ikhd", d_scores, query_heads, preferred_element_type=jnp.float32)
        * score_scale
    )
    flat_shape = projected.shape[1:]
    return jnp.stack(
        [d_query.reshape(flat_shape), d_key.reshape(flat_shape), d_value.reshape(flat_shape)]
    ).astype(jnp.bfloat16)


def adam_step(weight, grad, first, second, rate, decay):
    moment = 0.5 * first + 0.5 * grad
    square = 0.5 * second + 0.5 * grad * grad
    fix = 1.0 - 0.5**STEP
    update = weight - rate * (moment / fix / (jnp.sqrt(square / fix) + ADAM_EPS) + decay * weight)
    return (moment, square, update)


def plain(latents, live_keys, cotangent, inner_weights, outer_weights, norm_params):
    head_devices = lax.axis_size("head")
    data_devices = lax.axis_size("dp")
    row_count = latents.shape[0]
    item_count = row_count // LAT
    inner_b, outer_b = (
        lax.all_gather(
            lax.all_gather(inner_weights.astype(jnp.bfloat16), "dp", axis=1, tiled=True),
            "head", axis=2, tiled=True),
        lax.all_gather(
            lax.all_gather(outer_weights.astype(jnp.bfloat16), "dp", axis=2, tiled=True),
            "head", axis=1, tiled=True),
    )
    live_own = lax.dynamic_slice(
        live_keys, (lax.axis_index("head") * item_count,), (item_count,))
    source = latents.astype(jnp.float32)
    normed = layer_norm(source, norm_params[0], norm_params[1]).astype(jnp.bfloat16)
    qkv_b = inner_b[:3]
    proj_b = outer_b[0]
    up_b = inner_b[3]
    down_b = outer_b[1]
    projected = jnp.einsum(
        "rd,tdc->trc", normed, qkv_b, preferred_element_type=jnp.float32
    ).astype(jnp.bfloat16)
    attended, log_total = attend(projected, live_own, HEADS)
    residual = source + jnp.dot(attended, proj_b, preferred_element_type=jnp.float32)
    normed_two = layer_norm(residual, norm_params[2], norm_params[3]).astype(jnp.bfloat16)
    preact = jnp.dot(normed_two, up_b, preferred_element_type=jnp.float32)
    activation = gelu_exact(preact).astype(jnp.bfloat16)
    mlp_part = jnp.dot(activation, down_b, preferred_element_type=jnp.float32)
    block_output = (residual + mlp_part).astype(jnp.bfloat16)
    grad_down = jnp.einsum("rc,rd->cd", activation, cotangent, preferred_element_type=jnp.float32)
    d_activ = jnp.einsum("rd,cd->rc", cotangent, down_b, preferred_element_type=jnp.float32)
    gelu_back = jax.vjp(gelu_exact, preact)[1]
    d_pre = gelu_back(d_activ)[0].astype(jnp.bfloat16)
    grad_up = jnp.einsum("rd,rc->dc", normed_two, d_pre, preferred_element_type=jnp.float32)
    d_normed_two = jnp.einsum("rc,dc->rd", d_pre, up_b, preferred_element_type=jnp.float32)
    norm_back_two = jax.vjp(layer_norm, residual, norm_params[2], norm_params[3])[1]
    d_resid_norm, grad_gain_two, grad_bias_two = norm_back_two(d_normed_two)
    d_resid = cotangent.astype(jnp.float32) + d_resid_norm
    d_resid_b = d_resid.astype(jnp.bfloat16)
    grad_outproj = jnp.einsum(
        "rc,rd->cd", attended, d_resid_b, preferred_element_type=jnp.float32
    )
    d_attended = jnp.einsum(
        "rd,cd->rc", d_resid_b, proj_b, preferred_element_type=jnp.float32
    ).astype(jnp.bfloat16)
    d_proj = attend_back(projected, d_attended, log_total, live_own, HEADS)
    grad_qkv = jnp.einsum("rd,trc->tdc", normed, d_proj, preferred_element_type=jnp.float32)
    d_normed = jnp.einsum("trc,tdc->rd", d_proj, qkv_b, preferred_element_type=jnp.float32)
    norm_back_one = jax.vjp(layer_norm, source, norm_params[0], norm_params[1])[1]
    d_source_norm, grad_gain_one, grad_bias_one = norm_back_one(d_normed)
    latent_grad = (d_resid + d_source_norm).astype(jnp.bfloat16)
    grad_inner = jnp.concatenate([grad_qkv, grad_up[None]], axis=0)
    grad_outer = jnp.stack([grad_outproj, grad_down])
    grad_inner, grad_outer = (
        lax.psum_scatter(
            lax.psum_scatter(
                grad_inner.astype(jnp.bfloat16), "head", scatter_dimension=2, tiled=True
            ), "dp", scatter_dimension=1, tiled=True).astype(jnp.float32),
        lax.psum_scatter(
            lax.psum_scatter(
                grad_outer.astype(jnp.bfloat16), "head", scatter_dimension=1, tiled=True
            ), "dp", scatter_dimension=2, tiled=True).astype(jnp.float32),
    )
    norm_part = jnp.stack([grad_gain_one, grad_bias_one, grad_gain_two, grad_bias_two])
    local_squares = jnp.sum(grad_inner * grad_inner) + jnp.sum(grad_outer * grad_outer)
    grad_norms, squares_all = lax.psum((norm_part, local_squares), ("dp", "head"))
    return block_output, latent_grad, grad_inner, grad_outer, grad_norms, squares_all


def shards(
    latents,
    live_keys,
    cotangent,
    inner_weights,
    outer_weights,
    norm_params,
    inner_first,
    inner_second,
    inner_average,
    outer_first,
    outer_second,
    outer_average,
    norm_first,
    norm_second,
):
    head_devices = lax.axis_size("head")
    data_devices = lax.axis_size("dp")
    row_count = latents.shape[0]
    token_total = row_count * head_devices * data_devices
    if (data_devices, head_devices) == (8, 4):
        sh = jnp.concatenate(
            [inner_weights[:3], outer_weights[:1].swapaxes(1, 2), inner_weights[3:],
             outer_weights[1:].swapaxes(1, 2)]).astype(jnp.bfloat16)
        block_output, latent_grad, got, small = run_block(
            sh, latents, cotangent, live_keys, norm_params)
        got = got.reshape(NM, 160, 320)
        grad_inner = jnp.stack([got[0], got[1], got[2], got[4]])
        grad_outer = jnp.stack([got[3].T, got[5].T])
        grad_norms, squares_all = small[:4], small[4, 0]
    else:
        block_output, latent_grad, grad_inner, grad_outer, grad_norms, squares_all = plain(
            latents, live_keys, cotangent, inner_weights, outer_weights, norm_params)
    grad_norm = jnp.sqrt(squares_all + jnp.sum(grad_norms * grad_norms))
    clip_limit = CLIP_RATE * D * token_total**0.5
    factor = jnp.minimum(1.0, clip_limit / grad_norm)
    inner_rate = D ** (-0.5)
    outer_rate = jnp.array([(LAT / (3.0 * D)) ** 0.5, D ** (-0.5)], dtype=jnp.float32).reshape(
        2, 1, 1
    )
    clipped_norms = grad_norms * factor
    inner_new = adam_step(
        inner_weights, grad_inner * factor, inner_first, inner_second, inner_rate, DECAY_RATE
    )
    outer_new = adam_step(
        outer_weights, grad_outer * factor, outer_first, outer_second, outer_rate, DECAY_RATE
    )
    norm_new = adam_step(norm_params, clipped_norms, norm_first, norm_second, NORM_RATE, 0.0)
    inner_smooth = SMOOTH_RATE * inner_average + (1.0 - SMOOTH_RATE) * inner_new[2]
    outer_smooth = SMOOTH_RATE * outer_average + (1.0 - SMOOTH_RATE) * outer_new[2]
    return (
        block_output,
        latent_grad,
        grad_norm,
        inner_new[0],
        inner_new[1],
        inner_new[2],
        inner_smooth,
        inner_new[2].astype(jnp.bfloat16),
        outer_new[0],
        outer_new[1],
        outer_new[2],
        outer_smooth,
        outer_new[2].astype(jnp.bfloat16),
        norm_new[0],
        norm_new[1],
        norm_new[2],
        clipped_norms[2:4],
    )


def solution(mesh):
    return jax.shard_map(
        shards,
        mesh=mesh,
        in_specs=(
            P(("dp", "head"), None),
            P("dp"),
            P(("dp", "head"), None),
            P(None, "dp", "head"),
            P(None, "head", "dp"),
            P(),
            P(None, "dp", "head"),
            P(None, "dp", "head"),
            P(None, "dp", "head"),
            P(None, "head", "dp"),
            P(None, "head", "dp"),
            P(None, "head", "dp"),
            P(),
            P(),
        ),
        out_specs=(
            P(("dp", "head"), None),
            P(("dp", "head"), None),
            P(),
            P(None, "dp", "head"),
            P(None, "dp", "head"),
            P(None, "dp", "head"),
            P(None, "dp", "head"),
            P(None, "dp", "head"),
            P(None, "head", "dp"),
            P(None, "head", "dp"),
            P(None, "head", "dp"),
            P(None, "head", "dp"),
            P(None, "head", "dp"),
            P(),
            P(),
            P(),
            P(),
        ),
        check_vma=False,
    )
```

```python
import jax
import jax.numpy as jnp
from jax import lax
from jax.experimental import pallas as pl
from jax.experimental.pallas import tpu as pltpu
from jax.sharding import PartitionSpec as P

HEADS = 8
HS = 160
D = 1280
LAT = 256
STEP = 5


NORM_EPS = 1e-05
MASKED = -1e30
CLIP_RATE = 0.02
ADAM_EPS = 1e-08
DECAY_RATE = 0.1
NORM_RATE = 0.3
SMOOTH_RATE = 0.9


NM = 6
TOKENS = 16384
MESH = pl.DeviceIdType.MESH
NN = (((1,), (0,)), ((), ()))
NT = (((1,), (1,)), ((), ()))
TN = (((0,), (0,)), ((), ()))
ROWS = 512
CH = 64
SLOT = {5: 6, 4: 7, 3: 4, 0: 3, 1: 5, 2: 0}
RD_SLOTS = 2
RB_SLOTS = 3
ORDER = (5, 4, 3, 0, 1, 2)
PLACE = {0: 0, 1: 1, 2: 2, 4: 3, 3: 4, 5: 5}
ORD = {m: i for i, m in enumerate(ORDER)}
GATHER = "FMFMMF"
REDUCE = "FMFMMF"
BASE = [sum(8 if t == "F" else 9 for t in REDUCE[:i]) for i in range(7)]


def ids():
    d = lax.axis_index("dp")
    h = lax.axis_index("head")
    return d % 2, h // 2, d // 2, h % 2


def dev(x, y, z, c):
    return (z * 2 + x, y * 2 + c)


def dg(a, b, dims):
    return lax.dot_general(a, b, dims, preferred_element_type=jnp.float32)


def block_kernel(
    sh, lat_in, cot_in, live, norms,
    bo_out, lg_out, gout, nout,
    W, sh_in, lat, cot, n1, q, k, v, probs, att, resid, n2, act, gp, T,
    RD, RB, U, F, FX, NG, NX, SQ, SX,
    s0, r0, sz, rz, sa, ra, sb, rb, sd, rd,
    sD, rD, sB, rB, sU, rU, sF, rF, sN, rN, sS, rS, lsem, free, free_b,
):
    bf, f32 = jnp.bfloat16, jnp.float32
    x, y, z, c = ids()
    sib, xn, yn = dev(x, y, z, 1 - c), dev(1 - x, y, z, c), dev(x, 1 - y, z, c)
    zp = [dev(x, y, lax.rem(z + j, 4), c) for j in (1, 2, 3)]

    c_lat = pltpu.make_async_copy(lat_in, lat, lsem.at[0])
    c_cot = pltpu.make_async_copy(cot_in, cot, lsem.at[1])
    c_lat.start()
    c_cot.start()
    bar = pltpu.get_barrier_semaphore()
    for d in [sib, xn, yn] + zp:
        pl.semaphore_signal(bar, inc=1, device_id=d, device_id_type=MESH)
    pl.semaphore_wait(bar, 6)

    def cols(j):
        return pl.ds(pl.multiple_of(j * 640, 128), 640)

    def rc(src, dst, s, r, d):
        return pltpu.make_async_remote_copy(src, dst, s, r, device_id=d, device_id_type=MESH)

    def pick(a, b):
        return jnp.where(c == 0, a, b)

    an = tuple(pick(a, b) for a, b in zip(xn, yn))
    bn = tuple(pick(a, b) for a, b in zip(yn, xn))

    def at_x(a, b):
        return pick(1 - x if a else x, 1 - x if b else x)

    def at_y(a, b):
        return pick(1 - y if b else y, 1 - y if a else y)

    def unit(w, dz, a, b):
        return w.at[lax.rem(z + dz, 4), at_x(a, b), c, :, cols(at_y(a, b))]

    def line(w, a, b):
        return w.at[:, at_x(a, b), c, :, cols(at_y(a, b))]

    def g_pair(m):
        return rc(sh.at[m, 1 - c], sh_in.at[m], s0.at[m], r0.at[m], sib)

    def g_z(m, a, j, dz, i):
        u = unit(W.at[m], dz, a, 0)
        return rc(u, u, sz.at[m, a, i], rz.at[m, a, (dz - j) % 4], zp[j - 1])

    def g_a(m):
        u = line(W.at[m], 0, 0) if GATHER[m] == "F" else unit(W.at[m], 0, 0, 0)
        return rc(u, u, sa.at[m], ra.at[m], an)

    def g_b(m, a):
        u = line(W.at[m], a, 0)
        return rc(u, u, sb.at[m, a], rb.at[m, a], bn)

    def g_d(m, a, b):
        u = line(W.at[m], a, b)
        return rc(u, u, sd.at[m, 2 * a + b], rd.at[m, 2 * a + b], sib)

    def g_z_do(m, a, what):
        def act_on(cp):
            if what == "start":
                cp.start()
            else:
                cp.wait_send()

        act_on(g_z(m, a, 2, 0, 1))
        for j, end in ((1, 3), (3, 0)):
            @pl.when(z != end)
            def _():
                act_on(g_z(m, a, j, 0, j - 1))

    def g_z_on(m, a, what):
        for at, j in ((2, 1), (1, 3)):
            @pl.when(z == at)
            def _():
                if what == "start":
                    g_z(m, a, j, 2, 3).start()
                else:
                    g_z(m, a, j, 2, 3).wait_send()

    def g_p(m):
        g_pair(m).wait()
        own, oth = sh[m, c], sh_in[m]
        W[m, z, x, c, :, cols(y)] = jnp.concatenate(
            [jnp.where(c == 0, own, oth), jnp.where(c == 0, oth, own)], axis=-1
        )
        if GATHER[m] == "M":
            g_a(m).start()

    def g_go(m, a):
        if a:
            g_a(m).wait_recv()
        g_z_do(m, a, "start")

    def g_on(m, a):
        g_z(m, a, 2, 0, 1).wait_recv()
        g_z_on(m, a, "start")

    def g_line(m, a):
        if a and GATHER[m] == "F":
            g_a(m).wait_recv()
        else:
            for j in (1, 3):
                g_z(m, a, j, 0, j - 1).wait_recv()
        if not a and GATHER[m] == "F":
            g_a(m).start()
        g_b(m, a).start()
        g_d(m, a, 0).start()

    def g_far(m, a):
        g_b(m, a).wait_recv()
        g_d(m, a, 1).start()

    def g_end(m):
        for a in (0, 1):
            for b in (0, 1):
                g_d(m, a, b).wait()
            g_b(m, a).wait_send()
            if a == 0 or GATHER[m] == "M":
                g_z_do(m, a, "wait")
                g_z_on(m, a, "wait")
        g_a(m).wait_send()

    def r_d(i):
        return rc(W.at[SLOT[ORDER[i]], :, :, 1 - c], RD.at[i % RD_SLOTS], sD.at[i], rD.at[i], sib)

    def grd(i):
        return W.at[SLOT[ORDER[i]]]

    def r_b(i, a):
        return rc(line(grd(i), a, 1), RB.at[i % RB_SLOTS, a], sB.at[i, a], rB.at[i, a], bn)

    def r_a(i):
        k = BASE[i]
        if REDUCE[i] == "F":
            return rc(line(grd(i), 1, 0), U.at[pl.ds(k, 4)], sU.at[k], rU.at[k], an)
        return rc(unit(grd(i), 0, 1, 0), U.at[k], sU.at[k], rU.at[k], an)

    def place(i, a, rel):
        return BASE[i] + (4 if REDUCE[i] == "F" else 1) + 4 * a + rel

    def r_z(i, a, dz):
        k = place(i, a, 4 - dz)
        return rc(unit(grd(i), dz, a, 0), U.at[k], sU.at[place(i, a, dz)], rU.at[k], zp[dz - 1])

    def r_y(i, a, dz, j):
        k = place(i, a, 0)
        return rc(unit(grd(i), dz, a, 0), U.at[k], sU.at[place(i, a, dz)], rU.at[k], zp[j - 1])

    def r_f(m):
        return rc(F.at[m], FX.at[m], sF.at[m], rF.at[m], sib)

    def r_z_go(i, a):
        for dz, end, j in ((1, 3, 3), (3, 0, 1)):
            @pl.when(z == end)
            def _():
                r_y(i, a, dz, j).start()

            @pl.when(z != end)
            def _():
                r_z(i, a, dz).start()

    def st_r(i, a):
        @pl.when((z == 1) | (z == 2))
        def _():
            r_y(i, a, 1, 1).wait_recv()
            u = unit(grd(i), 2, a, 0)
            u[...] = u[...] + U[place(i, a, 0)]

        r_z(i, a, 2).start()

    def r_z_in(i, a):
        u = unit(grd(i), 0, a, 0)

        def add(rel):
            u[...] = u[...] + U[place(i, a, rel)]

        r_z(i, a, 2).wait_recv()
        add(2)
        for rel, end in ((3, 0), (1, 3)):
            @pl.when(z != end)
            def _():
                r_z(i, a, 4 - rel).wait_recv()
                add(rel)

    def r_z_end(i, a):
        for dz in (1, 2, 3):
            r_z(i, a, dz).wait_send()

    def add_line(i, a, src):
        kept = line(grd(i), a, 0)

        def body(j, _):
            kept[j] = kept[j] + src[j]
            return 0

        lax.fori_loop(0, 4, body, 0)

    def st_d(i):
        if i >= RD_SLOTS:
            pl.semaphore_wait(free, 1)
        r_d(i).start()

    def st_b(i):
        r_d(i).wait()
        g = grd(i)

        def body(j, _):
            a, b = j // 2, j % 2
            g[a, b, c] = g[a, b, c] + RD[i % RD_SLOTS, a, b]
            return 0

        lax.fori_loop(0, 8, body, 0)
        if i + RD_SLOTS < NM:
            pl.semaphore_signal(free, inc=1, device_id=sib, device_id_type=MESH)
        if i >= RB_SLOTS:
            pl.semaphore_wait(free_b, 1)
        r_b(i, 1).start()
        r_b(i, 0).start()

    def st_a(i):
        r_b(i, 1).wait()
        add_line(i, 1, RB.at[i % RB_SLOTS, 1])
        if REDUCE[i] == "F":
            r_a(i).start()
        else:
            r_z_go(i, 1)

    def st_c(i):
        r_b(i, 0).wait()
        add_line(i, 0, RB.at[i % RB_SLOTS, 0])
        if i + RB_SLOTS < NM:
            pl.semaphore_signal(free_b, inc=1, device_id=bn, device_id_type=MESH)
        if REDUCE[i] == "M":
            r_z_go(i, 0)

    def st_z(i):
        if REDUCE[i] == "F":
            r_a(i).wait()
            add_line(i, 0, U.at[pl.ds(BASE[i], 4)])
            r_z_go(i, 0)
        else:
            st_r(i, 1)

    def st_y(i):
        r_z_in(i, 1)
        r_a(i).start()

    def put(dst, w):
        dst[...] = jnp.where(c == 0, w[:, :320], w[:, 64:])

    def st_g(m):
        r_f(m).wait()
        put(gout.at[PLACE[m], 1 - c], FX[m])

    def st_f(i):
        m = ORDER[i]
        r_z_in(i, 0)
        f = unit(grd(i), 0, 0, 0)[...].astype(f32)
        if REDUCE[i] == "M":
            r_a(i).wait()
            f = f + U[BASE[i]].astype(f32)
            r_z_end(i, 1)
        r_z_end(i, 0)
        F[m] = jnp.where(c == 0, f[:, 256:], f[:, :384])
        mine = jnp.where(c == 0, f[:, :384], f[:, 256:])
        put(gout.at[PLACE[m], c], mine)
        r_f(m).start()
        ff = f * f
        ff = ff.reshape(10, 8, 640).sum(0)
        SQ[0] += ff[:, :128] + ff[:, 128:256] + ff[:, 256:384] + ff[:, 384:512] + ff[:, 512:]

    def mat(m):
        return W[m].reshape(D, D)

    def chunks(fn, init=0):
        return lax.fori_loop(
            0, ROWS // CH, lambda i, a: fn(pl.ds(pl.multiple_of(i * CH, CH), CH), a), init)

    def stats(vals):
        centre = vals - jnp.mean(vals, axis=-1, keepdims=True)
        r = lax.rsqrt(jnp.mean(centre * centre, axis=-1, keepdims=True) + NORM_EPS)
        return centre * r, r

    def ln_to(src, gi, dst):
        def body(r, a):
            xhat, _ = stats(src[r, :].astype(f32))
            dst[r, :] = (xhat * norms[gi:gi + 1, :] + norms[gi + 1:gi + 2, :]).astype(bf)
            return a

        chunks(body)

    def ln_back(src, gi, err, emit):
        def body(r, acc):
            xhat, inv = stats(src[r, :].astype(f32))
            e = err[r, :]
            eg = e * norms[gi:gi + 1, :]
            back = inv * (eg - jnp.mean(eg, axis=-1, keepdims=True)
                          - xhat * jnp.mean(eg * xhat, axis=-1, keepdims=True))
            emit(r, back)
            return (acc[0] + (e * xhat).reshape(CH // 8, 8, D).sum(0),
                    acc[1] + e.reshape(CH // 8, 8, D).sum(0))

        zero = jnp.zeros((8, D), f32)
        a, b = chunks(body, (zero, zero))
        NG[0, gi:gi + 1, :] = a.sum(0, keepdims=True)
        NG[0, gi + 1:gi + 2, :] = b.sum(0, keepdims=True)

    scale = HS ** (-0.5)
    lane = lax.broadcasted_iota(jnp.int32, (1, 256), 1)
    lane1 = lax.broadcasted_iota(jnp.int32, (1, 128), 1)

    def head_mask(hh):
        return jnp.where((lane >= 32 * hh) & (lane < 32 * hh + HS), 1.0, 0.0).astype(bf)

    def join(o, dst, rows, g):
        parts = [o[0][:, :128]]
        for hh in (1, 2, 3):
            parts.append(jnp.where(lane1 < 32 * hh, o[hh - 1][:, 128:], o[hh][:, :128]))
        parts.append(o[3][:, 128:])
        for j in range(5):
            dst[rows, pl.ds(pl.multiple_of(g * 640 + 128 * j, 128), 128)] = parts[j].astype(bf)

    h_first = (y * 2 + c) * 2

    def attn(i, g):
        rows = pl.ds(pl.multiple_of(i * LAT, LAT), LAT)
        count = live[h_first + i]
        outs = []
        for hh in range(4):
            win = pl.ds(pl.multiple_of(g * 640 + 128 * hh, 128), 256)
            s = dg(q[rows, win] * head_mask(hh), k[rows, win], NT) * scale
            s = jnp.where(lane < count, s, MASKED)
            e = jnp.exp(s - jnp.max(s, axis=-1, keepdims=True))
            p = (e * (1.0 / jnp.sum(e, axis=-1, keepdims=True))).astype(bf)
            probs[i * 8 + g * 4 + hh] = p
            outs.append(dg(p, v[rows, win], NN))
        join(outs, att, rows, g)

    def attn_back(i, g, do, dq, dk, dv):
        rows = pl.ds(pl.multiple_of(i * LAT, LAT), LAT)
        oq, ok, ov = [], [], []
        for hh in range(4):
            win = pl.ds(pl.multiple_of(g * 640 + 128 * hh, 128), 256)
            p = probs[i * 8 + g * 4 + hh]
            dow = do[rows, win]
            ov.append(dg(p, dow, TN))
            dp = dg(dow * head_mask(hh), v[rows, win], NT)
            pf = p.astype(f32)
            ds = (pf * (dp - jnp.sum(pf * dp, axis=-1, keepdims=True))).astype(bf)
            oq.append(dg(ds, k[rows, win], NN) * scale)
            ok.append(dg(ds, q[rows, win], TN) * scale)
        join(oq, dq, rows, g)
        join(ok, dk, rows, g)
        join(ov, dv, rows, g)

    def grad(m, left, right):
        W[SLOT[m]] = dg(left[...], right[...], TN).astype(bf).reshape(4, 2, 2, 80, D)
        st_d(ORD[m])

    def proj(dst, m):
        dst[...] = dg(n1[...], mat(m), NN).astype(bf)

    def begin():
        for m in range(NM):
            g_pair(m).start()
        g_p(0)
        g_go(0, 0)
        g_p(1)
        g_go(1, 0)
        for m in range(2, NM):
            g_p(m)
        g_go(1, 1)
        SQ[0] = jnp.zeros((8, 128), f32)

    def norm_one():
        c_lat.wait()
        ln_to(lat, 0, n1)

    def out_proj():
        T[...] = dg(att[...], mat(3), NT)

        def add_lat(r, a):
            resid[r, :] = T[r, :] + lat[r, :].astype(f32)
            return a

        chunks(add_lat)
        ln_to(resid, 2, n2)

    def up():
        T[...] = dg(n2[...], mat(4), NN)

        def gelu(r, a):
            p = T[r, :]
            cdf = 0.5 * (1.0 + lax.erf(p * (0.5 ** 0.5)))
            act[r, :] = (p * cdf).astype(bf)
            gp[r, :] = (cdf + p * (jnp.exp(-0.5 * p * p) * 0.3989422804014327)).astype(bf)
            return a

        chunks(gelu)
        c_cot.wait()

    def d_act():
        T[...] = dg(cot[...], mat(5), NN)

        def to_pre(r, a):
            gp[r, :] = (T[r, :] * gp[r, :].astype(f32)).astype(bf)
            return a

        chunks(to_pre)

    c_bo = pltpu.make_async_copy(act, bo_out, lsem.at[2])
    c_lg = pltpu.make_async_copy(n2, lg_out, lsem.at[3])

    def down():
        T[...] = dg(act[...], mat(5), NT)

        def to_bo(r, a):
            act[r, :] = (T[r, :] + resid[r, :]).astype(bf)
            return a

        chunks(to_bo)
        c_bo.start()

    def d_two():
        T[...] = dg(gp[...], mat(4), NT)

        def emit_two(r, back):
            d = cot[r, :].astype(f32) + back
            resid[r, :] = d
            n2[r, :] = d.astype(bf)

        ln_back(resid, 2, T, emit_two)

    def d_att():
        c_bo.wait()
        act[...] = dg(n2[...], mat(3), NN).astype(bf)

    def d_in(m, src):
        if m == 0:
            T[...] = dg(src[...], mat(0), NT)
        else:
            T[...] += dg(src[...], mat(m), NT)

    def d_one():
        def emit_one(r, back):
            n2[r, :] = (resid[r, :] + back).astype(bf)

        ln_back(lat, 0, T, emit_one)
        c_lg.start()

    def n_swap(t):
        return rc(NG.at[0], NX.at[t], sN.at[t], rN.at[t], ([sib, xn, yn] + zp)[t])

    def n_step(t):
        if t > 0:
            n_swap(t - 1).wait()
            NG[0] = NG[0] + NX[t - 1]
        for j in (t,) if t < 3 else (3, 4, 5):
            n_swap(j).start()

    def n_end():
        for j in (3, 4, 5):
            n_swap(j).wait()
        NG[0] = NG[0] + NX[3] + NX[4] + NX[5]

    def s_swap(t):
        return rc(SQ.at[0], SX.at[t], sS.at[t], rS.at[t], ([sib, xn, yn] + zp)[t])

    def finish():
        for t in range(3):
            s_swap(t).start()
            s_swap(t).wait()
            SQ[0] = SQ[0] + SX[t]
        for t in (3, 4, 5):
            s_swap(t).start()
        st_g(3)
        st_g(0)
        st_g(2)
        for t in (3, 4, 5):
            s_swap(t).wait()
        nout[0:4, :] = NG[0]
        tot = SQ[0] + SX[3] + SX[4] + SX[5]
        nout[4:8, :] = jnp.zeros((4, D), f32) + jnp.sum(tot)
        c_lg.wait()

    def heads(fn, g, i, *refs):
        fn(i, g, *refs)

    P0, P1, P2, P3 = ((heads, attn, g, i) for g in (0, 1) for i in (0, 1))
    Q0, Q1, Q2, Q3 = ((heads, attn_back, g, i, act, cot, gp, att) for g in (0, 1) for i in (0, 1))
    program = [
        (begin,),
        (g_on, 0, 0), (g_go, 2, 0), (g_line, 0, 0),
        (g_on, 1, 0), (g_on, 1, 1), (g_go, 3, 0), (g_go, 3, 1), (g_line, 1, 0), (g_line, 1, 1),
        (g_line, 0, 1), (norm_one,), (g_far, 0, 0),
        (g_on, 2, 0), (g_go, 4, 0), (g_go, 4, 1), (g_line, 2, 0),
        (g_far, 1, 0), (g_far, 0, 1), (g_end, 0),
        (proj, q, 0),
        (g_on, 3, 0), (g_on, 3, 1), (g_go, 5, 0), (g_line, 3, 0), (g_line, 3, 1),
        (g_line, 2, 1), (g_far, 2, 0), (g_far, 1, 1), (g_end, 1),
        (proj, k, 1),
        (g_on, 4, 0), (g_on, 4, 1), (g_line, 4, 0), (g_line, 4, 1),
        (g_far, 3, 0), (g_far, 2, 1), (g_end, 2),
        (proj, v, 2), P0,
        (g_on, 5, 0), (g_line, 5, 0), P1,
        (g_far, 4, 0), P2, (g_far, 3, 1), P3, (g_end, 3), (out_proj,),
        (g_line, 5, 1), (g_far, 5, 0), (g_far, 4, 1), (g_end, 4),
        (up,), (grad, 5, cot, act), (g_far, 5, 1),
        (st_b, 0), (g_end, 5), (d_act,), (grad, 4, n2, gp), (down,), (st_a, 0), (d_two,), (st_b, 1),
        (grad, 3, n2, att), (st_c, 0), (st_z, 0), (d_att,), Q0, (st_a, 1), (st_b, 2), Q1, Q2, (st_c, 1),
        (st_r, 0, 0), Q3, (st_z, 1), (grad, 0, n1, cot), (st_a, 2), (st_r, 1, 0), (grad, 1, n1, gp),
        (st_c, 2), (st_b, 3), (st_z, 2), (d_in, 0, cot), (st_a, 3), (st_b, 4), (grad, 2, n1, att), (st_c, 3),
        (st_a, 4), (st_b, 5), (d_in, 1, gp), (st_c, 4), (st_z, 4), (st_a, 5), (st_r, 4, 0), (d_in, 2, att),
        (st_y, 4), (st_z, 3), (st_c, 5), (st_r, 3, 0), (st_z, 5), (st_r, 2, 0), (st_y, 1), (st_f, 0),
        (d_one,), (n_step, 0), (st_f, 1), (st_f, 4), (n_step, 1), (st_r, 5, 0), (st_y, 3), (n_step, 2),
        (st_g, 5), (st_f, 2), (st_g, 4), (st_f, 3), (n_step, 3), (st_g, 1), (n_end,), (st_f, 5), (finish,),
    ]
    for fn, *given in program:
        fn(*given)


def run_block(sh, lat, cot, live, norms):
    bf, f32 = jnp.bfloat16, jnp.float32
    dma = pltpu.SemaphoreType.DMA
    act = pltpu.VMEM((ROWS, D), bf)
    wide = pltpu.VMEM((ROWS, D), f32)
    vm, hbm = pl.BlockSpec(memory_space=pltpu.VMEM), pl.BlockSpec(memory_space=pl.ANY)
    return pl.pallas_call(
        block_kernel,
        out_shape=(
            jax.ShapeDtypeStruct((ROWS, D), bf),
            jax.ShapeDtypeStruct((ROWS, D), bf),
            jax.ShapeDtypeStruct((NM, 2, 80, 320), f32),
            jax.ShapeDtypeStruct((8, D), f32),
        ),
        in_specs=[vm, hbm, hbm, pl.BlockSpec(memory_space=pltpu.SMEM), vm],
        out_specs=(hbm, hbm, vm, vm),
        scratch_shapes=[
            pltpu.VMEM((8, 4, 2, 2, 80, D), bf), pltpu.VMEM((NM, 80, 320), bf),
            act, act, act, act, act, act, pltpu.VMEM((16, LAT, LAT), bf), act, wide, act, act, act, wide,
            pltpu.VMEM((RD_SLOTS, 4, 2, 80, D), bf), pltpu.VMEM((RB_SLOTS, 2, 4, 80, 640), bf),
            pltpu.VMEM((BASE[6], 80, 640), bf),
            pltpu.VMEM((NM, 80, 384), f32), pltpu.VMEM((NM, 80, 384), f32),
            pltpu.VMEM((1, 4, D), f32), pltpu.VMEM((6, 4, D), f32),
            pltpu.VMEM((1, 8, 128), f32), pltpu.VMEM((6, 8, 128), f32),
            dma((NM,)), dma((NM,)), dma((NM, 2, 4)), dma((NM, 2, 4)), dma((NM,)), dma((NM,)),
            dma((NM, 2)), dma((NM, 2)), dma((NM, 4)), dma((NM, 4)),
            dma((NM,)), dma((NM,)), dma((NM, 2)), dma((NM, 2)), dma((BASE[6],)), dma((BASE[6],)),
            dma((NM,)), dma((NM,)), dma((6,)), dma((6,)), dma((6,)), dma((6,)), dma((4,)),
            pltpu.SemaphoreType.REGULAR, pltpu.SemaphoreType.REGULAR,
        ],
        compiler_params=pltpu.CompilerParams(
            collective_id=0, has_side_effects=True, vmem_limit_bytes=66 * 1000 * 1000),
        name="block",
    )(sh.reshape(NM, 2, 80, 320), lat, cot, live, norms)


def update_kernel(small, gin, gother, wi, fi, si, ai, wo, fo, so, ao, wn, fn, sn,
                  gn, mi, qi, ui, ei, bi, mo, qo, uo, eo, bo, mn, qn, un, tn):
    f32 = jnp.float32
    gnorm = small[0:4, :]
    norm = jnp.sqrt(small[4:5, 0:1] + jnp.sum(gnorm * gnorm, keepdims=True))
    factor = jnp.minimum(1.0, CLIP_RATE * D * TOKENS ** 0.5 / norm)

    def step(weight, grad, first, second, rate, decay, moment, square, update):
        moment_new, square_new, new = adam_step(weight, grad, first, second, rate, decay)
        moment[...] = moment_new
        square[...] = square_new
        update[...] = new
        return new

    new = step(wi[0], gin[0] * factor, fi[0], si[0], D ** (-0.5), DECAY_RATE,
               mi.at[0], qi.at[0], ui.at[0])
    ei[0] = SMOOTH_RATE * ai[0] + (1.0 - SMOOTH_RATE) * new
    bi[0] = new.astype(jnp.bfloat16)
    for j, rate in enumerate(((LAT / (3.0 * D)) ** 0.5, D ** (-0.5))):
        new = step(wo[j], gother[j] * factor, fo[j], so[j], rate, DECAY_RATE,
                   mo.at[j], qo.at[j], uo.at[j])
        eo[j] = SMOOTH_RATE * ao[j] + (1.0 - SMOOTH_RATE) * new
        bo[j] = new.astype(jnp.bfloat16)

    @pl.when(pl.program_id(0) == 0)
    def _():
        gn[...] = norm
        g = gnorm * factor
        step(wn[...], g, fn[...], sn[...], NORM_RATE, 0.0, mn, qn, un)
        tn[...] = g[2:4]


def run_update(small, grads, inner, outer, norm):
    f32, bf = jnp.float32, jnp.bfloat16
    vi = pl.BlockSpec((1, 160, 320), lambda i: (i, 0, 0))
    vo = pl.BlockSpec((2, 40, 320), lambda i: (0, i, 0))
    go = pl.BlockSpec((2, 40, 320), lambda i: (2, i, 0))

    def whole(*shape):
        return pl.BlockSpec(shape, lambda i: (0, 0))

    def out(shape, kind=f32):
        return jax.ShapeDtypeStruct(shape, kind)

    si, so = (4, 160, 320), (2, 160, 320)
    return pl.pallas_call(
        update_kernel,
        grid=(4,),
        out_shape=(out((1, 1)),) + (out(si),) * 4 + (out(si, bf),) + (out(so),) * 4 + (out(so, bf),)
        + (out((4, D)),) * 3 + (out((2, D)),),
        in_specs=[whole(8, D), vi, go] + [vi] * 4 + [vo] * 4 + [whole(4, D)] * 3,
        out_specs=(whole(1, 1),) + (vi,) * 5 + (vo,) * 5 + (whole(4, D),) * 3 + (whole(2, D),),
        compiler_params=pltpu.CompilerParams(vmem_limit_bytes=64 * 1000 * 1000),
        name="update",
    )(small, grads, grads, *inner, *outer, *norm)


def layer_norm(values, gain_row, bias_row):
    centre = values - jnp.mean(values, axis=-1, keepdims=True)
    spread = jnp.mean(centre * centre, axis=-1, keepdims=True)
    return centre * lax.rsqrt(spread + NORM_EPS) * gain_row + bias_row


def gelu_exact(values):
    return jax.nn.gelu(values, approximate=False)


def split_heads(matrix, item_count, head_count):
    return matrix.reshape(
        item_count, matrix.shape[0] // item_count, head_count, matrix.shape[1] // head_count
    )


def masked_scores(query_heads, key_heads, live_rows):
    scores = jnp.einsum(
        "iqhd,ikhd->ihqk", query_heads, key_heads, preferred_element_type=jnp.float32
    ) * HS ** (-0.5)
    length = key_heads.shape[1]
    valid = lax.broadcasted_iota(jnp.int32, (1, 1, 1, length), 3) < live_rows[:, None, None, None]
    return jnp.where(valid, scores, MASKED)


def attend(projected, live_rows, head_count):
    item_count = live_rows.shape[0]
    query_heads = split_heads(projected[0], item_count, head_count)
    key_heads = split_heads(projected[1], item_count, head_count)
    value_heads = split_heads(projected[2], item_count, head_count)
    scores = masked_scores(query_heads, key_heads, live_rows)
    row_peak = jnp.max(scores, axis=-1, keepdims=True)
    log_total = row_peak + jnp.log(jnp.sum(jnp.exp(scores - row_peak), axis=-1, keepdims=True))
    probs_b = jnp.exp(scores - log_total).astype(jnp.bfloat16)
    attended = jnp.einsum(
        "ihqk,ikhd->iqhd", probs_b, value_heads, preferred_element_type=jnp.float32
    )
    return (
        attended.reshape(projected.shape[1], projected.shape[2]).astype(jnp.bfloat16),
        log_total,
    )


def attend_back(projected, d_attended, log_total, live_rows, head_count):
    item_count = live_rows.shape[0]
    query_heads = split_heads(projected[0], item_count, head_count)
    key_heads = split_heads(projected[1], item_count, head_count)
    value_heads = split_heads(projected[2], item_count, head_count)
    back_heads = split_heads(d_attended, item_count, head_count)
    scores = masked_scores(query_heads, key_heads, live_rows)
    attn_probs = jnp.exp(scores - log_total)
    probs_b = attn_probs.astype(jnp.bfloat16)
    d_value = jnp.einsum("ihqk,iqhd->ikhd", probs_b, back_heads, preferred_element_type=jnp.float32)
    d_probs = jnp.einsum(
        "iqhd,ikhd->ihqk", back_heads, value_heads, preferred_element_type=jnp.float32
    )
    d_scores = (
        attn_probs * (d_probs - jnp.sum(attn_probs * d_probs, axis=-1, keepdims=True))
    ).astype(jnp.bfloat16)
    score_scale = HS ** (-0.5)
    d_query = (
        jnp.einsum("ihqk,ikhd->iqhd", d_scores, key_heads, preferred_element_type=jnp.float32)
        * score_scale
    )
    d_key = (
        jnp.einsum("ihqk,iqhd->ikhd", d_scores, query_heads, preferred_element_type=jnp.float32)
        * score_scale
    )
    flat_shape = projected.shape[1:]
    return jnp.stack(
        [d_query.reshape(flat_shape), d_key.reshape(flat_shape), d_value.reshape(flat_shape)]
    ).astype(jnp.bfloat16)


def adam_step(weight, grad, first, second, rate, decay):
    moment = 0.5 * first + 0.5 * grad
    square = 0.5 * second + 0.5 * grad * grad
    fix = 1.0 - 0.5**STEP
    update = weight - rate * (moment / fix / (jnp.sqrt(square / fix) + ADAM_EPS) + decay * weight)
    return (moment, square, update)


def plain(latents, live_keys, cotangent, inner_weights, outer_weights, norm_params):
    head_devices = lax.axis_size("head")
    data_devices = lax.axis_size("dp")
    row_count = latents.shape[0]
    item_count = row_count // LAT
    inner_b, outer_b = (
        lax.all_gather(
            lax.all_gather(inner_weights.astype(jnp.bfloat16), "dp", axis=1, tiled=True),
            "head", axis=2, tiled=True),
        lax.all_gather(
            lax.all_gather(outer_weights.astype(jnp.bfloat16), "dp", axis=2, tiled=True),
            "head", axis=1, tiled=True),
    )
    live_own = lax.dynamic_slice(
        live_keys, (lax.axis_index("head") * item_count,), (item_count,))
    source = latents.astype(jnp.float32)
    normed = layer_norm(source, norm_params[0], norm_params[1]).astype(jnp.bfloat16)
    qkv_b = inner_b[:3]
    proj_b = outer_b[0]
    up_b = inner_b[3]
    down_b = outer_b[1]
    projected = jnp.einsum(
        "rd,tdc->trc", normed, qkv_b, preferred_element_type=jnp.float32
    ).astype(jnp.bfloat16)
    attended, log_total = attend(projected, live_own, HEADS)
    residual = source + jnp.dot(attended, proj_b, preferred_element_type=jnp.float32)
    normed_two = layer_norm(residual, norm_params[2], norm_params[3]).astype(jnp.bfloat16)
    preact = jnp.dot(normed_two, up_b, preferred_element_type=jnp.float32)
    activation = gelu_exact(preact).astype(jnp.bfloat16)
    mlp_part = jnp.dot(activation, down_b, preferred_element_type=jnp.float32)
    block_output = (residual + mlp_part).astype(jnp.bfloat16)
    grad_down = jnp.einsum("rc,rd->cd", activation, cotangent, preferred_element_type=jnp.float32)
    d_activ = jnp.einsum("rd,cd->rc", cotangent, down_b, preferred_element_type=jnp.float32)
    gelu_back = jax.vjp(gelu_exact, preact)[1]
    d_pre = gelu_back(d_activ)[0].astype(jnp.bfloat16)
    grad_up = jnp.einsum("rd,rc->dc", normed_two, d_pre, preferred_element_type=jnp.float32)
    d_normed_two = jnp.einsum("rc,dc->rd", d_pre, up_b, preferred_element_type=jnp.float32)
    norm_back_two = jax.vjp(layer_norm, residual, norm_params[2], norm_params[3])[1]
    d_resid_norm, grad_gain_two, grad_bias_two = norm_back_two(d_normed_two)
    d_resid = cotangent.astype(jnp.float32) + d_resid_norm
    d_resid_b = d_resid.astype(jnp.bfloat16)
    grad_outproj = jnp.einsum(
        "rc,rd->cd", attended, d_resid_b, preferred_element_type=jnp.float32
    )
    d_attended = jnp.einsum(
        "rd,cd->rc", d_resid_b, proj_b, preferred_element_type=jnp.float32
    ).astype(jnp.bfloat16)
    d_proj = attend_back(projected, d_attended, log_total, live_own, HEADS)
    grad_qkv = jnp.einsum("rd,trc->tdc", normed, d_proj, preferred_element_type=jnp.float32)
    d_normed = jnp.einsum("trc,tdc->rd", d_proj, qkv_b, preferred_element_type=jnp.float32)
    norm_back_one = jax.vjp(layer_norm, source, norm_params[0], norm_params[1])[1]
    d_source_norm, grad_gain_one, grad_bias_one = norm_back_one(d_normed)
    latent_grad = (d_resid + d_source_norm).astype(jnp.bfloat16)
    grad_inner = jnp.concatenate([grad_qkv, grad_up[None]], axis=0)
    grad_outer = jnp.stack([grad_outproj, grad_down])
    grad_inner, grad_outer = (
        lax.psum_scatter(
            lax.psum_scatter(
                grad_inner.astype(jnp.bfloat16), "head", scatter_dimension=2, tiled=True
            ), "dp", scatter_dimension=1, tiled=True).astype(jnp.float32),
        lax.psum_scatter(
            lax.psum_scatter(
                grad_outer.astype(jnp.bfloat16), "head", scatter_dimension=1, tiled=True
            ), "dp", scatter_dimension=2, tiled=True).astype(jnp.float32),
    )
    norm_part = jnp.stack([grad_gain_one, grad_bias_one, grad_gain_two, grad_bias_two])
    local_squares = jnp.sum(grad_inner * grad_inner) + jnp.sum(grad_outer * grad_outer)
    grad_norms, squares_all = lax.psum((norm_part, local_squares), ("dp", "head"))
    return block_output, latent_grad, grad_inner, grad_outer, grad_norms, squares_all


def shards(
    latents,
    live_keys,
    cotangent,
    inner_weights,
    outer_weights,
    norm_params,
    inner_first,
    inner_second,
    inner_average,
    outer_first,
    outer_second,
    outer_average,
    norm_first,
    norm_second,
):
    head_devices = lax.axis_size("head")
    data_devices = lax.axis_size("dp")
    row_count = latents.shape[0]
    token_total = row_count * head_devices * data_devices
    if (data_devices, head_devices) == (8, 4) and token_total == TOKENS:
        sh = jnp.concatenate(
            [inner_weights[:3], outer_weights[:1].swapaxes(1, 2), inner_weights[3:],
             outer_weights[1:].swapaxes(1, 2)]).astype(jnp.bfloat16)
        block_output, latent_grad, grads, small = run_block(
            sh, latents, cotangent, live_keys, norm_params)
        outer = (outer_weights, outer_first, outer_second, outer_average)
        done = run_update(
            small, grads.reshape(NM, 160, 320),
            (inner_weights, inner_first, inner_second, inner_average),
            [v.swapaxes(1, 2) for v in outer], (norm_params, norm_first, norm_second))
        return (block_output, latent_grad, done[0][0, 0], *done[1:6],
                *(v.swapaxes(1, 2) for v in done[6:11]), *done[11:])
    block_output, latent_grad, grad_inner, grad_outer, grad_norms, squares_all = plain(
        latents, live_keys, cotangent, inner_weights, outer_weights, norm_params)
    grad_norm = jnp.sqrt(squares_all + jnp.sum(grad_norms * grad_norms))
    clip_limit = CLIP_RATE * D * token_total**0.5
    factor = jnp.minimum(1.0, clip_limit / grad_norm)
    inner_rate = D ** (-0.5)
    outer_rate = jnp.array([(LAT / (3.0 * D)) ** 0.5, D ** (-0.5)], dtype=jnp.float32).reshape(
        2, 1, 1
    )
    clipped_norms = grad_norms * factor
    inner_new = adam_step(
        inner_weights, grad_inner * factor, inner_first, inner_second, inner_rate, DECAY_RATE
    )
    outer_new = adam_step(
        outer_weights, grad_outer * factor, outer_first, outer_second, outer_rate, DECAY_RATE
    )
    norm_new = adam_step(norm_params, clipped_norms, norm_first, norm_second, NORM_RATE, 0.0)
    inner_smooth = SMOOTH_RATE * inner_average + (1.0 - SMOOTH_RATE) * inner_new[2]
    outer_smooth = SMOOTH_RATE * outer_average + (1.0 - SMOOTH_RATE) * outer_new[2]
    return (
        block_output,
        latent_grad,
        grad_norm,
        inner_new[0],
        inner_new[1],
        inner_new[2],
        inner_smooth,
        inner_new[2].astype(jnp.bfloat16),
        outer_new[0],
        outer_new[1],
        outer_new[2],
        outer_smooth,
        outer_new[2].astype(jnp.bfloat16),
        norm_new[0],
        norm_new[1],
        norm_new[2],
        clipped_norms[2:4],
    )


def solution(mesh):
    return jax.shard_map(
        shards,
        mesh=mesh,
        in_specs=(
            P(("dp", "head"), None),
            P("dp"),
            P(("dp", "head"), None),
            P(None, "dp", "head"),
            P(None, "head", "dp"),
            P(),
            P(None, "dp", "head"),
            P(None, "dp", "head"),
            P(None, "dp", "head"),
            P(None, "head", "dp"),
            P(None, "head", "dp"),
            P(None, "head", "dp"),
            P(),
            P(),
        ),
        out_specs=(
            P(("dp", "head"), None),
            P(("dp", "head"), None),
            P(),
            P(None, "dp", "head"),
            P(None, "dp", "head"),
            P(None, "dp", "head"),
            P(None, "dp", "head"),
            P(None, "dp", "head"),
            P(None, "head", "dp"),
            P(None, "head", "dp"),
            P(None, "head", "dp"),
            P(None, "head", "dp"),
            P(None, "head", "dp"),
            P(),
            P(),
            P(),
            P(),
        ),
        check_vma=False,
    )
```

```python
import jax
import jax.numpy as jnp
from jax import lax
from jax.experimental import pallas as pl
from jax.experimental.pallas import tpu as pltpu
from jax.sharding import PartitionSpec as P

HEADS = 8
HS = 160
D = 1280
LAT = 256
STEP = 5


NORM_EPS = 1e-05
MASKED = -1e30
CLIP_RATE = 0.02
ADAM_EPS = 1e-08
DECAY_RATE = 0.1
NORM_RATE = 0.3
SMOOTH_RATE = 0.9


NM = 6
TOKENS = 16384
MESH = pl.DeviceIdType.MESH
NN = (((1,), (0,)), ((), ()))
NT = (((1,), (1,)), ((), ()))
TN = (((0,), (0,)), ((), ()))
ROWS = 512
CH = 64
SLOT = {5: 6, 4: 7, 3: 4, 0: 3, 1: 5, 2: 0}
RD_SLOTS = 2
RB_SLOTS = 3
ORDER = (5, 4, 3, 0, 1, 2)
PLACE = {0: 0, 1: 1, 2: 2, 4: 3, 3: 4, 5: 5}
ORD = {m: i for i, m in enumerate(ORDER)}
GATHER = "FMFMMF"
REDUCE = "FMFMMF"
BASE = [sum(8 if t == "F" else 9 for t in REDUCE[:i]) for i in range(7)]


def ids():
    d = lax.axis_index("dp")
    h = lax.axis_index("head")
    return d % 2, h // 2, d // 2, h % 2


def dev(x, y, z, c):
    return (z * 2 + x, y * 2 + c)


def dg(a, b, dims):
    return lax.dot_general(a, b, dims, preferred_element_type=jnp.float32)


def block_kernel(
    sh, lat_in, cot_in, live, norms,
    bo_out, lg_out, gout, nout,
    W, sh_in, lat, cot, n1, q, k, v, probs, att, resid, n2, act, gp, T,
    RD, RB, U, F, FX, NG, NX, SQ, SX,
    s0, r0, sz, rz, sa, ra, sb, rb, sd, rd,
    sD, rD, sB, rB, sU, rU, sF, rF, sN, rN, sS, rS, lsem, free, free_b,
):
    bf, f32 = jnp.bfloat16, jnp.float32
    x, y, z, c = ids()
    sib, xn, yn = dev(x, y, z, 1 - c), dev(1 - x, y, z, c), dev(x, 1 - y, z, c)
    zp = [dev(x, y, lax.rem(z + j, 4), c) for j in (1, 2, 3)]

    c_lat = pltpu.make_async_copy(lat_in, lat, lsem.at[0])
    c_cot = pltpu.make_async_copy(cot_in, cot, lsem.at[1])
    c_lat.start()
    c_cot.start()
    bar = pltpu.get_barrier_semaphore()
    plane = [xn, yn] + [
        dev(1 - x if i else x, 1 - y if j else y, z, 1 - c if o else c)
        for i, j, o in ((1, 1, 0), (1, 0, 1), (0, 1, 1), (1, 1, 1))
    ]
    for d in [sib] + plane + zp:
        pl.semaphore_signal(bar, inc=1, device_id=d, device_id_type=MESH)
    pl.semaphore_wait(bar, 10)

    def cols(j):
        return pl.ds(pl.multiple_of(j * 640, 128), 640)

    def rc(src, dst, s, r, d):
        return pltpu.make_async_remote_copy(src, dst, s, r, device_id=d, device_id_type=MESH)

    def pick(a, b):
        return jnp.where(c == 0, a, b)

    an = tuple(pick(a, b) for a, b in zip(xn, yn))
    bn = tuple(pick(a, b) for a, b in zip(yn, xn))

    def at_x(a, b):
        return pick(1 - x if a else x, 1 - x if b else x)

    def at_y(a, b):
        return pick(1 - y if b else y, 1 - y if a else y)

    def unit(w, dz, a, b):
        return w.at[lax.rem(z + dz, 4), at_x(a, b), c, :, cols(at_y(a, b))]

    def line(w, a, b):
        return w.at[:, at_x(a, b), c, :, cols(at_y(a, b))]

    def g_pair(m):
        return rc(sh.at[m, 1 - c], sh_in.at[m], s0.at[m], r0.at[m], sib)

    def g_z(m, a, j, dz, i):
        u = unit(W.at[m], dz, a, 0)
        return rc(u, u, sz.at[m, a, i], rz.at[m, a, (dz - j) % 4], zp[j - 1])

    def g_a(m):
        u = line(W.at[m], 0, 0) if GATHER[m] == "F" else unit(W.at[m], 0, 0, 0)
        return rc(u, u, sa.at[m], ra.at[m], an)

    def g_b(m, a):
        u = line(W.at[m], a, 0)
        return rc(u, u, sb.at[m, a], rb.at[m, a], bn)

    def g_d(m, a, b):
        u = line(W.at[m], a, b)
        return rc(u, u, sd.at[m, 2 * a + b], rd.at[m, 2 * a + b], sib)

    def g_z_do(m, a, what):
        def act_on(cp):
            if what == "start":
                cp.start()
            else:
                cp.wait_send()

        act_on(g_z(m, a, 2, 0, 1))
        for j, end in ((1, 3), (3, 0)):
            @pl.when(z != end)
            def _():
                act_on(g_z(m, a, j, 0, j - 1))

    def g_z_on(m, a, what):
        for at, j in ((2, 1), (1, 3)):
            @pl.when(z == at)
            def _():
                if what == "start":
                    g_z(m, a, j, 2, 3).start()
                else:
                    g_z(m, a, j, 2, 3).wait_send()

    def g_p(m):
        g_pair(m).wait()
        own, oth = sh[m, c], sh_in[m]
        W[m, z, x, c, :, cols(y)] = jnp.concatenate(
            [jnp.where(c == 0, own, oth), jnp.where(c == 0, oth, own)], axis=-1
        )
        if GATHER[m] == "M":
            g_a(m).start()

    def g_go(m, a):
        if a:
            g_a(m).wait_recv()
        g_z_do(m, a, "start")

    def g_on(m, a):
        g_z(m, a, 2, 0, 1).wait_recv()
        g_z_on(m, a, "start")

    def g_line(m, a):
        if a and GATHER[m] == "F":
            g_a(m).wait_recv()
        else:
            for j in (1, 3):
                g_z(m, a, j, 0, j - 1).wait_recv()
        if not a and GATHER[m] == "F":
            g_a(m).start()
        g_b(m, a).start()
        g_d(m, a, 0).start()

    def g_far(m, a):
        g_b(m, a).wait_recv()
        g_d(m, a, 1).start()

    def g_end(m):
        for a in (0, 1):
            for b in (0, 1):
                g_d(m, a, b).wait()
            g_b(m, a).wait_send()
            if a == 0 or GATHER[m] == "M":
                g_z_do(m, a, "wait")
                g_z_on(m, a, "wait")
        g_a(m).wait_send()

    def r_d(i):
        return rc(W.at[SLOT[ORDER[i]], :, :, 1 - c], RD.at[i % RD_SLOTS], sD.at[i], rD.at[i], sib)

    def grd(i):
        return W.at[SLOT[ORDER[i]]]

    def r_b(i, a):
        return rc(line(grd(i), a, 1), RB.at[i % RB_SLOTS, a], sB.at[i, a], rB.at[i, a], bn)

    def r_a(i):
        k = BASE[i]
        if REDUCE[i] == "F":
            return rc(line(grd(i), 1, 0), U.at[pl.ds(k, 4)], sU.at[k], rU.at[k], an)
        return rc(unit(grd(i), 0, 1, 0), U.at[k], sU.at[k], rU.at[k], an)

    def place(i, a, rel):
        return BASE[i] + (4 if REDUCE[i] == "F" else 1) + 4 * a + rel

    def r_z(i, a, dz):
        k = place(i, a, 4 - dz)
        return rc(unit(grd(i), dz, a, 0), U.at[k], sU.at[place(i, a, dz)], rU.at[k], zp[dz - 1])

    def r_y(i, a, dz, j):
        k = place(i, a, 0)
        return rc(unit(grd(i), dz, a, 0), U.at[k], sU.at[place(i, a, dz)], rU.at[k], zp[j - 1])

    def r_f(m):
        return rc(F.at[m], FX.at[m], sF.at[m], rF.at[m], sib)

    def r_z_go(i, a):
        for dz, end, j in ((1, 3, 3), (3, 0, 1)):
            @pl.when(z == end)
            def _():
                r_y(i, a, dz, j).start()

            @pl.when(z != end)
            def _():
                r_z(i, a, dz).start()

    def st_r(i, a):
        @pl.when((z == 1) | (z == 2))
        def _():
            r_y(i, a, 1, 1).wait_recv()
            u = unit(grd(i), 2, a, 0)
            u[...] = u[...] + U[place(i, a, 0)]

        r_z(i, a, 2).start()

    def r_z_in(i, a):
        u = unit(grd(i), 0, a, 0)

        def add(rel):
            u[...] = u[...] + U[place(i, a, rel)]

        r_z(i, a, 2).wait_recv()
        add(2)
        for rel, end in ((3, 0), (1, 3)):
            @pl.when(z != end)
            def _():
                r_z(i, a, 4 - rel).wait_recv()
                add(rel)

    def r_z_end(i, a):
        for dz in (1, 2, 3):
            r_z(i, a, dz).wait_send()

    def add_line(i, a, src):
        kept = line(grd(i), a, 0)

        def body(j, _):
            kept[j] = kept[j] + src[j]
            return 0

        lax.fori_loop(0, 4, body, 0)

    def st_d(i):
        if i >= RD_SLOTS:
            pl.semaphore_wait(free, 1)
        r_d(i).start()

    def st_b(i):
        r_d(i).wait()
        g = grd(i)

        def body(j, _):
            a, b = j // 2, j % 2
            g[a, b, c] = g[a, b, c] + RD[i % RD_SLOTS, a, b]
            return 0

        lax.fori_loop(0, 8, body, 0)
        if i + RD_SLOTS < NM:
            pl.semaphore_signal(free, inc=1, device_id=sib, device_id_type=MESH)
        if i >= RB_SLOTS:
            pl.semaphore_wait(free_b, 1)
        r_b(i, 1).start()
        r_b(i, 0).start()

    def st_a(i):
        r_b(i, 1).wait()
        add_line(i, 1, RB.at[i % RB_SLOTS, 1])
        if REDUCE[i] == "F":
            r_a(i).start()
        else:
            r_z_go(i, 1)

    def st_c(i):
        r_b(i, 0).wait()
        add_line(i, 0, RB.at[i % RB_SLOTS, 0])
        if i + RB_SLOTS < NM:
            pl.semaphore_signal(free_b, inc=1, device_id=bn, device_id_type=MESH)
        if REDUCE[i] == "M":
            r_z_go(i, 0)

    def st_z(i):
        if REDUCE[i] == "F":
            r_a(i).wait()
            add_line(i, 0, U.at[pl.ds(BASE[i], 4)])
            r_z_go(i, 0)
        else:
            st_r(i, 1)

    def st_y(i):
        r_z_in(i, 1)
        r_a(i).start()

    def put(dst, w):
        dst[...] = jnp.where(c == 0, w[:, :320], w[:, 64:])

    def st_g(m):
        r_f(m).wait()
        put(gout.at[PLACE[m], 1 - c], FX[m])

    def st_f(i):
        m = ORDER[i]
        r_z_in(i, 0)
        f = unit(grd(i), 0, 0, 0)[...].astype(f32)
        if REDUCE[i] == "M":
            r_a(i).wait()
            f = f + U[BASE[i]].astype(f32)
            r_z_end(i, 1)
        r_z_end(i, 0)
        F[m] = jnp.where(c == 0, f[:, 256:], f[:, :384])
        mine = jnp.where(c == 0, f[:, :384], f[:, 256:])
        put(gout.at[PLACE[m], c], mine)
        r_f(m).start()
        ff = f * f
        ff = ff.reshape(10, 8, 640).sum(0)
        SQ[0] += ff[:, :128] + ff[:, 128:256] + ff[:, 256:384] + ff[:, 384:512] + ff[:, 512:]

    def mat(m):
        return W[m].reshape(D, D)

    def chunks(fn, init=0):
        return lax.fori_loop(
            0, ROWS // CH, lambda i, a: fn(pl.ds(pl.multiple_of(i * CH, CH), CH), a), init)

    def stats(vals):
        centre = vals - jnp.mean(vals, axis=-1, keepdims=True)
        r = lax.rsqrt(jnp.mean(centre * centre, axis=-1, keepdims=True) + NORM_EPS)
        return centre * r, r

    def ln_to(src, gi, dst):
        def body(r, a):
            xhat, _ = stats(src[r, :].astype(f32))
            dst[r, :] = (xhat * norms[gi:gi + 1, :] + norms[gi + 1:gi + 2, :]).astype(bf)
            return a

        chunks(body)

    def ln_back(src, gi, err, emit):
        def body(r, acc):
            xhat, inv = stats(src[r, :].astype(f32))
            e = err[r, :]
            eg = e * norms[gi:gi + 1, :]
            back = inv * (eg - jnp.mean(eg, axis=-1, keepdims=True)
                          - xhat * jnp.mean(eg * xhat, axis=-1, keepdims=True))
            emit(r, back)
            return (acc[0] + (e * xhat).reshape(CH // 8, 8, D).sum(0),
                    acc[1] + e.reshape(CH // 8, 8, D).sum(0))

        zero = jnp.zeros((8, D), f32)
        a, b = chunks(body, (zero, zero))
        NG[0, gi:gi + 1, :] = a.sum(0, keepdims=True)
        NG[0, gi + 1:gi + 2, :] = b.sum(0, keepdims=True)

    scale = HS ** (-0.5)
    lane = lax.broadcasted_iota(jnp.int32, (1, 256), 1)
    lane1 = lax.broadcasted_iota(jnp.int32, (1, 128), 1)

    def head_mask(hh):
        return jnp.where((lane >= 32 * hh) & (lane < 32 * hh + HS), 1.0, 0.0).astype(bf)

    def join(o, dst, rows, g):
        parts = [o[0][:, :128]]
        for hh in (1, 2, 3):
            parts.append(jnp.where(lane1 < 32 * hh, o[hh - 1][:, 128:], o[hh][:, :128]))
        parts.append(o[3][:, 128:])
        for j in range(5):
            dst[rows, pl.ds(pl.multiple_of(g * 640 + 128 * j, 128), 128)] = parts[j].astype(bf)

    h_first = (y * 2 + c) * 2

    def attn(i, g):
        rows = pl.ds(pl.multiple_of(i * LAT, LAT), LAT)
        count = live[h_first + i]
        outs = []
        for hh in range(4):
            win = pl.ds(pl.multiple_of(g * 640 + 128 * hh, 128), 256)
            s = dg(q[rows, win] * head_mask(hh), k[rows, win], NT) * scale
            s = jnp.where(lane < count, s, MASKED)
            e = jnp.exp(s - jnp.max(s, axis=-1, keepdims=True))
            p = (e * (1.0 / jnp.sum(e, axis=-1, keepdims=True))).astype(bf)
            probs[i * 8 + g * 4 + hh] = p
            outs.append(dg(p, v[rows, win], NN))
        join(outs, att, rows, g)

    def attn_back(i, g, do, dq, dk, dv):
        rows = pl.ds(pl.multiple_of(i * LAT, LAT), LAT)
        oq, ok, ov = [], [], []
        for hh in range(4):
            win = pl.ds(pl.multiple_of(g * 640 + 128 * hh, 128), 256)
            p = probs[i * 8 + g * 4 + hh]
            dow = do[rows, win]
            ov.append(dg(p, dow, TN))
            dp = dg(dow * head_mask(hh), v[rows, win], NT)
            pf = p.astype(f32)
            ds = (pf * (dp - jnp.sum(pf * dp, axis=-1, keepdims=True))).astype(bf)
            oq.append(dg(ds, k[rows, win], NN) * scale)
            ok.append(dg(ds, q[rows, win], TN) * scale)
        join(oq, dq, rows, g)
        join(ok, dk, rows, g)
        join(ov, dv, rows, g)

    def grad(m, left, right):
        W[SLOT[m]] = dg(left[...], right[...], TN).astype(bf).reshape(4, 2, 2, 80, D)
        st_d(ORD[m])

    def proj(dst, m):
        dst[...] = dg(n1[...], mat(m), NN).astype(bf)

    def begin():
        for m in range(NM):
            g_pair(m).start()
        g_p(0)
        g_go(0, 0)
        g_p(1)
        g_go(1, 0)
        for m in range(2, NM):
            g_p(m)
        g_go(1, 1)
        SQ[0] = jnp.zeros((8, 128), f32)

    def norm_one():
        c_lat.wait()
        ln_to(lat, 0, n1)

    def out_proj():
        T[...] = dg(att[...], mat(3), NT)

        def add_lat(r, a):
            resid[r, :] = T[r, :] + lat[r, :].astype(f32)
            return a

        chunks(add_lat)
        ln_to(resid, 2, n2)

    def up():
        T[...] = dg(n2[...], mat(4), NN)

        def gelu(r, a):
            p = T[r, :]
            cdf = 0.5 * (1.0 + lax.erf(p * (0.5 ** 0.5)))
            act[r, :] = (p * cdf).astype(bf)
            gp[r, :] = (cdf + p * (jnp.exp(-0.5 * p * p) * 0.3989422804014327)).astype(bf)
            return a

        chunks(gelu)
        c_cot.wait()

    def d_act():
        T[...] = dg(cot[...], mat(5), NN)

        def to_pre(r, a):
            gp[r, :] = (T[r, :] * gp[r, :].astype(f32)).astype(bf)
            return a

        chunks(to_pre)

    c_bo = pltpu.make_async_copy(act, bo_out, lsem.at[2])
    c_lg = pltpu.make_async_copy(n2, lg_out, lsem.at[3])

    def down():
        T[...] = dg(act[...], mat(5), NT)

        def to_bo(r, a):
            act[r, :] = (T[r, :] + resid[r, :]).astype(bf)
            return a

        chunks(to_bo)
        c_bo.start()

    def d_two():
        T[...] = dg(gp[...], mat(4), NT)

        def emit_two(r, back):
            d = cot[r, :].astype(f32) + back
            resid[r, :] = d
            n2[r, :] = d.astype(bf)

        ln_back(resid, 2, T, emit_two)

    def d_att():
        c_bo.wait()
        act[...] = dg(n2[...], mat(3), NN).astype(bf)

    def d_in(m, src):
        if m == 0:
            T[...] = dg(src[...], mat(0), NT)
        else:
            T[...] += dg(src[...], mat(m), NT)

    def d_one():
        def emit_one(r, back):
            n2[r, :] = (resid[r, :] + back).astype(bf)

        ln_back(lat, 0, T, emit_one)
        c_lg.start()

    def n_swap(t):
        return rc(NG.at[0], NX.at[t], sN.at[t], rN.at[t], ([sib, xn, yn] + zp)[t])

    def sum_z(own, one, two, three):
        even = lax.rem(z, 2) == 0
        return (own + jnp.where(even, three, one)) + (two + jnp.where(even, one, three))

    def n_step(t):
        if t > 0:
            n_swap(t - 1).wait()
            NG[0] = NG[0] + NX[t - 1]
        for j in (t,) if t < 3 else (3, 4, 5):
            n_swap(j).start()

    def n_end():
        for j in (3, 4, 5):
            n_swap(j).wait()
        NG[0] = sum_z(NG[0], NX[3], NX[4], NX[5])

    def s_swap(t):
        return rc(SQ.at[0], SX.at[t], sS.at[t], rS.at[t], (zp + [sib] + plane)[t])

    def finish():
        for t in range(3):
            s_swap(t).start()
        for t in range(3):
            s_swap(t).wait()
        SQ[0] = sum_z(SQ[0], SX[0], SX[1], SX[2])
        for t in range(3, 10):
            s_swap(t).start()
        st_g(3)
        st_g(0)
        st_g(2)
        nout[0:4, :] = NG[0]
        for t in range(3, 10):
            s_swap(t).wait()
        tot = ((SQ[0] + SX[4]) + (SX[5] + SX[6])) + ((SX[3] + SX[7]) + (SX[8] + SX[9]))
        nout[4:8, :] = jnp.zeros((4, D), f32) + jnp.sum(tot)
        c_lg.wait()

    def heads(fn, g, i, *refs):
        fn(i, g, *refs)

    P0, P1, P2, P3 = ((heads, attn, g, i) for g in (0, 1) for i in (0, 1))
    Q0, Q1, Q2, Q3 = ((heads, attn_back, g, i, act, cot, gp, att) for g in (0, 1) for i in (0, 1))
    program = [
        (begin,),
        (g_on, 0, 0), (g_go, 2, 0), (g_line, 0, 0),
        (g_on, 1, 0), (g_on, 1, 1), (g_go, 3, 0), (g_go, 3, 1), (g_line, 1, 0), (g_line, 1, 1),
        (g_line, 0, 1), (norm_one,), (g_far, 0, 0),
        (g_on, 2, 0), (g_go, 4, 0), (g_go, 4, 1), (g_line, 2, 0),
        (g_far, 1, 0), (g_far, 0, 1), (g_end, 0),
        (proj, q, 0),
        (g_on, 3, 0), (g_on, 3, 1), (g_go, 5, 0), (g_line, 3, 0), (g_line, 3, 1),
        (g_line, 2, 1), (g_far, 2, 0), (g_far, 1, 1), (g_end, 1),
        (proj, k, 1),
        (g_on, 4, 0), (g_on, 4, 1), (g_line, 4, 0), (g_line, 4, 1),
        (g_far, 3, 0), (g_far, 2, 1), (g_end, 2),
        (proj, v, 2), P0,
        (g_on, 5, 0), (g_line, 5, 0), P1,
        (g_far, 4, 0), P2, (g_far, 3, 1), P3, (g_end, 3), (out_proj,),
        (g_line, 5, 1), (g_far, 5, 0), (g_far, 4, 1), (g_end, 4),
        (up,), (grad, 5, cot, act), (g_far, 5, 1),
        (st_b, 0), (g_end, 5), (d_act,), (grad, 4, n2, gp), (down,), (st_a, 0), (d_two,), (st_b, 1),
        (grad, 3, n2, att), (st_c, 0), (st_z, 0), (d_att,), Q0, (st_a, 1), (st_b, 2), Q1, Q2, (st_c, 1),
        (st_r, 0, 0), Q3, (st_z, 1), (grad, 0, n1, cot), (st_a, 2), (st_r, 1, 0), (grad, 1, n1, gp),
        (st_c, 2), (st_b, 3), (st_z, 2), (d_in, 0, cot), (st_a, 3), (st_b, 4), (grad, 2, n1, att), (st_c, 3),
        (st_a, 4), (st_b, 5), (d_in, 1, gp), (st_c, 4), (st_z, 4), (st_a, 5), (st_r, 4, 0), (d_in, 2, att),
        (st_y, 4), (st_z, 3), (st_c, 5), (st_r, 3, 0), (st_z, 5), (st_r, 2, 0), (st_y, 1), (st_f, 0),
        (d_one,), (n_step, 0), (st_f, 1), (st_f, 4), (n_step, 1), (st_r, 5, 0), (st_y, 3), (n_step, 2),
        (st_g, 5), (st_f, 2), (st_g, 4), (st_f, 3), (n_step, 3), (st_g, 1), (n_end,), (st_f, 5), (finish,),
    ]
    for fn, *given in program:
        fn(*given)


def run_block(sh, lat, cot, live, norms):
    bf, f32 = jnp.bfloat16, jnp.float32
    dma = pltpu.SemaphoreType.DMA
    act = pltpu.VMEM((ROWS, D), bf)
    wide = pltpu.VMEM((ROWS, D), f32)
    vm, hbm = pl.BlockSpec(memory_space=pltpu.VMEM), pl.BlockSpec(memory_space=pl.ANY)
    return pl.pallas_call(
        block_kernel,
        out_shape=(
            jax.ShapeDtypeStruct((ROWS, D), bf),
            jax.ShapeDtypeStruct((ROWS, D), bf),
            jax.ShapeDtypeStruct((NM, 2, 80, 320), f32),
            jax.ShapeDtypeStruct((8, D), f32),
        ),
        in_specs=[vm, hbm, hbm, pl.BlockSpec(memory_space=pltpu.SMEM), vm],
        out_specs=(hbm, hbm, vm, vm),
        scratch_shapes=[
            pltpu.VMEM((8, 4, 2, 2, 80, D), bf), pltpu.VMEM((NM, 80, 320), bf),
            act, act, act, act, act, act, pltpu.VMEM((16, LAT, LAT), bf), act, wide, act, act, act, wide,
            pltpu.VMEM((RD_SLOTS, 4, 2, 80, D), bf), pltpu.VMEM((RB_SLOTS, 2, 4, 80, 640), bf),
            pltpu.VMEM((BASE[6], 80, 640), bf),
            pltpu.VMEM((NM, 80, 384), f32), pltpu.VMEM((NM, 80, 384), f32),
            pltpu.VMEM((1, 4, D), f32), pltpu.VMEM((6, 4, D), f32),
            pltpu.VMEM((1, 8, 128), f32), pltpu.VMEM((10, 8, 128), f32),
            dma((NM,)), dma((NM,)), dma((NM, 2, 4)), dma((NM, 2, 4)), dma((NM,)), dma((NM,)),
            dma((NM, 2)), dma((NM, 2)), dma((NM, 4)), dma((NM, 4)),
            dma((NM,)), dma((NM,)), dma((NM, 2)), dma((NM, 2)), dma((BASE[6],)), dma((BASE[6],)),
            dma((NM,)), dma((NM,)), dma((6,)), dma((6,)), dma((10,)), dma((10,)), dma((4,)),
            pltpu.SemaphoreType.REGULAR, pltpu.SemaphoreType.REGULAR,
        ],
        compiler_params=pltpu.CompilerParams(
            collective_id=0, has_side_effects=True, vmem_limit_bytes=66 * 1000 * 1000),
        name="block",
    )(sh.reshape(NM, 2, 80, 320), lat, cot, live, norms)


def update_kernel(small, gin, gother, wi, fi, si, ai, wo, fo, so, ao, wn, fn, sn,
                  gn, mi, qi, ui, ei, bi, mo, qo, uo, eo, bo, mn, qn, un, tn):
    f32 = jnp.float32
    gnorm = small[0:4, :]
    norm = jnp.sqrt(small[4:5, 0:1] + jnp.sum(gnorm * gnorm, keepdims=True))
    factor = jnp.minimum(1.0, CLIP_RATE * D * TOKENS ** 0.5 / norm)

    def step(weight, grad, first, second, rate, decay, moment, square, update):
        moment_new = 0.5 * first + 0.5 * grad
        square_new = 0.5 * second + 0.5 * grad * grad
        fix = 1.0 / (1.0 - 0.5 ** STEP)
        new = weight - rate * (
            moment_new * fix / (jnp.sqrt(square_new * fix) + ADAM_EPS) + decay * weight)
        moment[...] = moment_new
        square[...] = square_new
        update[...] = new
        return new

    new = step(wi[...], gin[...] * factor, fi[...], si[...], D ** (-0.5), DECAY_RATE, mi, qi, ui)
    ei[...] = SMOOTH_RATE * ai[...] + (1.0 - SMOOTH_RATE) * new
    bi[...] = new.astype(jnp.bfloat16)
    part = wo.shape[0]
    row = lax.broadcasted_iota(jnp.int32, (part, 1), 0) + part * pl.program_id(0)
    rate = jnp.where(row < 160, (LAT / (3.0 * D)) ** 0.5, D ** (-0.5))
    new = step(wo[...], gother[...] * factor, fo[...], so[...], rate, DECAY_RATE, mo, qo, uo)
    eo[...] = SMOOTH_RATE * ao[...] + (1.0 - SMOOTH_RATE) * new
    bo[...] = new.astype(jnp.bfloat16)

    @pl.when(pl.program_id(0) == 0)
    def _():
        gn[...] = norm
        g = gnorm * factor
        step(wn[...], g, fn[...], sn[...], NORM_RATE, 0.0, mn, qn, un)
        tn[...] = g[2:4]


def run_update(small, grads, inner, outer, norm):
    f32, bf = jnp.float32, jnp.bfloat16
    steps = 2
    vi = pl.BlockSpec((640 // steps, 320), lambda i: (i, 0))
    vo = pl.BlockSpec((320 // steps, 320), lambda i: (i, 0))
    go = pl.BlockSpec((320 // steps, 320), lambda i: (i + 2 * steps, 0))

    def whole(*shape):
        return pl.BlockSpec(shape, lambda i: (0, 0))

    def out(shape, kind=f32):
        return jax.ShapeDtypeStruct(shape, kind)

    si, so = (640, 320), (320, 320)
    return pl.pallas_call(
        update_kernel,
        grid=(steps,),
        out_shape=(out((1, 1)),) + (out(si),) * 4 + (out(si, bf),) + (out(so),) * 4 + (out(so, bf),)
        + (out((4, D)),) * 3 + (out((2, D)),),
        in_specs=[whole(8, D), vi, go] + [vi] * 4 + [vo] * 4 + [whole(4, D)] * 3,
        out_specs=(whole(1, 1),) + (vi,) * 5 + (vo,) * 5 + (whole(4, D),) * 3 + (whole(2, D),),
        compiler_params=pltpu.CompilerParams(vmem_limit_bytes=64 * 1000 * 1000),
        name="update",
    )(small, grads, grads, *inner, *outer, *norm)


def layer_norm(values, gain_row, bias_row):
    centre = values - jnp.mean(values, axis=-1, keepdims=True)
    spread = jnp.mean(centre * centre, axis=-1, keepdims=True)
    return centre * lax.rsqrt(spread + NORM_EPS) * gain_row + bias_row


def gelu_exact(values):
    return jax.nn.gelu(values, approximate=False)


def split_heads(matrix, item_count, head_count):
    return matrix.reshape(
        item_count, matrix.shape[0] // item_count, head_count, matrix.shape[1] // head_count
    )


def masked_scores(query_heads, key_heads, live_rows):
    scores = jnp.einsum(
        "iqhd,ikhd->ihqk", query_heads, key_heads, preferred_element_type=jnp.float32
    ) * HS ** (-0.5)
    length = key_heads.shape[1]
    valid = lax.broadcasted_iota(jnp.int32, (1, 1, 1, length), 3) < live_rows[:, None, None, None]
    return jnp.where(valid, scores, MASKED)


def attend(projected, live_rows, head_count):
    item_count = live_rows.shape[0]
    query_heads = split_heads(projected[0], item_count, head_count)
    key_heads = split_heads(projected[1], item_count, head_count)
    value_heads = split_heads(projected[2], item_count, head_count)
    scores = masked_scores(query_heads, key_heads, live_rows)
    row_peak = jnp.max(scores, axis=-1, keepdims=True)
    log_total = row_peak + jnp.log(jnp.sum(jnp.exp(scores - row_peak), axis=-1, keepdims=True))
    probs_b = jnp.exp(scores - log_total).astype(jnp.bfloat16)
    attended = jnp.einsum(
        "ihqk,ikhd->iqhd", probs_b, value_heads, preferred_element_type=jnp.float32
    )
    return (
        attended.reshape(projected.shape[1], projected.shape[2]).astype(jnp.bfloat16),
        log_total,
    )


def attend_back(projected, d_attended, log_total, live_rows, head_count):
    item_count = live_rows.shape[0]
    query_heads = split_heads(projected[0], item_count, head_count)
    key_heads = split_heads(projected[1], item_count, head_count)
    value_heads = split_heads(projected[2], item_count, head_count)
    back_heads = split_heads(d_attended, item_count, head_count)
    scores = masked_scores(query_heads, key_heads, live_rows)
    attn_probs = jnp.exp(scores - log_total)
    probs_b = attn_probs.astype(jnp.bfloat16)
    d_value = jnp.einsum("ihqk,iqhd->ikhd", probs_b, back_heads, preferred_element_type=jnp.float32)
    d_probs = jnp.einsum(
        "iqhd,ikhd->ihqk", back_heads, value_heads, preferred_element_type=jnp.float32
    )
    d_scores = (
        attn_probs * (d_probs - jnp.sum(attn_probs * d_probs, axis=-1, keepdims=True))
    ).astype(jnp.bfloat16)
    score_scale = HS ** (-0.5)
    d_query = (
        jnp.einsum("ihqk,ikhd->iqhd", d_scores, key_heads, preferred_element_type=jnp.float32)
        * score_scale
    )
    d_key = (
        jnp.einsum("ihqk,iqhd->ikhd", d_scores, query_heads, preferred_element_type=jnp.float32)
        * score_scale
    )
    flat_shape = projected.shape[1:]
    return jnp.stack(
        [d_query.reshape(flat_shape), d_key.reshape(flat_shape), d_value.reshape(flat_shape)]
    ).astype(jnp.bfloat16)


def adam_step(weight, grad, first, second, rate, decay):
    moment = 0.5 * first + 0.5 * grad
    square = 0.5 * second + 0.5 * grad * grad
    fix = 1.0 - 0.5**STEP
    update = weight - rate * (moment / fix / (jnp.sqrt(square / fix) + ADAM_EPS) + decay * weight)
    return (moment, square, update)


def plain(latents, live_keys, cotangent, inner_weights, outer_weights, norm_params):
    head_devices = lax.axis_size("head")
    data_devices = lax.axis_size("dp")
    row_count = latents.shape[0]
    item_count = row_count // LAT
    inner_b, outer_b = (
        lax.all_gather(
            lax.all_gather(inner_weights.astype(jnp.bfloat16), "dp", axis=1, tiled=True),
            "head", axis=2, tiled=True),
        lax.all_gather(
            lax.all_gather(outer_weights.astype(jnp.bfloat16), "dp", axis=2, tiled=True),
            "head", axis=1, tiled=True),
    )
    live_own = lax.dynamic_slice(
        live_keys, (lax.axis_index("head") * item_count,), (item_count,))
    source = latents.astype(jnp.float32)
    normed = layer_norm(source, norm_params[0], norm_params[1]).astype(jnp.bfloat16)
    qkv_b = inner_b[:3]
    proj_b = outer_b[0]
    up_b = inner_b[3]
    down_b = outer_b[1]
    projected = jnp.einsum(
        "rd,tdc->trc", normed, qkv_b, preferred_element_type=jnp.float32
    ).astype(jnp.bfloat16)
    attended, log_total = attend(projected, live_own, HEADS)
    residual = source + jnp.dot(attended, proj_b, preferred_element_type=jnp.float32)
    normed_two = layer_norm(residual, norm_params[2], norm_params[3]).astype(jnp.bfloat16)
    preact = jnp.dot(normed_two, up_b, preferred_element_type=jnp.float32)
    activation = gelu_exact(preact).astype(jnp.bfloat16)
    mlp_part = jnp.dot(activation, down_b, preferred_element_type=jnp.float32)
    block_output = (residual + mlp_part).astype(jnp.bfloat16)
    grad_down = jnp.einsum("rc,rd->cd", activation, cotangent, preferred_element_type=jnp.float32)
    d_activ = jnp.einsum("rd,cd->rc", cotangent, down_b, preferred_element_type=jnp.float32)
    gelu_back = jax.vjp(gelu_exact, preact)[1]
    d_pre = gelu_back(d_activ)[0].astype(jnp.bfloat16)
    grad_up = jnp.einsum("rd,rc->dc", normed_two, d_pre, preferred_element_type=jnp.float32)
    d_normed_two = jnp.einsum("rc,dc->rd", d_pre, up_b, preferred_element_type=jnp.float32)
    norm_back_two = jax.vjp(layer_norm, residual, norm_params[2], norm_params[3])[1]
    d_resid_norm, grad_gain_two, grad_bias_two = norm_back_two(d_normed_two)
    d_resid = cotangent.astype(jnp.float32) + d_resid_norm
    d_resid_b = d_resid.astype(jnp.bfloat16)
    grad_outproj = jnp.einsum(
        "rc,rd->cd", attended, d_resid_b, preferred_element_type=jnp.float32
    )
    d_attended = jnp.einsum(
        "rd,cd->rc", d_resid_b, proj_b, preferred_element_type=jnp.float32
    ).astype(jnp.bfloat16)
    d_proj = attend_back(projected, d_attended, log_total, live_own, HEADS)
    grad_qkv = jnp.einsum("rd,trc->tdc", normed, d_proj, preferred_element_type=jnp.float32)
    d_normed = jnp.einsum("trc,tdc->rd", d_proj, qkv_b, preferred_element_type=jnp.float32)
    norm_back_one = jax.vjp(layer_norm, source, norm_params[0], norm_params[1])[1]
    d_source_norm, grad_gain_one, grad_bias_one = norm_back_one(d_normed)
    latent_grad = (d_resid + d_source_norm).astype(jnp.bfloat16)
    grad_inner = jnp.concatenate([grad_qkv, grad_up[None]], axis=0)
    grad_outer = jnp.stack([grad_outproj, grad_down])
    grad_inner, grad_outer = (
        lax.psum_scatter(
            lax.psum_scatter(
                grad_inner.astype(jnp.bfloat16), "head", scatter_dimension=2, tiled=True
            ), "dp", scatter_dimension=1, tiled=True).astype(jnp.float32),
        lax.psum_scatter(
            lax.psum_scatter(
                grad_outer.astype(jnp.bfloat16), "head", scatter_dimension=1, tiled=True
            ), "dp", scatter_dimension=2, tiled=True).astype(jnp.float32),
    )
    norm_part = jnp.stack([grad_gain_one, grad_bias_one, grad_gain_two, grad_bias_two])
    local_squares = jnp.sum(grad_inner * grad_inner) + jnp.sum(grad_outer * grad_outer)
    grad_norms, squares_all = lax.psum((norm_part, local_squares), ("dp", "head"))
    return block_output, latent_grad, grad_inner, grad_outer, grad_norms, squares_all


def shards(
    latents,
    live_keys,
    cotangent,
    inner_weights,
    outer_weights,
    norm_params,
    inner_first,
    inner_second,
    inner_average,
    outer_first,
    outer_second,
    outer_average,
    norm_first,
    norm_second,
):
    head_devices = lax.axis_size("head")
    data_devices = lax.axis_size("dp")
    row_count = latents.shape[0]
    token_total = row_count * head_devices * data_devices
    if (data_devices, head_devices) == (8, 4) and token_total == TOKENS:
        sh = jnp.concatenate(
            [inner_weights[:3], outer_weights[:1].swapaxes(1, 2), inner_weights[3:],
             outer_weights[1:].swapaxes(1, 2)]).astype(jnp.bfloat16)
        block_output, latent_grad, grads, small = run_block(
            sh, latents, cotangent, live_keys, norm_params)
        inner = (inner_weights, inner_first, inner_second, inner_average)
        outer = (outer_weights, outer_first, outer_second, outer_average)
        done = run_update(
            small, grads.reshape(960, 320),
            [v.reshape(640, 320) for v in inner],
            [v.swapaxes(1, 2).reshape(320, 320) for v in outer], (norm_params, norm_first, norm_second))
        return (block_output, latent_grad, done[0][0, 0],
                *(v.reshape(4, 160, 320) for v in done[1:6]),
                *(v.reshape(2, 160, 320).swapaxes(1, 2) for v in done[6:11]), *done[11:])
    block_output, latent_grad, grad_inner, grad_outer, grad_norms, squares_all = plain(
        latents, live_keys, cotangent, inner_weights, outer_weights, norm_params)
    grad_norm = jnp.sqrt(squares_all + jnp.sum(grad_norms * grad_norms))
    clip_limit = CLIP_RATE * D * token_total**0.5
    factor = jnp.minimum(1.0, clip_limit / grad_norm)
    inner_rate = D ** (-0.5)
    outer_rate = jnp.array([(LAT / (3.0 * D)) ** 0.5, D ** (-0.5)], dtype=jnp.float32).reshape(
        2, 1, 1
    )
    clipped_norms = grad_norms * factor
    inner_new = adam_step(
        inner_weights, grad_inner * factor, inner_first, inner_second, inner_rate, DECAY_RATE
    )
    outer_new = adam_step(
        outer_weights, grad_outer * factor, outer_first, outer_second, outer_rate, DECAY_RATE
    )
    norm_new = adam_step(norm_params, clipped_norms, norm_first, norm_second, NORM_RATE, 0.0)
    inner_smooth = SMOOTH_RATE * inner_average + (1.0 - SMOOTH_RATE) * inner_new[2]
    outer_smooth = SMOOTH_RATE * outer_average + (1.0 - SMOOTH_RATE) * outer_new[2]
    return (
        block_output,
        latent_grad,
        grad_norm,
        inner_new[0],
        inner_new[1],
        inner_new[2],
        inner_smooth,
        inner_new[2].astype(jnp.bfloat16),
        outer_new[0],
        outer_new[1],
        outer_new[2],
        outer_smooth,
        outer_new[2].astype(jnp.bfloat16),
        norm_new[0],
        norm_new[1],
        norm_new[2],
        clipped_norms[2:4],
    )


def solution(mesh):
    return jax.shard_map(
        shards,
        mesh=mesh,
        in_specs=(
            P(("dp", "head"), None),
            P("dp"),
            P(("dp", "head"), None),
            P(None, "dp", "head"),
            P(None, "head", "dp"),
            P(),
            P(None, "dp", "head"),
            P(None, "dp", "head"),
            P(None, "dp", "head"),
            P(None, "head", "dp"),
            P(None, "head", "dp"),
            P(None, "head", "dp"),
            P(),
            P(),
        ),
        out_specs=(
            P(("dp", "head"), None),
            P(("dp", "head"), None),
            P(),
            P(None, "dp", "head"),
            P(None, "dp", "head"),
            P(None, "dp", "head"),
            P(None, "dp", "head"),
            P(None, "dp", "head"),
            P(None, "head", "dp"),
            P(None, "head", "dp"),
            P(None, "head", "dp"),
            P(None, "head", "dp"),
            P(None, "head", "dp"),
            P(),
            P(),
            P(),
            P(),
        ),
        check_vma=False,
    )
```

```python
import jax
import jax.numpy as jnp
from jax import lax
from jax.experimental import pallas as pl
from jax.experimental.pallas import tpu as pltpu
from jax.sharding import PartitionSpec as P

HEADS = 8
HS = 160
D = 1280
LAT = 256
STEP = 5


NORM_EPS = 1e-05
MASKED = -1e30
CLIP_RATE = 0.02
ADAM_EPS = 1e-08
DECAY_RATE = 0.1
NORM_RATE = 0.3
SMOOTH_RATE = 0.9


NM = 6
TOKENS = 16384
MESH = pl.DeviceIdType.MESH
NN = (((1,), (0,)), ((), ()))
NT = (((1,), (1,)), ((), ()))
TN = (((0,), (0,)), ((), ()))
ROWS = 512
CH = 64
SLOT = {5: 6, 4: 7, 3: 4, 0: 3, 1: 5, 2: 0}
RD_SLOTS = 2
RB_SLOTS = 3
ORDER = (5, 4, 3, 0, 1, 2)
PLACE = {0: 0, 1: 1, 2: 2, 4: 3, 3: 4, 5: 5}
ORD = {m: i for i, m in enumerate(ORDER)}
GATHER = "FMFMMF"
REDUCE = "FMFMMF"
BASE = [sum(8 if t == "F" else 9 for t in REDUCE[:i]) for i in range(7)]


def ids():
    d = lax.axis_index("dp")
    h = lax.axis_index("head")
    return d % 2, h // 2, d // 2, h % 2


def dev(x, y, z, c):
    return (z * 2 + x, y * 2 + c)


def dg(a, b, dims):
    return lax.dot_general(a, b, dims, preferred_element_type=jnp.float32)


def block_kernel(
    sh, lat_in, cot_in, live, norms,
    bo_out, lg_out, gout, nout,
    W, sh_in, lat, cot, n1, q, k, v, probs, att, resid, n2, act, gp, T,
    RD, RB, U, F, FX, NG, NX, SQ, SX,
    s0, r0, sz, rz, sa, ra, sb, rb, sd, rd,
    sD, rD, sB, rB, sU, rU, sF, rF, sN, rN, sS, rS, lsem, free, free_b,
):
    bf, f32 = jnp.bfloat16, jnp.float32
    x, y, z, c = ids()
    sib, xn, yn = dev(x, y, z, 1 - c), dev(1 - x, y, z, c), dev(x, 1 - y, z, c)
    zp = [dev(x, y, lax.rem(z + j, 4), c) for j in (1, 2, 3)]

    c_lat = pltpu.make_async_copy(lat_in, lat, lsem.at[0])
    c_cot = pltpu.make_async_copy(cot_in, cot, lsem.at[1])
    c_lat.start()
    c_cot.start()
    bar = pltpu.get_barrier_semaphore()
    plane = [xn, yn] + [
        dev(1 - x if i else x, 1 - y if j else y, z, 1 - c if o else c)
        for i, j, o in ((1, 1, 0), (1, 0, 1), (0, 1, 1), (1, 1, 1))
    ]
    for d in [sib] + plane + zp:
        pl.semaphore_signal(bar, inc=1, device_id=d, device_id_type=MESH)
    pl.semaphore_wait(bar, 10)

    def cols(j):
        return pl.ds(pl.multiple_of(j * 640, 128), 640)

    def rc(src, dst, s, r, d):
        return pltpu.make_async_remote_copy(src, dst, s, r, device_id=d, device_id_type=MESH)

    def pick(a, b):
        return jnp.where(c == 0, a, b)

    an = tuple(pick(a, b) for a, b in zip(xn, yn))
    bn = tuple(pick(a, b) for a, b in zip(yn, xn))

    def at_x(a, b):
        return pick(1 - x if a else x, 1 - x if b else x)

    def at_y(a, b):
        return pick(1 - y if b else y, 1 - y if a else y)

    def unit(w, dz, a, b):
        return w.at[lax.rem(z + dz, 4), at_x(a, b), c, :, cols(at_y(a, b))]

    def line(w, a, b):
        return w.at[:, at_x(a, b), c, :, cols(at_y(a, b))]

    def g_pair(m):
        return rc(sh.at[m, 1 - c], sh_in.at[m], s0.at[m], r0.at[m], sib)

    def g_z(m, a, j, dz, i):
        u = unit(W.at[m], dz, a, 0)
        return rc(u, u, sz.at[m, a, i], rz.at[m, a, (dz - j) % 4], zp[j - 1])

    def g_a(m):
        u = line(W.at[m], 0, 0) if GATHER[m] == "F" else unit(W.at[m], 0, 0, 0)
        return rc(u, u, sa.at[m], ra.at[m], an)

    def g_b(m, a):
        u = line(W.at[m], a, 0)
        return rc(u, u, sb.at[m, a], rb.at[m, a], bn)

    def g_d(m, a, b):
        u = line(W.at[m], a, b)
        return rc(u, u, sd.at[m, 2 * a + b], rd.at[m, 2 * a + b], sib)

    def g_z_do(m, a, what):
        def act_on(cp):
            if what == "start":
                cp.start()
            else:
                cp.wait_send()

        act_on(g_z(m, a, 2, 0, 1))
        for j, end in ((1, 3), (3, 0)):
            @pl.when(z != end)
            def _():
                act_on(g_z(m, a, j, 0, j - 1))

    def g_z_on(m, a, what):
        for at, j in ((2, 1), (1, 3)):
            @pl.when(z == at)
            def _():
                if what == "start":
                    g_z(m, a, j, 2, 3).start()
                else:
                    g_z(m, a, j, 2, 3).wait_send()

    def g_p(m):
        g_pair(m).wait()
        own, oth = sh[m, c], sh_in[m]
        W[m, z, x, c, :, cols(y)] = jnp.concatenate(
            [jnp.where(c == 0, own, oth), jnp.where(c == 0, oth, own)], axis=-1
        )
        if GATHER[m] == "M":
            g_a(m).start()

    def g_go(m, a):
        if a:
            g_a(m).wait_recv()
        g_z_do(m, a, "start")

    def g_on(m, a):
        g_z(m, a, 2, 0, 1).wait_recv()
        g_z_on(m, a, "start")

    def g_line(m, a):
        if a and GATHER[m] == "F":
            g_a(m).wait_recv()
        else:
            for j in (1, 3):
                g_z(m, a, j, 0, j - 1).wait_recv()
        if not a and GATHER[m] == "F":
            g_a(m).start()
        g_b(m, a).start()
        g_d(m, a, 0).start()

    def g_far(m, a):
        g_b(m, a).wait_recv()
        g_d(m, a, 1).start()

    def g_end(m):
        for a in (0, 1):
            for b in (0, 1):
                g_d(m, a, b).wait()
            g_b(m, a).wait_send()
            if a == 0 or GATHER[m] == "M":
                g_z_do(m, a, "wait")
                g_z_on(m, a, "wait")
        g_a(m).wait_send()

    def r_d(i):
        return rc(W.at[SLOT[ORDER[i]], :, :, 1 - c], RD.at[i % RD_SLOTS], sD.at[i], rD.at[i], sib)

    def grd(i):
        return W.at[SLOT[ORDER[i]]]

    def r_b(i, a):
        return rc(line(grd(i), a, 1), RB.at[i % RB_SLOTS, a], sB.at[i, a], rB.at[i, a], bn)

    def r_a(i):
        k = BASE[i]
        if REDUCE[i] == "F":
            return rc(line(grd(i), 1, 0), U.at[pl.ds(k, 4)], sU.at[k], rU.at[k], an)
        return rc(unit(grd(i), 0, 1, 0), U.at[k], sU.at[k], rU.at[k], an)

    def place(i, a, rel):
        return BASE[i] + (4 if REDUCE[i] == "F" else 1) + 4 * a + rel

    def r_z(i, a, dz):
        k = place(i, a, 4 - dz)
        return rc(unit(grd(i), dz, a, 0), U.at[k], sU.at[place(i, a, dz)], rU.at[k], zp[dz - 1])

    def r_y(i, a, dz, j):
        k = place(i, a, 0)
        return rc(unit(grd(i), dz, a, 0), U.at[k], sU.at[place(i, a, dz)], rU.at[k], zp[j - 1])

    def r_f(m):
        return rc(F.at[m], FX.at[m], sF.at[m], rF.at[m], sib)

    def r_z_go(i, a):
        for dz, end, j in ((1, 3, 3), (3, 0, 1)):
            @pl.when(z == end)
            def _():
                r_y(i, a, dz, j).start()

            @pl.when(z != end)
            def _():
                r_z(i, a, dz).start()

    def st_r(i, a):
        @pl.when((z == 1) | (z == 2))
        def _():
            r_y(i, a, 1, 1).wait_recv()
            u = unit(grd(i), 2, a, 0)
            u[...] = u[...] + U[place(i, a, 0)]

        r_z(i, a, 2).start()

    def r_z_in(i, a):
        u = unit(grd(i), 0, a, 0)

        def add(rel):
            u[...] = u[...] + U[place(i, a, rel)]

        r_z(i, a, 2).wait_recv()
        add(2)
        for rel, end in ((3, 0), (1, 3)):
            @pl.when(z != end)
            def _():
                r_z(i, a, 4 - rel).wait_recv()
                add(rel)

    def r_z_end(i, a):
        for dz in (1, 2, 3):
            r_z(i, a, dz).wait_send()

    def add_line(i, a, src):
        kept = line(grd(i), a, 0)

        def body(j, _):
            kept[j] = kept[j] + src[j]
            return 0

        lax.fori_loop(0, 4, body, 0)

    def st_d(i):
        if i >= RD_SLOTS:
            pl.semaphore_wait(free, 1)
        r_d(i).start()

    def st_b(i):
        r_d(i).wait()
        g = grd(i)

        def body(j, _):
            a, b = j // 2, j % 2
            g[a, b, c] = g[a, b, c] + RD[i % RD_SLOTS, a, b]
            return 0

        lax.fori_loop(0, 8, body, 0)
        if i + RD_SLOTS < NM:
            pl.semaphore_signal(free, inc=1, device_id=sib, device_id_type=MESH)
        if i >= RB_SLOTS:
            pl.semaphore_wait(free_b, 1)
        r_b(i, 1).start()
        r_b(i, 0).start()

    def st_a(i):
        r_b(i, 1).wait()
        add_line(i, 1, RB.at[i % RB_SLOTS, 1])
        if REDUCE[i] == "F":
            r_a(i).start()
        else:
            r_z_go(i, 1)

    def st_c(i):
        r_b(i, 0).wait()
        add_line(i, 0, RB.at[i % RB_SLOTS, 0])
        if i + RB_SLOTS < NM:
            pl.semaphore_signal(free_b, inc=1, device_id=bn, device_id_type=MESH)
        if REDUCE[i] == "M":
            r_z_go(i, 0)

    def st_z(i):
        if REDUCE[i] == "F":
            r_a(i).wait()
            add_line(i, 0, U.at[pl.ds(BASE[i], 4)])
            r_z_go(i, 0)
        else:
            st_r(i, 1)

    def st_y(i):
        r_z_in(i, 1)
        r_a(i).start()

    def put(dst, w):
        dst[...] = jnp.where(c == 0, w[:, :320], w[:, 64:])

    def st_g(m):
        r_f(m).wait()
        put(gout.at[PLACE[m], 1 - c], FX[m])

    def st_f(i):
        m = ORDER[i]
        r_z_in(i, 0)
        f = unit(grd(i), 0, 0, 0)[...].astype(f32)
        if REDUCE[i] == "M":
            r_a(i).wait()
            f = f + U[BASE[i]].astype(f32)
            r_z_end(i, 1)
        r_z_end(i, 0)
        F[m] = jnp.where(c == 0, f[:, 256:], f[:, :384])
        mine = jnp.where(c == 0, f[:, :384], f[:, 256:])
        put(gout.at[PLACE[m], c], mine)
        r_f(m).start()
        ff = f * f
        ff = ff.reshape(10, 8, 640).sum(0)
        SQ[0] += ff[:, :128] + ff[:, 128:256] + ff[:, 256:384] + ff[:, 384:512] + ff[:, 512:]

    def mat(m):
        return W[m].reshape(D, D)

    def chunks(fn, init=0):
        return lax.fori_loop(
            0, ROWS // CH, lambda i, a: fn(pl.ds(pl.multiple_of(i * CH, CH), CH), a), init)

    def stats(vals):
        centre = vals - jnp.mean(vals, axis=-1, keepdims=True)
        r = lax.rsqrt(jnp.mean(centre * centre, axis=-1, keepdims=True) + NORM_EPS)
        return centre * r, r

    def ln_to(src, gi, dst):
        def body(r, a):
            xhat, _ = stats(src[r, :].astype(f32))
            dst[r, :] = (xhat * norms[gi:gi + 1, :] + norms[gi + 1:gi + 2, :]).astype(bf)
            return a

        chunks(body)

    def ln_back(src, gi, err, emit):
        def body(r, acc):
            xhat, inv = stats(src[r, :].astype(f32))
            e = err[r, :]
            eg = e * norms[gi:gi + 1, :]
            back = inv * (eg - jnp.mean(eg, axis=-1, keepdims=True)
                          - xhat * jnp.mean(eg * xhat, axis=-1, keepdims=True))
            emit(r, back)
            return (acc[0] + (e * xhat).reshape(CH // 8, 8, D).sum(0),
                    acc[1] + e.reshape(CH // 8, 8, D).sum(0))

        zero = jnp.zeros((8, D), f32)
        a, b = chunks(body, (zero, zero))
        NG[0, gi:gi + 1, :] = a.sum(0, keepdims=True)
        NG[0, gi + 1:gi + 2, :] = b.sum(0, keepdims=True)

    scale = HS ** (-0.5)
    lane = lax.broadcasted_iota(jnp.int32, (1, 256), 1)
    lane1 = lax.broadcasted_iota(jnp.int32, (1, 128), 1)

    def head_mask(hh):
        return jnp.where((lane >= 32 * hh) & (lane < 32 * hh + HS), 1.0, 0.0).astype(bf)

    def join(o, dst, rows, g):
        parts = [o[0][:, :128]]
        for hh in (1, 2, 3):
            parts.append(jnp.where(lane1 < 32 * hh, o[hh - 1][:, 128:], o[hh][:, :128]))
        parts.append(o[3][:, 128:])
        for j in range(5):
            dst[rows, pl.ds(pl.multiple_of(g * 640 + 128 * j, 128), 128)] = parts[j].astype(bf)

    h_first = (y * 2 + c) * 2

    def attn(i, g):
        rows = pl.ds(pl.multiple_of(i * LAT, LAT), LAT)
        count = live[h_first + i]
        outs = []
        for hh in range(4):
            win = pl.ds(pl.multiple_of(g * 640 + 128 * hh, 128), 256)
            s = dg(q[rows, win] * head_mask(hh), k[rows, win], NT) * scale
            s = jnp.where(lane < count, s, MASKED)
            e = jnp.exp(s - jnp.max(s, axis=-1, keepdims=True))
            p = (e * (1.0 / jnp.sum(e, axis=-1, keepdims=True))).astype(bf)
            probs[i * 8 + g * 4 + hh] = p
            outs.append(dg(p, v[rows, win], NN))
        join(outs, att, rows, g)

    def attn_back(i, g, do, dq, dk, dv):
        rows = pl.ds(pl.multiple_of(i * LAT, LAT), LAT)
        oq, ok, ov = [], [], []
        for hh in range(4):
            win = pl.ds(pl.multiple_of(g * 640 + 128 * hh, 128), 256)
            p = probs[i * 8 + g * 4 + hh]
            dow = do[rows, win]
            ov.append(dg(p, dow, TN))
            dp = dg(dow * head_mask(hh), v[rows, win], NT)
            pf = p.astype(f32)
            ds = (pf * (dp - jnp.sum(pf * dp, axis=-1, keepdims=True))).astype(bf)
            oq.append(dg(ds, k[rows, win], NN) * scale)
            ok.append(dg(ds, q[rows, win], TN) * scale)
        join(oq, dq, rows, g)
        join(ok, dk, rows, g)
        join(ov, dv, rows, g)

    def grad(m, left, right):
        W[SLOT[m]] = dg(left[...], right[...], TN).astype(bf).reshape(4, 2, 2, 80, D)
        st_d(ORD[m])

    def proj(dst, m):
        dst[...] = dg(n1[...], mat(m), NN).astype(bf)

    def begin():
        for m in range(NM):
            g_pair(m).start()
        g_p(0)
        g_go(0, 0)
        g_p(1)
        g_go(1, 0)
        for m in range(2, NM):
            g_p(m)
        g_go(1, 1)
        SQ[0] = jnp.zeros((8, 128), f32)

    def norm_one():
        c_lat.wait()
        ln_to(lat, 0, n1)

    def out_proj():
        resid[...] = dg(att[...], mat(3), NT) + lat[...].astype(f32)
        ln_to(resid, 2, n2)

    def up():
        T[...] = dg(n2[...], mat(4), NN)

        def gelu(r, a):
            p = T[r, :]
            cdf = 0.5 * (1.0 + lax.erf(p * (0.5 ** 0.5)))
            act[r, :] = (p * cdf).astype(bf)
            gp[r, :] = (cdf + p * (jnp.exp(-0.5 * p * p) * 0.3989422804014327)).astype(bf)
            return a

        chunks(gelu)
        c_cot.wait()

    def d_act():
        gp[...] = (dg(cot[...], mat(5), NN) * gp[...].astype(f32)).astype(bf)

    c_bo = pltpu.make_async_copy(act, bo_out, lsem.at[2])
    c_lg = pltpu.make_async_copy(n2, lg_out, lsem.at[3])

    def down():
        T[...] = dg(act[...], mat(5), NT)

        def to_bo(r, a):
            act[r, :] = (T[r, :] + resid[r, :]).astype(bf)
            return a

        chunks(to_bo)
        c_bo.start()

    def d_two():
        T[...] = dg(gp[...], mat(4), NT)

        def emit_two(r, back):
            d = cot[r, :].astype(f32) + back
            resid[r, :] = d
            n2[r, :] = d.astype(bf)

        ln_back(resid, 2, T, emit_two)

    def d_att():
        c_bo.wait()
        act[...] = dg(n2[...], mat(3), NN).astype(bf)

    def d_in(m, src):
        if m == 0:
            T[...] = dg(src[...], mat(0), NT)
        else:
            T[...] += dg(src[...], mat(m), NT)

    def d_one():
        def emit_one(r, back):
            n2[r, :] = (resid[r, :] + back).astype(bf)

        ln_back(lat, 0, T, emit_one)
        c_lg.start()

    def n_swap(t):
        return rc(NG.at[0], NX.at[t], sN.at[t], rN.at[t], ([sib, xn, yn] + zp)[t])

    def sum_z(own, one, two, three):
        even = lax.rem(z, 2) == 0
        return (own + jnp.where(even, three, one)) + (two + jnp.where(even, one, three))

    def n_step(t):
        if t > 0:
            n_swap(t - 1).wait()
            NG[0] = NG[0] + NX[t - 1]
        for j in (t,) if t < 3 else (3, 4, 5):
            n_swap(j).start()

    def n_end():
        for j in (3, 4, 5):
            n_swap(j).wait()
        NG[0] = sum_z(NG[0], NX[3], NX[4], NX[5])

    def s_swap(t):
        return rc(SQ.at[0], SX.at[t], sS.at[t], rS.at[t], (zp + [sib] + plane)[t])

    def finish():
        for t in range(3):
            s_swap(t).start()
        for t in range(3):
            s_swap(t).wait()
        SQ[0] = sum_z(SQ[0], SX[0], SX[1], SX[2])
        for t in range(3, 10):
            s_swap(t).start()
        st_g(3)
        st_g(0)
        st_g(2)
        nout[0:4, :] = NG[0]
        for t in range(3, 10):
            s_swap(t).wait()
        tot = ((SQ[0] + SX[4]) + (SX[5] + SX[6])) + ((SX[3] + SX[7]) + (SX[8] + SX[9]))
        nout[4:8, :] = jnp.zeros((4, D), f32) + jnp.sum(tot)
        c_lg.wait()

    def heads(fn, g, i, *refs):
        fn(i, g, *refs)

    P0, P1, P2, P3 = ((heads, attn, g, i) for g in (0, 1) for i in (0, 1))
    Q0, Q1, Q2, Q3 = ((heads, attn_back, g, i, act, cot, gp, att) for g in (0, 1) for i in (0, 1))
    program = [
        (begin,),
        (g_on, 0, 0), (g_go, 2, 0), (g_line, 0, 0),
        (g_on, 1, 0), (g_on, 1, 1), (g_go, 3, 0), (g_go, 3, 1), (g_line, 1, 0), (g_line, 1, 1),
        (g_line, 0, 1), (norm_one,), (g_far, 0, 0),
        (g_on, 2, 0), (g_go, 4, 0), (g_go, 4, 1), (g_line, 2, 0),
        (g_far, 1, 0), (g_far, 0, 1), (g_end, 0),
        (proj, q, 0),
        (g_on, 3, 0), (g_on, 3, 1), (g_go, 5, 0), (g_line, 3, 0), (g_line, 3, 1),
        (g_line, 2, 1), (g_far, 2, 0), (g_far, 1, 1), (g_end, 1),
        (proj, k, 1),
        (g_on, 4, 0), (g_on, 4, 1), (g_line, 4, 0), (g_line, 4, 1),
        (g_far, 3, 0), (g_far, 2, 1), (g_end, 2),
        (proj, v, 2), P0,
        (g_on, 5, 0), (g_line, 5, 0), P1,
        (g_far, 4, 0), P2, (g_far, 3, 1), P3, (g_end, 3), (out_proj,),
        (g_line, 5, 1), (g_far, 5, 0), (g_far, 4, 1), (g_end, 4),
        (up,), (grad, 5, cot, act), (g_far, 5, 1),
        (st_b, 0), (g_end, 5), (d_act,), (grad, 4, n2, gp), (down,), (st_a, 0), (d_two,), (st_b, 1),
        (grad, 3, n2, att), (st_c, 0), (st_z, 0), (d_att,), Q0, (st_a, 1), (st_b, 2), Q1, Q2, (st_c, 1),
        (st_r, 0, 0), Q3, (st_z, 1), (grad, 0, n1, cot), (st_a, 2), (st_r, 1, 0), (grad, 1, n1, gp),
        (st_c, 2), (st_b, 3), (st_z, 2), (d_in, 0, cot), (st_a, 3), (st_b, 4), (grad, 2, n1, att), (st_c, 3),
        (st_a, 4), (st_b, 5), (d_in, 1, gp), (st_c, 4), (st_z, 4), (st_a, 5), (st_r, 4, 0), (d_in, 2, att),
        (st_y, 4), (st_z, 3), (st_c, 5), (st_r, 3, 0), (st_z, 5), (st_r, 2, 0), (st_y, 1), (st_f, 0),
        (d_one,), (n_step, 0), (st_f, 1), (st_f, 4), (n_step, 1), (st_r, 5, 0), (st_y, 3), (n_step, 2),
        (st_g, 5), (st_f, 2), (st_g, 4), (st_f, 3), (n_step, 3), (st_g, 1), (n_end,), (st_f, 5), (finish,),
    ]
    for fn, *given in program:
        fn(*given)


def run_block(sh, lat, cot, live, norms):
    bf, f32 = jnp.bfloat16, jnp.float32
    dma = pltpu.SemaphoreType.DMA
    act = pltpu.VMEM((ROWS, D), bf)
    wide = pltpu.VMEM((ROWS, D), f32)
    vm, hbm = pl.BlockSpec(memory_space=pltpu.VMEM), pl.BlockSpec(memory_space=pl.ANY)
    return pl.pallas_call(
        block_kernel,
        out_shape=(
            jax.ShapeDtypeStruct((ROWS, D), bf),
            jax.ShapeDtypeStruct((ROWS, D), bf),
            jax.ShapeDtypeStruct((NM, 2, 80, 320), f32),
            jax.ShapeDtypeStruct((8, D), f32),
        ),
        in_specs=[vm, hbm, hbm, pl.BlockSpec(memory_space=pltpu.SMEM), vm],
        out_specs=(hbm, hbm, vm, vm),
        scratch_shapes=[
            pltpu.VMEM((8, 4, 2, 2, 80, D), bf), pltpu.VMEM((NM, 80, 320), bf),
            act, act, act, act, act, act, pltpu.VMEM((16, LAT, LAT), bf), act, wide, act, act, act, wide,
            pltpu.VMEM((RD_SLOTS, 4, 2, 80, D), bf), pltpu.VMEM((RB_SLOTS, 2, 4, 80, 640), bf),
            pltpu.VMEM((BASE[6], 80, 640), bf),
            pltpu.VMEM((NM, 80, 384), f32), pltpu.VMEM((NM, 80, 384), f32),
            pltpu.VMEM((1, 4, D), f32), pltpu.VMEM((6, 4, D), f32),
            pltpu.VMEM((1, 8, 128), f32), pltpu.VMEM((10, 8, 128), f32),
            dma((NM,)), dma((NM,)), dma((NM, 2, 4)), dma((NM, 2, 4)), dma((NM,)), dma((NM,)),
            dma((NM, 2)), dma((NM, 2)), dma((NM, 4)), dma((NM, 4)),
            dma((NM,)), dma((NM,)), dma((NM, 2)), dma((NM, 2)), dma((BASE[6],)), dma((BASE[6],)),
            dma((NM,)), dma((NM,)), dma((6,)), dma((6,)), dma((10,)), dma((10,)), dma((4,)),
            pltpu.SemaphoreType.REGULAR, pltpu.SemaphoreType.REGULAR,
        ],
        compiler_params=pltpu.CompilerParams(
            collective_id=0, has_side_effects=True, vmem_limit_bytes=66 * 1000 * 1000),
        name="block",
    )(sh.reshape(NM, 2, 80, 320), lat, cot, live, norms)


def update_kernel(small, gin, gother, wi, fi, si, ai, wo, fo, so, ao, wn, fn, sn,
                  gn, mi, qi, ui, ei, bi, mo, qo, uo, eo, bo, mn, qn, un, tn):
    f32 = jnp.float32
    gnorm = small[0:4, :]
    norm = jnp.sqrt(small[4:5, 0:1] + jnp.sum(gnorm * gnorm, keepdims=True))
    factor = jnp.minimum(1.0, CLIP_RATE * D * TOKENS ** 0.5 / norm)

    def step(weight, grad, first, second, rate, decay, moment, square, update):
        moment_new = 0.5 * first + 0.5 * grad
        square_new = 0.5 * second + 0.5 * grad * grad
        fix = 1.0 / (1.0 - 0.5 ** STEP)
        new = weight - rate * (
            moment_new * fix / (jnp.sqrt(square_new * fix) + ADAM_EPS) + decay * weight)
        moment[...] = moment_new
        square[...] = square_new
        update[...] = new
        return new

    new = step(wi[...], gin[...] * factor, fi[...], si[...], D ** (-0.5), DECAY_RATE, mi, qi, ui)
    ei[...] = SMOOTH_RATE * ai[...] + (1.0 - SMOOTH_RATE) * new
    bi[...] = new.astype(jnp.bfloat16)
    part = wo.shape[0]
    row = lax.broadcasted_iota(jnp.int32, (part, 1), 0) + part * pl.program_id(0)
    rate = jnp.where(row < 160, (LAT / (3.0 * D)) ** 0.5, D ** (-0.5))
    new = step(wo[...], gother[...] * factor, fo[...], so[...], rate, DECAY_RATE, mo, qo, uo)
    eo[...] = SMOOTH_RATE * ao[...] + (1.0 - SMOOTH_RATE) * new
    bo[...] = new.astype(jnp.bfloat16)

    @pl.when(pl.program_id(0) == 0)
    def _():
        gn[...] = norm
        g = gnorm * factor
        step(wn[...], g, fn[...], sn[...], NORM_RATE, 0.0, mn, qn, un)
        tn[...] = g[2:4]


def run_update(small, grads, inner, outer, norm):
    f32, bf = jnp.float32, jnp.bfloat16
    steps = 2
    vi = pl.BlockSpec((640 // steps, 320), lambda i: (i, 0))
    vo = pl.BlockSpec((320 // steps, 320), lambda i: (i, 0))
    go = pl.BlockSpec((320 // steps, 320), lambda i: (i + 2 * steps, 0))

    def whole(*shape):
        return pl.BlockSpec(shape, lambda i: (0, 0))

    def out(shape, kind=f32):
        return jax.ShapeDtypeStruct(shape, kind)

    si, so = (640, 320), (320, 320)
    return pl.pallas_call(
        update_kernel,
        grid=(steps,),
        out_shape=(out((1, 1)),) + (out(si),) * 4 + (out(si, bf),) + (out(so),) * 4 + (out(so, bf),)
        + (out((4, D)),) * 3 + (out((2, D)),),
        in_specs=[whole(8, D), vi, go] + [vi] * 4 + [vo] * 4 + [whole(4, D)] * 3,
        out_specs=(whole(1, 1),) + (vi,) * 5 + (vo,) * 5 + (whole(4, D),) * 3 + (whole(2, D),),
        compiler_params=pltpu.CompilerParams(vmem_limit_bytes=64 * 1000 * 1000),
        name="update",
    )(small, grads, grads, *inner, *outer, *norm)


def layer_norm(values, gain_row, bias_row):
    centre = values - jnp.mean(values, axis=-1, keepdims=True)
    spread = jnp.mean(centre * centre, axis=-1, keepdims=True)
    return centre * lax.rsqrt(spread + NORM_EPS) * gain_row + bias_row


def gelu_exact(values):
    return jax.nn.gelu(values, approximate=False)


def split_heads(matrix, item_count, head_count):
    return matrix.reshape(
        item_count, matrix.shape[0] // item_count, head_count, matrix.shape[1] // head_count
    )


def masked_scores(query_heads, key_heads, live_rows):
    scores = jnp.einsum(
        "iqhd,ikhd->ihqk", query_heads, key_heads, preferred_element_type=jnp.float32
    ) * HS ** (-0.5)
    length = key_heads.shape[1]
    valid = lax.broadcasted_iota(jnp.int32, (1, 1, 1, length), 3) < live_rows[:, None, None, None]
    return jnp.where(valid, scores, MASKED)


def attend(projected, live_rows, head_count):
    item_count = live_rows.shape[0]
    query_heads = split_heads(projected[0], item_count, head_count)
    key_heads = split_heads(projected[1], item_count, head_count)
    value_heads = split_heads(projected[2], item_count, head_count)
    scores = masked_scores(query_heads, key_heads, live_rows)
    row_peak = jnp.max(scores, axis=-1, keepdims=True)
    log_total = row_peak + jnp.log(jnp.sum(jnp.exp(scores - row_peak), axis=-1, keepdims=True))
    probs_b = jnp.exp(scores - log_total).astype(jnp.bfloat16)
    attended = jnp.einsum(
        "ihqk,ikhd->iqhd", probs_b, value_heads, preferred_element_type=jnp.float32
    )
    return (
        attended.reshape(projected.shape[1], projected.shape[2]).astype(jnp.bfloat16),
        log_total,
    )


def attend_back(projected, d_attended, log_total, live_rows, head_count):
    item_count = live_rows.shape[0]
    query_heads = split_heads(projected[0], item_count, head_count)
    key_heads = split_heads(projected[1], item_count, head_count)
    value_heads = split_heads(projected[2], item_count, head_count)
    back_heads = split_heads(d_attended, item_count, head_count)
    scores = masked_scores(query_heads, key_heads, live_rows)
    attn_probs = jnp.exp(scores - log_total)
    probs_b = attn_probs.astype(jnp.bfloat16)
    d_value = jnp.einsum("ihqk,iqhd->ikhd", probs_b, back_heads, preferred_element_type=jnp.float32)
    d_probs = jnp.einsum(
        "iqhd,ikhd->ihqk", back_heads, value_heads, preferred_element_type=jnp.float32
    )
    d_scores = (
        attn_probs * (d_probs - jnp.sum(attn_probs * d_probs, axis=-1, keepdims=True))
    ).astype(jnp.bfloat16)
    score_scale = HS ** (-0.5)
    d_query = (
        jnp.einsum("ihqk,ikhd->iqhd", d_scores, key_heads, preferred_element_type=jnp.float32)
        * score_scale
    )
    d_key = (
        jnp.einsum("ihqk,iqhd->ikhd", d_scores, query_heads, preferred_element_type=jnp.float32)
        * score_scale
    )
    flat_shape = projected.shape[1:]
    return jnp.stack(
        [d_query.reshape(flat_shape), d_key.reshape(flat_shape), d_value.reshape(flat_shape)]
    ).astype(jnp.bfloat16)


def adam_step(weight, grad, first, second, rate, decay):
    moment = 0.5 * first + 0.5 * grad
    square = 0.5 * second + 0.5 * grad * grad
    fix = 1.0 - 0.5**STEP
    update = weight - rate * (moment / fix / (jnp.sqrt(square / fix) + ADAM_EPS) + decay * weight)
    return (moment, square, update)


def plain(latents, live_keys, cotangent, inner_weights, outer_weights, norm_params):
    head_devices = lax.axis_size("head")
    data_devices = lax.axis_size("dp")
    row_count = latents.shape[0]
    item_count = row_count // LAT
    inner_b, outer_b = (
        lax.all_gather(
            lax.all_gather(inner_weights.astype(jnp.bfloat16), "dp", axis=1, tiled=True),
            "head", axis=2, tiled=True),
        lax.all_gather(
            lax.all_gather(outer_weights.astype(jnp.bfloat16), "dp", axis=2, tiled=True),
            "head", axis=1, tiled=True),
    )
    live_own = lax.dynamic_slice(
        live_keys, (lax.axis_index("head") * item_count,), (item_count,))
    source = latents.astype(jnp.float32)
    normed = layer_norm(source, norm_params[0], norm_params[1]).astype(jnp.bfloat16)
    qkv_b = inner_b[:3]
    proj_b = outer_b[0]
    up_b = inner_b[3]
    down_b = outer_b[1]
    projected = jnp.einsum(
        "rd,tdc->trc", normed, qkv_b, preferred_element_type=jnp.float32
    ).astype(jnp.bfloat16)
    attended, log_total = attend(projected, live_own, HEADS)
    residual = source + jnp.dot(attended, proj_b, preferred_element_type=jnp.float32)
    normed_two = layer_norm(residual, norm_params[2], norm_params[3]).astype(jnp.bfloat16)
    preact = jnp.dot(normed_two, up_b, preferred_element_type=jnp.float32)
    activation = gelu_exact(preact).astype(jnp.bfloat16)
    mlp_part = jnp.dot(activation, down_b, preferred_element_type=jnp.float32)
    block_output = (residual + mlp_part).astype(jnp.bfloat16)
    grad_down = jnp.einsum("rc,rd->cd", activation, cotangent, preferred_element_type=jnp.float32)
    d_activ = jnp.einsum("rd,cd->rc", cotangent, down_b, preferred_element_type=jnp.float32)
    gelu_back = jax.vjp(gelu_exact, preact)[1]
    d_pre = gelu_back(d_activ)[0].astype(jnp.bfloat16)
    grad_up = jnp.einsum("rd,rc->dc", normed_two, d_pre, preferred_element_type=jnp.float32)
    d_normed_two = jnp.einsum("rc,dc->rd", d_pre, up_b, preferred_element_type=jnp.float32)
    norm_back_two = jax.vjp(layer_norm, residual, norm_params[2], norm_params[3])[1]
    d_resid_norm, grad_gain_two, grad_bias_two = norm_back_two(d_normed_two)
    d_resid = cotangent.astype(jnp.float32) + d_resid_norm
    d_resid_b = d_resid.astype(jnp.bfloat16)
    grad_outproj = jnp.einsum(
        "rc,rd->cd", attended, d_resid_b, preferred_element_type=jnp.float32
    )
    d_attended = jnp.einsum(
        "rd,cd->rc", d_resid_b, proj_b, preferred_element_type=jnp.float32
    ).astype(jnp.bfloat16)
    d_proj = attend_back(projected, d_attended, log_total, live_own, HEADS)
    grad_qkv = jnp.einsum("rd,trc->tdc", normed, d_proj, preferred_element_type=jnp.float32)
    d_normed = jnp.einsum("trc,tdc->rd", d_proj, qkv_b, preferred_element_type=jnp.float32)
    norm_back_one = jax.vjp(layer_norm, source, norm_params[0], norm_params[1])[1]
    d_source_norm, grad_gain_one, grad_bias_one = norm_back_one(d_normed)
    latent_grad = (d_resid + d_source_norm).astype(jnp.bfloat16)
    grad_inner = jnp.concatenate([grad_qkv, grad_up[None]], axis=0)
    grad_outer = jnp.stack([grad_outproj, grad_down])
    grad_inner, grad_outer = (
        lax.psum_scatter(
            lax.psum_scatter(
                grad_inner.astype(jnp.bfloat16), "head", scatter_dimension=2, tiled=True
            ), "dp", scatter_dimension=1, tiled=True).astype(jnp.float32),
        lax.psum_scatter(
            lax.psum_scatter(
                grad_outer.astype(jnp.bfloat16), "head", scatter_dimension=1, tiled=True
            ), "dp", scatter_dimension=2, tiled=True).astype(jnp.float32),
    )
    norm_part = jnp.stack([grad_gain_one, grad_bias_one, grad_gain_two, grad_bias_two])
    local_squares = jnp.sum(grad_inner * grad_inner) + jnp.sum(grad_outer * grad_outer)
    grad_norms, squares_all = lax.psum((norm_part, local_squares), ("dp", "head"))
    return block_output, latent_grad, grad_inner, grad_outer, grad_norms, squares_all


def shards(
    latents,
    live_keys,
    cotangent,
    inner_weights,
    outer_weights,
    norm_params,
    inner_first,
    inner_second,
    inner_average,
    outer_first,
    outer_second,
    outer_average,
    norm_first,
    norm_second,
):
    head_devices = lax.axis_size("head")
    data_devices = lax.axis_size("dp")
    row_count = latents.shape[0]
    token_total = row_count * head_devices * data_devices
    if (data_devices, head_devices) == (8, 4) and token_total == TOKENS:
        sh = jnp.concatenate(
            [inner_weights[:3], outer_weights[:1].swapaxes(1, 2), inner_weights[3:],
             outer_weights[1:].swapaxes(1, 2)]).astype(jnp.bfloat16)
        block_output, latent_grad, grads, small = run_block(
            sh, latents, cotangent, live_keys, norm_params)
        inner = (inner_weights, inner_first, inner_second, inner_average)
        outer = (outer_weights, outer_first, outer_second, outer_average)
        done = run_update(
            small, grads.reshape(960, 320),
            [v.reshape(640, 320) for v in inner],
            [v.swapaxes(1, 2).reshape(320, 320) for v in outer], (norm_params, norm_first, norm_second))
        return (block_output, latent_grad, done[0][0, 0],
                *(v.reshape(4, 160, 320) for v in done[1:6]),
                *(v.reshape(2, 160, 320).swapaxes(1, 2) for v in done[6:11]), *done[11:])
    block_output, latent_grad, grad_inner, grad_outer, grad_norms, squares_all = plain(
        latents, live_keys, cotangent, inner_weights, outer_weights, norm_params)
    grad_norm = jnp.sqrt(squares_all + jnp.sum(grad_norms * grad_norms))
    clip_limit = CLIP_RATE * D * token_total**0.5
    factor = jnp.minimum(1.0, clip_limit / grad_norm)
    inner_rate = D ** (-0.5)
    outer_rate = jnp.array([(LAT / (3.0 * D)) ** 0.5, D ** (-0.5)], dtype=jnp.float32).reshape(
        2, 1, 1
    )
    clipped_norms = grad_norms * factor
    inner_new = adam_step(
        inner_weights, grad_inner * factor, inner_first, inner_second, inner_rate, DECAY_RATE
    )
    outer_new = adam_step(
        outer_weights, grad_outer * factor, outer_first, outer_second, outer_rate, DECAY_RATE
    )
    norm_new = adam_step(norm_params, clipped_norms, norm_first, norm_second, NORM_RATE, 0.0)
    inner_smooth = SMOOTH_RATE * inner_average + (1.0 - SMOOTH_RATE) * inner_new[2]
    outer_smooth = SMOOTH_RATE * outer_average + (1.0 - SMOOTH_RATE) * outer_new[2]
    return (
        block_output,
        latent_grad,
        grad_norm,
        inner_new[0],
        inner_new[1],
        inner_new[2],
        inner_smooth,
        inner_new[2].astype(jnp.bfloat16),
        outer_new[0],
        outer_new[1],
        outer_new[2],
        outer_smooth,
        outer_new[2].astype(jnp.bfloat16),
        norm_new[0],
        norm_new[1],
        norm_new[2],
        clipped_norms[2:4],
    )


def solution(mesh):
    return jax.shard_map(
        shards,
        mesh=mesh,
        in_specs=(
            P(("dp", "head"), None),
            P("dp"),
            P(("dp", "head"), None),
            P(None, "dp", "head"),
            P(None, "head", "dp"),
            P(),
            P(None, "dp", "head"),
            P(None, "dp", "head"),
            P(None, "dp", "head"),
            P(None, "head", "dp"),
            P(None, "head", "dp"),
            P(None, "head", "dp"),
            P(),
            P(),
        ),
        out_specs=(
            P(("dp", "head"), None),
            P(("dp", "head"), None),
            P(),
            P(None, "dp", "head"),
            P(None, "dp", "head"),
            P(None, "dp", "head"),
            P(None, "dp", "head"),
            P(None, "dp", "head"),
            P(None, "head", "dp"),
            P(None, "head", "dp"),
            P(None, "head", "dp"),
            P(None, "head", "dp"),
            P(None, "head", "dp"),
            P(),
            P(),
            P(),
            P(),
        ),
        check_vma=False,
    )
```
